128 devices in a mesh: seq: 32 (over z, y, core), wsh: 4 (over x).
Axes of the slice: x: 4, y: 4, z: 4, core: 2. Of those that a mesh axis runs over, the one named last changes fastest.
Arguments:
- tokens: bfloat16 [49152, 640], P(('wsh', 'seq')), may hold values from -6 to 6
- cotangent: bfloat16 [49152, 640], P(('wsh', 'seq')), may hold values from -6 to 6
- segment: int32 [49152], P(('wsh', 'seq')), may hold values from 0 to 2, as said below
- qkv_weight: float32 [640, 1536], P(None, 'wsh'), may hold values from -0.25 to 0.25
- out_weight: float32 [1024, 640], P('wsh'), may hold values from -0.1875 to 0.1875
- gate_weight: float32 [640, 2048], P(None, 'wsh'), may hold values from -0.25 to 0.25
- up_weight: float32 [640, 2048], P(None, 'wsh'), may hold values from -0.25 to 0.25
- down_weight: float32 [2048, 640], P('wsh'), may hold values from -0.125 to 0.125
- gains: float32 [3072], P('wsh'), may hold values from 0.5 to 1.5
- qkv_first: float32 [640, 1536], P(None, 'wsh'), may hold values from -128 to 128
- qkv_second: float32 [640, 1536], P(None, 'wsh'), may hold values from 24.576 to 196.608
- out_first: float32 [1024, 640], P('wsh'), may hold values from -128 to 128
- out_second: float32 [1024, 640], P('wsh'), may hold values from 24.576 to 196.608
- gate_first: float32 [640, 2048], P(None, 'wsh'), may hold values from -128 to 128
- gate_second: float32 [640, 2048], P(None, 'wsh'), may hold values from 24.576 to 196.608
- up_first: float32 [640, 2048], P(None, 'wsh'), may hold values from -128 to 128
- up_second: float32 [640, 2048], P(None, 'wsh'), may hold values from 24.576 to 196.608
- down_first: float32 [2048, 640], P('wsh'), may hold values from -128 to 128
- down_second: float32 [2048, 640], P('wsh'), may hold values from 24.576 to 196.608
- gain_first: float32 [3072], P('wsh'), may hold values from -128 to 128
- gain_second: float32 [3072], P('wsh'), may hold values from 24.576 to 196.608
Outputs:
- block_output: bfloat16 [49152, 640], P(('wsh', 'seq'))
- input_grad: float32 [49152, 640], P(('wsh', 'seq'))
- new_qkv: float32 [640, 1536], P(None, 'wsh')
- new_qkv_first: float32 [640, 1536], P(None, 'wsh')
- new_qkv_second: float32 [640, 1536], P(None, 'wsh')
- new_out: float32 [1024, 640], P('wsh')
- new_out_first: float32 [1024, 640], P('wsh')
- new_out_second: float32 [1024, 640], P('wsh')
- new_gate: float32 [640, 2048], P(None, 'wsh')
- new_gate_first: float32 [640, 2048], P(None, 'wsh')
- new_gate_second: float32 [640, 2048], P(None, 'wsh')
- new_up: float32 [640, 2048], P(None, 'wsh')
- new_up_first: float32 [640, 2048], P(None, 'wsh')
- new_up_second: float32 [640, 2048], P(None, 'wsh')
- new_down: float32 [2048, 640], P('wsh')
- new_down_first: float32 [2048, 640], P('wsh')
- new_down_second: float32 [2048, 640], P('wsh')
- new_gains: float32 [3072], P('wsh')
- new_gain_first: float32 [3072], P('wsh')
- new_gain_second: float32 [3072], P('wsh')
The draws below stay inside these ranges and needn't reach their ends.
Inputs may be any that keep to these rules, and one draw needn't show every extreme that they name: `segment`: within each aligned block of 12288 tokens the numbers never fall and take each of the values 0, 1 and 2.
All inputs are finite; a program needn't handle non-finite values.
Results may differ from the reference program's by a relative error of at most 0.035.
Values may be sent and summed in bfloat16 or wider, within the bound.
A program may use at most 192 MiB of HBM per device.

```python
import math
import jax
import jax.numpy as jnp
from jax import lax

D = 640
H = 4
HD = 256
FF = 2048
WIN = 512
STEP = 10
TOK_DEV = 384
SEQLEN = 12288
TOKENS = 49152
QKV = 1536
GAINS = 3072


def draw_segment(key, part):
    key = jax.random.fold_in(key, 11)
    head_key, tail_key = jax.random.split(key)
    run_count = TOKENS // SEQLEN
    head_len = jax.random.randint(head_key, (run_count, 1), 1, TOK_DEV)
    tail_len = jax.random.randint(tail_key, (run_count, 1), 1, TOK_DEV)
    positions = jnp.arange(SEQLEN, dtype=jnp.int32)[None, :]
    labels = (positions >= head_len).astype(jnp.int32) + (positions >= SEQLEN - tail_len).astype(jnp.int32)
    return labels.reshape(TOKENS)


def block_levels(own_key, extent, shards, least, high):
    loudness, own = 1.0, jax.random.fold_in(own_key, 6)
    for position, blocks in shards:
        draws = jnp.exp(jax.random.uniform(jax.random.fold_in(own, position), (blocks,), jnp.float32, least / len(shards), high / len(shards)))
        loudness = loudness * jnp.repeat(draws, extent[position] // blocks).reshape([-1 if axis == position else 1 for axis in range(len(extent))])
    return loudness


def centred(rng, dims, deviation, bound, cuts=(), kind=jnp.bfloat16):
    result = jax.random.normal(rng, dims, jnp.float32) * deviation
    if len(cuts) > 0:
        result = block_levels(rng, dims, cuts, -0.22, 0.18) * result
    return jnp.clip(result, min=-bound, max=bound).astype(kind)


def setup_inputs(seed: int = 0) -> dict:
    key_list = jax.random.split(jax.random.key(seed), 22)
    tokens = centred(key_list[0], (TOKENS, D), 1.0, 6.0, ((0, 128),))
    cotangent = centred(key_list[1], (TOKENS, D), 1.0, 6.0, ((0, 128),))
    segment = draw_segment(jax.random.fold_in(key_list[21], 71), 0)
    qkv_weight = centred(key_list[3], (D, QKV), D ** -0.5, 0.25, ((1, 4),), jnp.float32)
    out_weight = centred(key_list[4], (H * HD, D), (H * HD) ** -0.5, 0.1875, ((0, 4),), jnp.float32)
    gate_weight = centred(key_list[5], (D, FF), D ** -0.5, 0.25, ((1, 4),), jnp.float32)
    up_weight = centred(key_list[6], (D, FF), D ** -0.5, 0.25, ((1, 4),), jnp.float32)
    down_weight = centred(key_list[7], (FF, D), FF ** -0.5, 0.125, ((0, 4),), jnp.float32)
    gains = jnp.clip(1.0 + 0.1 * jax.random.normal(key_list[8], (GAINS,), jnp.float32), 0.5, 1.5)
    qkv_first = centred(key_list[9], (D, QKV), (0.1 * TOKENS ** 0.5), 128.0, ((1, 4),), jnp.float32)
    qkv_second = jnp.clip(jnp.exp(math.log(196.608) - 2.0794415 * jax.random.uniform(key_list[10], (D, QKV), jnp.float32) ** block_levels(key_list[10], (D, QKV), ((1, 4),), -0.2, 0.2)), 24.576, 196.608)
    out_first = centred(key_list[11], (H * HD, D), (0.1 * TOKENS ** 0.5), 128.0, ((0, 4),), jnp.float32)
    out_second = jnp.clip(jnp.exp(math.log(196.608) - 2.0794415 * jax.random.uniform(key_list[12], (H * HD, D), jnp.float32) ** block_levels(key_list[12], (H * HD, D), ((0, 4),), -0.2, 0.2)), 24.576, 196.608)
    gate_first = centred(key_list[13], (D, FF), (0.1 * TOKENS ** 0.5), 128.0, ((1, 4),), jnp.float32)
    gate_second = jnp.clip(jnp.exp(math.log(196.608) - 2.0794415 * jax.random.uniform(key_list[14], (D, FF), jnp.float32) ** block_levels(key_list[14], (D, FF), ((1, 4),), -0.2, 0.2)), 24.576, 196.608)
    up_first = centred(key_list[15], (D, FF), (0.1 * TOKENS ** 0.5), 128.0, ((1, 4),), jnp.float32)
    up_second = jnp.clip(jnp.exp(math.log(196.608) - 2.0794415 * jax.random.uniform(key_list[16], (D, FF), jnp.float32) ** block_levels(key_list[16], (D, FF), ((1, 4),), -0.2, 0.2)), 24.576, 196.608)
    down_first = centred(key_list[17], (FF, D), (0.1 * TOKENS ** 0.5), 128.0, ((0, 4),), jnp.float32)
    down_second = jnp.clip(jnp.exp(math.log(196.608) - 2.0794415 * jax.random.uniform(key_list[18], (FF, D), jnp.float32) ** block_levels(key_list[18], (FF, D), ((0, 4),), -0.2, 0.2)), 24.576, 196.608)
    gain_first = centred(key_list[19], (GAINS,), (0.1 * TOKENS ** 0.5), 128.0, ((0, 4),), jnp.float32)
    gain_second = jnp.clip(jnp.exp(math.log(196.608) - 2.0794415 * jax.random.uniform(key_list[20], (GAINS,), jnp.float32) ** block_levels(key_list[20], (GAINS,), ((0, 4),), -0.2, 0.2)), 24.576, 196.608)
    return {"tokens": tokens, "cotangent": cotangent, "segment": segment, "qkv_weight": qkv_weight, "out_weight": out_weight, "gate_weight": gate_weight, "up_weight": up_weight, "down_weight": down_weight, "gains": gains, "qkv_first": qkv_first, "qkv_second": qkv_second, "out_first": out_first, "out_second": out_second, "gate_first": gate_first, "gate_second": gate_second, "up_first": up_first, "up_second": up_second, "down_first": down_first, "down_second": down_second, "gain_first": gain_first, "gain_second": gain_second}


EPS = 1e-06
ADAM_ONE = 0.9
ADAM_TWO = 0.999
ADAM_EPS = 1e-08
MATRIX_DECAY = 0.1
MATRIX_RATE = 0.05
GAIN_RATE = 0.8
ROPE_BASE = 10000.0
HIGH = lax.Precision.HIGHEST

@jax.custom_vjp
def low(v):
    return lax.optimization_barrier(v.astype(jnp.bfloat16)).astype(jnp.float32)

@jax.custom_vjp
def low_back(v):
    return v

def low_keep(v):
    return (low(v), None)

def low_pass(kept, grad):
    return (grad,)

def back_keep(v):
    return (v, None)

def back_low(kept, grad):
    return (low(grad),)
low.defvjp(low_keep, low_pass)
low_back.defvjp(back_keep, back_low)

def rms_norm(value, gain):
    return value * lax.rsqrt(lax.optimization_barrier(jnp.mean(value * value, axis=-1, keepdims=True)) + EPS) * gain

def rotate(value, place):
    half = value.shape[-1] // 2
    freqs = ROPE_BASE ** (-jnp.arange(half, dtype=jnp.float32) * 2.0 / value.shape[-1])
    angle = place.astype(jnp.float32)[..., None] * freqs
    cosine = jnp.concatenate([jnp.cos(angle), jnp.cos(angle)], axis=-1)
    sine = jnp.concatenate([jnp.sin(angle), jnp.sin(angle)], axis=-1)
    turned = jnp.concatenate([-value[..., half:], value[..., :half]], axis=-1)
    return value * cosine + turned * sine

def split_gains(gain_all):
    return (gain_all[0:D], gain_all[D:2 * D], gain_all[2 * D:3 * D], gain_all[3 * D:4 * D], gain_all[4 * D:4 * D + HD], gain_all[4 * D + HD:4 * D + 2 * HD])

def adamw(weight, gradient, first, second, rate, decay):
    first_new = ADAM_ONE * first + (1.0 - ADAM_ONE) * gradient
    second_new = ADAM_TWO * second + (1.0 - ADAM_TWO) * gradient * gradient
    first_hat = first_new / (1.0 - ADAM_ONE ** STEP)
    second_hat = second_new / (1.0 - ADAM_TWO ** STEP)
    weight_new = weight - rate * (first_hat / (jnp.sqrt(second_hat) + ADAM_EPS) + decay * weight)
    return (weight_new, first_new, second_new)

def attend(query, keys, values, labels):
    length = query.shape[0]
    block = min(512, length)
    keys_pad = jnp.concatenate([jnp.zeros((WIN, HD), jnp.float32), keys], axis=0)
    values_pad = jnp.concatenate([jnp.zeros((WIN, HD), jnp.float32), values], axis=0)
    labels_pad = jnp.concatenate([jnp.full((WIN,), -1, jnp.int32), labels], axis=0)
    starts = jnp.arange(length // block, dtype=jnp.int32) * block

    def one_block(start):
        query_part = lax.dynamic_slice_in_dim(query, start, block, 0)
        key_part = lax.dynamic_slice_in_dim(keys_pad, start, block + WIN, 0)
        value_part = lax.dynamic_slice_in_dim(values_pad, start, block + WIN, 0)
        key_label = lax.dynamic_slice_in_dim(labels_pad, start, block + WIN, 0)
        query_label = lax.dynamic_slice_in_dim(labels, start, block, 0)
        scores = low_back(jnp.einsum('thd,kd->htk', query_part, key_part, precision=HIGH) * HD ** (-0.5))
        query_place = start + jnp.arange(block, dtype=jnp.int32)
        key_place = start - WIN + jnp.arange(block + WIN, dtype=jnp.int32)
        allowed = (key_place[None, :] <= query_place[:, None]) & (key_place[None, :] > query_place[:, None] - WIN) & (key_label[None, :] == query_label[:, None])
        probs = low(jax.nn.softmax(jnp.where(allowed[None], scores, -1e+30), axis=-1))
        return jnp.einsum('htk,kd->thd', probs, value_part, precision=HIGH)
    parts = lax.map(jax.checkpoint(one_block), starts)
    return parts.reshape(length, H, HD)

def block_forward(inputs, segment, qkv_mat, out_mat, gate_mat, up_mat, down_mat, gain_vec):
    qkv_low = low(qkv_mat)
    out_low = low(out_mat)
    gate_low = low(gate_mat)
    up_low = low(up_mat)
    down_low = low(down_mat)
    g_in, g_att, g_pre, g_post, g_q, g_k = split_gains(low(gain_vec))

    def one_sequence(pair):
        seq_in, labels = pair
        place = jnp.arange(SEQLEN, dtype=jnp.int32)
        normed = low(rms_norm(seq_in, g_in))
        mixed = low_back(jnp.dot(normed, qkv_low, precision=HIGH))
        query = mixed[:, :H * HD].reshape(SEQLEN, H, HD)
        keys = mixed[:, H * HD:H * HD + HD]
        values = mixed[:, H * HD + HD:]
        query_rot = low(rotate(rms_norm(query, g_q), place[:, None]))
        key_rot = low(rotate(rms_norm(keys, g_k), place))
        value_low = low(values)
        attended = low_back(low(attend(query_rot, key_rot, value_low, labels)))
        projected = low_back(jnp.dot(attended.reshape(SEQLEN, H * HD), out_low, precision=HIGH))
        hidden = seq_in + rms_norm(projected, g_att)
        second = low(rms_norm(hidden, g_pre))
        gate = low_back(jnp.dot(second, gate_low, precision=HIGH))
        up_val = low_back(jnp.dot(second, up_low, precision=HIGH))
        activ = low(jax.nn.gelu(gate, approximate=True) * up_val)
        down_val = low_back(jnp.dot(activ, down_low, precision=HIGH))
        return hidden + rms_norm(down_val, g_post)
    outputs = lax.map(one_sequence, (inputs.reshape(TOKENS // SEQLEN, SEQLEN, D), segment.reshape(TOKENS // SEQLEN, SEQLEN)))
    return outputs.reshape(TOKENS, D)

def reference(tokens, cotangent, segment, qkv_weight, out_weight, gate_weight, up_weight, down_weight, gains, qkv_first, qkv_second, out_first, out_second, gate_first, gate_second, up_first, up_second, down_first, down_second, gain_first, gain_second):
    inputs = tokens.astype(jnp.float32)

    def forward(in_vals, qkv_mat, out_mat, gate_mat, up_mat, down_mat, gain_vec):
        return block_forward(in_vals, segment, qkv_mat, out_mat, gate_mat, up_mat, down_mat, gain_vec)
    output, pullback = jax.vjp(forward, inputs, qkv_weight, out_weight, gate_weight, up_weight, down_weight, gains)
    gradients = pullback(cotangent.astype(jnp.float32))
    qkv_new = adamw(qkv_weight, gradients[1], qkv_first, qkv_second, MATRIX_RATE, MATRIX_DECAY)
    out_new = adamw(out_weight, gradients[2], out_first, out_second, MATRIX_RATE, MATRIX_DECAY)
    gate_new = adamw(gate_weight, gradients[3], gate_first, gate_second, MATRIX_RATE, MATRIX_DECAY)
    up_new = adamw(up_weight, gradients[4], up_first, up_second, MATRIX_RATE, MATRIX_DECAY)
    down_new = adamw(down_weight, gradients[5], down_first, down_second, MATRIX_RATE, MATRIX_DECAY)
    gain_new = adamw(gains, gradients[6], gain_first, gain_second, GAIN_RATE, 0.0)
    return (output.astype(jnp.bfloat16), gradients[0], qkv_new[0], qkv_new[1], qkv_new[2], out_new[0], out_new[1], out_new[2], gate_new[0], gate_new[1], gate_new[2], up_new[0], up_new[1], up_new[2], down_new[0], down_new[1], down_new[2], gain_new[0], gain_new[1], gain_new[2])
```

```python
import functools

import jax
import jax.numpy as jnp
from jax import lax
from jax.experimental import pallas as pl
from jax.experimental.pallas import tpu as pltpu
from jax.sharding import PartitionSpec as P

D = 640
H = 4
HD = 256
WIN = 512
STEP = 10


EPS = 1e-06
ADAM_ONE = 0.9
ADAM_TWO = 0.999
ADAM_EPS = 1e-08
MATRIX_DECAY = 0.1
MATRIX_RATE = 0.05
GAIN_RATE = 0.8
ROPE_BASE = 10000.0


MESH = pl.DeviceIdType.MESH
AXES = 4
SHARD = {"qkv": (640, 384), "out": (256, 640), "gate": (640, 512), "up": (640, 512), "down": (512, 640)}
GATHERED = (
    ("qkv", 0, 256, "y"),
    ("qkv", 256, 128, "z"),
    ("out", 0, 384, "z"),
    ("out", 384, 256, "y"),
    ("gate", 0, 512, "y"),
    ("up", 0, 512, "z"),
    ("down", 0, 384, "y"),
    ("down", 384, 256, "z"),
)
REDUCED = (
    ("down", 0, 256, "y", "y"),
    ("down", 256, 256, "z", "z"),
    ("down", 512, 128, "y", "x"),
    ("gate", 0, 256, "y", "y"),
    ("gate", 256, 128, "z", "z"),
    ("gate", 384, 128, "z", "x"),
    ("up", 0, 256, "z", "z"),
    ("up", 256, 128, "y", "y"),
    ("up", 384, 128, "y", "x"),
    ("out", 0, 256, "y", "y"),
    ("out", 256, 256, "z", "z"),
    ("out", 512, 128, "z", "x"),
    ("qkv", 0, 128, "y", "y"),
    ("qkv", 128, 128, "z", "z"),
    ("qkv", 256, 128, "y", "x"),
)
GATHER_COPIES = len(GATHERED) * 15 + 3
REDUCE_COPIES = len(REDUCED) * 14 + 10
OTHER = {"y": "z", "z": "y"}


def part_rows(name):
    return SHARD[name][0]


class Net:
    def __init__(self, send_sems, recv_sems):
        token = lax.axis_index("seq")
        self.at = {"x": lax.axis_index("wsh"), "y": (token // 2) % 4, "z": token // 8, "c": token % 2}
        self.send_sems, self.recv_sems, self.count, self.started = (send_sems, recv_sems, 0, [])

    def peer(self, axis, by):
        size = 2 if axis == "c" else AXES
        return (self.at[axis] + by) % size

    def device(self, axis, by):
        at = dict(self.at)
        at[axis] = self.peer(axis, by)
        return ((at["z"] * 4 + at["y"]) * 2 + at["c"], at["x"])

    def greet(self):
        barrier = pltpu.get_barrier_semaphore()
        peers = [(axis, by) for axis in "xyz" for by in (1, 2, 3)] + [("c", 1)]
        for axis, by in peers:
            pl.semaphore_signal(
                barrier, inc=1, device_id=self.device(axis, by), device_id_type=MESH
            )
        pl.semaphore_wait(barrier, len(peers))

    def send(self, src, dst, axis, by):
        copy = pltpu.make_async_remote_copy(
            src_ref=src,
            dst_ref=dst,
            send_sem=self.send_sems.at[self.count],
            recv_sem=self.recv_sems.at[self.count],
            device_id=self.device(axis, by),
            device_id_type=MESH,
        )
        self.count += 1
        copy.start()
        self.started.append(copy)
        return copy

    def drain(self):
        for copy in self.started:
            copy.wait_send()


class Gather:
    def __init__(self, net, part, full):
        self.net, (self.name, self.first, self.width, self.axis) = (net, part)
        self.full, self.rows = (full, part_rows(self.name))

    def block(self, x, q):
        eighth = self.rows // 8
        start = pl.multiple_of(self.net.at["c"] * (4 * eighth) + q * eighth, 16)
        return self.full.at[x, pl.ds(start, eighth), pl.ds(self.first, self.width)]

    def half(self, x):
        start = pl.multiple_of(self.net.at["c"] * (self.rows // 2), 16)
        return self.full.at[x, pl.ds(start, self.rows // 2), pl.ds(self.first, self.width)]

    def start(self):
        mine = self.block(self.net.at["x"], self.net.at[self.axis])
        self.along_x = [self.net.send(mine, mine, "x", j) for j in (1, 2, 3)]

    def spread(self):
        self.along_q = []
        for j in (1, 2, 3):
            self.along_x[j - 1].wait_recv()
            got = self.block(self.net.peer("x", -j), self.net.at[self.axis])
            self.along_q.append([self.net.send(got, got, self.axis, k) for k in (1, 2, 3)])

    def share(self):
        self.to_core = []
        for j in (1, 2, 3):
            for copy in self.along_q[j - 1]:
                copy.wait_recv()
            got = self.half(self.net.peer("x", -j))
            self.to_core.append(self.net.send(got, got, "c", 1))

    def finish(self):
        for copy in self.to_core:
            copy.wait_recv()


class Reduce:
    def __init__(self, net, part, grad, core_got, first_got, second_got, third_got, total):
        self.net, (self.name, self.at_column, self.width, self.axis, self.order) = (net, part)
        self.rows, self.grad, self.total = (part_rows(self.name), grad, total)
        self.core_got, self.first_got, self.second_got, self.third_got = (
            core_got,
            first_got,
            second_got,
            third_got,
        )
        self.columns = pl.ds(self.at_column, self.width)
        self.eighth = self.rows // 8
        self.half_start = pl.multiple_of(net.at["c"] * (self.rows // 2), 16)

    def start_of(self, q):
        return pl.multiple_of(self.half_start + q * self.eighth, 16)

    def start(self):
        there = pl.multiple_of((1 - self.net.at["c"]) * (self.rows // 2), 16)
        self.core = self.net.send(
            self.grad.at[:, pl.ds(there, self.rows // 2), self.columns], self.core_got, "c", 1
        )

    def after_core(self):
        self.core.wait_recv()

        def add(step, carry):
            x, block = (step // 4, step % 4)
            local = pl.ds(pl.multiple_of(block * self.eighth, 16), self.eighth)
            rows = pl.ds(self.start_of(block), self.eighth)
            both = self.grad[x, rows, self.columns].astype(jnp.float32) + self.core_got[
                x, local, :
            ].astype(jnp.float32)
            self.grad[x, rows, self.columns] = both.astype(jnp.bfloat16)
            return carry

        lax.fori_loop(0, 16, add, 0)
        self.firsts = []
        for j in (1, 2, 3):
            if self.order == "x":
                src = self.grad.at[
                    self.net.peer("x", j), pl.ds(self.half_start, self.rows // 2), self.columns
                ]
            else:
                rows = pl.ds(self.start_of(self.net.peer(self.axis, j)), self.eighth)
                src = self.grad.at[:, rows, self.columns]
            self.firsts.append(self.net.send(src, self.first_got.at[j - 1], self.order, j))

    def after_first(self):
        for copy in self.firsts:
            copy.wait_recv()
        own = self.net.at[self.axis]

        def add(step, carry):
            if self.order == "x":
                x, rows = (self.net.at["x"], pl.ds(self.start_of(step), self.eighth))
                got = [
                    self.first_got[j, pl.ds(pl.multiple_of(step * self.eighth, 16), self.eighth), :]
                    for j in range(3)
                ]
            else:
                x, rows = (step, pl.ds(self.start_of(own), self.eighth))
                got = [self.first_got[j, step] for j in range(3)]
            total = self.grad[x, rows, self.columns].astype(jnp.float32)
            for piece in got:
                total = total + piece.astype(jnp.float32)
            self.grad[x, rows, self.columns] = total.astype(jnp.bfloat16)
            return carry

        lax.fori_loop(0, 4, add, 0)
        self.seconds = []
        for j in (1, 2, 3):
            if self.order == "x":
                x, q, axis = (self.net.at["x"], self.net.peer(self.axis, j), self.axis)
            else:
                x, q, axis = (self.net.peer("x", j), own, "x")
            src = self.grad.at[x, pl.ds(self.start_of(q), self.eighth), self.columns]
            self.seconds.append(self.net.send(src, self.second_got.at[j - 1], axis, j))

    def after_second(self):
        for copy in self.seconds:
            copy.wait_recv()
        rows = pl.ds(self.start_of(self.net.at[self.axis]), self.eighth)
        total = self.grad[self.net.at["x"], rows, self.columns].astype(jnp.float32)
        for j in range(3):
            total = total + self.second_got[j].astype(jnp.float32)
        last = OTHER[self.axis]
        mine = self.third_got.at[self.net.at[last]]
        mine[...] = total.astype(jnp.bfloat16)
        self.thirds = [self.net.send(mine, mine, last, j) for j in (1, 2, 3)]

    def after_third(self):
        for copy in self.thirds:
            copy.wait_recv()
        rows = pl.ds(self.start_of(self.net.at[self.axis]), self.eighth)
        total = self.third_got[0].astype(jnp.float32)
        for j in range(1, 4):
            total = total + self.third_got[j].astype(jnp.float32)
        mine = self.total.at[rows, self.columns]
        mine[...] = total.astype(jnp.bfloat16)
        self.fourths = [self.net.send(mine, mine, self.axis, j) for j in (1, 2, 3)]

    def share(self):
        for copy in self.fourths:
            copy.wait_recv()
        mine = self.total.at[pl.ds(self.half_start, self.rows // 2), self.columns]
        self.fifth = self.net.send(mine, mine, "c", 1)

    def finish(self):
        self.fifth.wait_recv()


class ReduceGains:
    def __init__(self, net, got):
        self.net, self.got = (net, got)

    def slot(self, stage):
        return self.got.at[stage, self.net.at["cxyz"[stage]]]

    def start(self, value):
        self.slot(0)[...] = value
        self.post(0)

    def post(self, stage):
        axis, mine = ("cxyz"[stage], self.slot(stage))
        self.copies = [
            self.net.send(mine, mine, axis, j) for j in ((1,) if axis == "c" else (1, 2, 3))
        ]

    def step(self, stage):
        for copy in self.copies:
            copy.wait_recv()
        total = self.got[stage, 0] + self.got[stage, 1]
        if stage:
            total = total + self.got[stage, 2] + self.got[stage, 3]
        if stage < 3:
            self.slot(stage + 1)[...] = total
            self.post(stage + 1)
        return total


def gather_kernel(*refs):
    masters, (gain_ref,), fulls, (gain_out,), stages, (send_sems, recv_sems, load_sems) = (
        dict(zip(SHARD, refs[0:5])),
        refs[5:6],
        dict(zip(SHARD, refs[6:11])),
        refs[11:12],
        dict(zip(SHARD, refs[12:17])),
        refs[17:20],
    )
    net = Net(send_sems, recv_sems)
    loads = {}
    for k, name in enumerate(SHARD):
        loads[name] = pltpu.make_async_copy(masters[name], stages[name], load_sems.at[k])
        loads[name].start()
    own = net.at["x"]
    gain_out[own] = gain_ref[...].astype(jnp.bfloat16).astype(jnp.float32)
    net.greet()
    gain_copies = [net.send(gain_out.at[own], gain_out.at[own], "x", j) for j in (1, 2, 3)]
    parts = [Gather(net, part, fulls[part[0]]) for part in GATHERED]
    for name in SHARD:
        loads[name].wait()
        rows = SHARD[name][0] // 8

        def cast(step, carry):
            at = pl.ds(pl.multiple_of(step * rows, 16), rows)
            fulls[name][own, at, :] = stages[name][at, :].astype(jnp.bfloat16)
            return carry

        lax.fori_loop(0, 8, cast, 0)
        for part in parts:
            if part.name == name:
                part.start()
    for part in parts:
        part.spread()
    for part in parts:
        part.share()
    for part in parts:
        part.finish()
    for copy in gain_copies:
        copy.wait_recv()
    net.drain()


def gather_weights(qkv, out, gate, up, down, gains):
    vmem, anywhere = (pl.BlockSpec(memory_space=pltpu.VMEM), pl.BlockSpec(memory_space=pl.ANY))
    gain_rows = jnp.pad(gains.reshape(6, 128), ((0, 2), (0, 0)))
    got = pl.pallas_call(
        gather_kernel,
        out_shape=[
            jax.ShapeDtypeStruct((4, rows, columns), jnp.bfloat16) for rows, columns in SHARD.values()
        ]
        + [jax.ShapeDtypeStruct((4, 8, 128), jnp.float32)],
        in_specs=[anywhere] * 5 + [vmem],
        out_specs=[vmem] * 6,
        scratch_shapes=[pltpu.VMEM(shape, jnp.float32) for shape in SHARD.values()]
        + [
            pltpu.SemaphoreType.DMA((GATHER_COPIES,)),
            pltpu.SemaphoreType.DMA((GATHER_COPIES,)),
            pltpu.SemaphoreType.DMA((5,)),
        ],
        compiler_params=pltpu.CompilerParams(
            collective_id=0, has_side_effects=True, vmem_limit_bytes=60 * 2**20
        ),
        name="gather_weights",
    )(qkv, out, gate, up, down, gain_rows)
    by_column = lambda a: a.transpose(1, 0, 2).reshape(a.shape[1], -1)
    by_row = lambda a: a.reshape(-1, a.shape[2])
    return (
        by_column(got[0]),
        by_row(got[1]),
        by_column(got[2]),
        by_column(got[3]),
        by_row(got[4]),
        got[5][:, :6].reshape(-1),
    )


def reduce_kernel(*refs):
    grads_in, gain_in, totals, gain_total = (
        dict(zip(SHARD, refs[0:5])),
        refs[5],
        dict(zip(SHARD, refs[6:11])),
        refs[11],
    )
    grads, scratch, (gain_got, send_sems, recv_sems, load_sems) = (
        dict(zip(SHARD, refs[12:17])),
        refs[17 : 17 + 4 * len(REDUCED)],
        refs[17 + 4 * len(REDUCED) :],
    )
    net = Net(send_sems, recv_sems)
    loads = {}
    for k, name in enumerate(SHARD):
        loads[name] = pltpu.make_async_copy(grads_in[name], grads[name], load_sems.at[k])
        loads[name].start()
    net.greet()
    gains = ReduceGains(net, gain_got)
    gains.start(gain_in[...])
    parts = [
        Reduce(net, part, grads[part[0]], *scratch[4 * k : 4 * k + 4], totals[part[0]])
        for k, part in enumerate(REDUCED)
    ]
    for name in loads:
        loads[name].wait()
    for part in parts:
        part.start()
    for part in parts:
        part.after_core()
    gains.step(0)
    for part in parts:
        part.after_first()
    gains.step(1)
    for part in parts:
        part.after_second()
    gains.step(2)
    for part in parts:
        part.after_third()
    gain_total[...] = gains.step(3)
    for part in parts:
        part.share()
    for part in parts:
        part.finish()
    net.drain()


def reduce_scratch():
    shapes = []
    for name, _, width, _, order in REDUCED:
        rows = part_rows(name)
        shapes += [
            (4, rows // 2, width),
            (3, rows // 2, width) if order == "x" else (3, 4, rows // 8, width),
            (3, rows // 8, width),
            (4, rows // 8, width),
        ]
    return [pltpu.VMEM(shape, jnp.bfloat16) for shape in shapes]


def reduce_gradients(qkv, out, gate, up, down, gain):
    vmem, anywhere = (pl.BlockSpec(memory_space=pltpu.VMEM), pl.BlockSpec(memory_space=pl.ANY))
    by_column = lambda a: a.reshape(a.shape[0], 4, -1).transpose(1, 0, 2)
    by_row = lambda a: a.reshape(4, -1, a.shape[1])
    gain_rows = jnp.pad(gain.reshape(4, 6, 128), ((0, 0), (0, 2), (0, 0)))
    got = pl.pallas_call(
        reduce_kernel,
        out_shape=[jax.ShapeDtypeStruct(shape, jnp.bfloat16) for shape in SHARD.values()]
        + [jax.ShapeDtypeStruct((4, 8, 128), jnp.float32)],
        in_specs=[anywhere] * 5 + [vmem],
        out_specs=[vmem] * 6,
        scratch_shapes=[pltpu.VMEM((4,) + shape, jnp.bfloat16) for shape in SHARD.values()]
        + reduce_scratch()
        + [
            pltpu.VMEM((4, 4, 4, 8, 128), jnp.float32),
            pltpu.SemaphoreType.DMA((REDUCE_COPIES,)),
            pltpu.SemaphoreType.DMA((REDUCE_COPIES,)),
            pltpu.SemaphoreType.DMA((5,)),
        ],
        compiler_params=pltpu.CompilerParams(
            collective_id=1, has_side_effects=True, vmem_limit_bytes=60 * 2**20
        ),
        name="reduce_gradients",
    )(
        by_column(qkv.astype(jnp.bfloat16)),
        by_row(out.astype(jnp.bfloat16)),
        by_column(gate.astype(jnp.bfloat16)),
        by_column(up.astype(jnp.bfloat16)),
        by_row(down.astype(jnp.bfloat16)),
        gain_rows,
    )
    own = lax.dynamic_index_in_dim(got[5], lax.axis_index("wsh"), 0, keepdims=False)
    return [value.astype(jnp.float32) for value in got[:5]] + [own[:6].reshape(-1)]


def from_behind(x, axis, by):
    count = lax.axis_size(axis)
    pairs = [(i, i + by) for i in range(count) if 0 <= i + by < count]
    return lax.ppermute(x, axis, pairs)


def rms_norm(value, gain):
    return value * lax.rsqrt(jnp.mean(value * value, axis=-1, keepdims=True) + EPS) * gain


def rotate(value, place):
    half = value.shape[-1] // 2
    freqs = ROPE_BASE ** (-jnp.arange(half, dtype=jnp.float32) * 2.0 / value.shape[-1])
    angle = place.astype(jnp.float32)[..., None] * freqs
    cosine = jnp.concatenate([jnp.cos(angle), jnp.cos(angle)], axis=-1)
    sine = jnp.concatenate([jnp.sin(angle), jnp.sin(angle)], axis=-1)
    turned = jnp.concatenate([-value[..., half:], value[..., :half]], axis=-1)
    return value * cosine + turned * sine


def split_gains(gain_all):
    return (
        gain_all[0:D],
        gain_all[D : 2 * D],
        gain_all[2 * D : 3 * D],
        gain_all[3 * D : 4 * D],
        gain_all[4 * D : 4 * D + HD],
        gain_all[4 * D + HD : 4 * D + 2 * HD],
    )


def adamw(weight, gradient, first, second, rate, decay):
    first_new = ADAM_ONE * first + (1.0 - ADAM_ONE) * gradient
    second_new = ADAM_TWO * second + (1.0 - ADAM_TWO) * gradient * gradient
    first_hat = first_new / (1.0 - ADAM_ONE**STEP)
    second_hat = second_new / (1.0 - ADAM_TWO**STEP)
    weight_new = weight - rate * (first_hat / (jnp.sqrt(second_hat) + ADAM_EPS) + decay * weight)
    return (weight_new, first_new, second_new)


def on_device(
    tokens,
    cotangent,
    segment,
    qkv_weight,
    out_weight,
    gate_weight,
    up_weight,
    down_weight,
    gains,
    qkv_first,
    qkv_second,
    out_first,
    out_second,
    gate_first,
    gate_second,
    up_first,
    up_second,
    down_first,
    down_second,
    gain_first,
    gain_second,
):
    tok_rows = tokens.shape[0]
    reach = (WIN - 1) // tok_rows + 1
    w_qkv, w_out, w_gate, w_up, w_down, gain_low = gather_weights(
        qkv_weight, out_weight, gate_weight, up_weight, down_weight, gains
    )
    g_in, g_att, g_pre, g_post, g_q, g_k = split_gains(gain_low.astype(jnp.float32))
    x_in = tokens.astype(jnp.float32)
    base = lax.axis_index("seq") * tok_rows
    place = base + jnp.arange(tok_rows, dtype=jnp.int32)
    normed, in_pull = jax.vjp(rms_norm, x_in, g_in)
    normed_low = normed.astype(jnp.bfloat16)
    mixed = jnp.dot(normed_low, w_qkv, preferred_element_type=jnp.float32)
    q_raw = mixed[:, : H * HD].reshape(tok_rows, H, HD)
    k_raw = mixed[:, H * HD : H * HD + HD]
    v_raw = mixed[:, H * HD + HD :]

    def query_piece(raw, gain):
        return rotate(rms_norm(raw, gain), place[:, None])

    def key_piece(raw, gain):
        return rotate(rms_norm(raw, gain), place)

    q_rot, query_pull = jax.vjp(query_piece, q_raw, g_q)
    k_rot, key_pull = jax.vjp(key_piece, k_raw, g_k)
    query_low = q_rot.astype(jnp.bfloat16)
    own_kv = jnp.concatenate([k_rot.astype(jnp.bfloat16), v_raw.astype(jnp.bfloat16)], axis=1)
    own_ids = segment.astype(jnp.bfloat16)
    fetched = [from_behind((own_kv, own_ids), "seq", distance) for distance in range(reach, 0, -1)]
    key_vals = jnp.concatenate([piece[0] for piece in fetched] + [own_kv], axis=0)
    key_ids = jnp.concatenate([piece[1] for piece in fetched] + [own_ids], axis=0)
    keys_low = key_vals[:, :HD]
    values_low = key_vals[:, HD:]
    key_place = base - reach * tok_rows + jnp.arange((reach + 1) * tok_rows, dtype=jnp.int32)
    allowed = (
        (key_place[None, :] <= place[:, None])
        & (key_place[None, :] > place[:, None] - WIN)
        & (key_place[None, :] >= 0)
        & (key_ids[None, :] == own_ids[:, None])
    )
    scale = HD ** (-0.5)
    scores = (
        jnp.einsum("thd,kd->htk", query_low, keys_low, preferred_element_type=jnp.float32) * scale
    )
    probs = jax.nn.softmax(jnp.where(allowed[None], scores, -1e30), axis=-1)
    probs_low = probs.astype(jnp.bfloat16)
    attended = jnp.einsum("htk,kd->thd", probs_low, values_low, preferred_element_type=jnp.float32)
    att_low = attended.astype(jnp.bfloat16).reshape(tok_rows, H * HD)
    projected = jnp.dot(att_low, w_out, preferred_element_type=jnp.float32)
    branch_one, att_pull = jax.vjp(rms_norm, projected, g_att)
    hidden = x_in + branch_one
    normed_two, pre_pull = jax.vjp(rms_norm, hidden, g_pre)
    second_low = normed_two.astype(jnp.bfloat16)
    gate_val = jnp.dot(second_low, w_gate, preferred_element_type=jnp.float32)
    up_val = jnp.dot(second_low, w_up, preferred_element_type=jnp.float32)

    def gated(gate_in, up_in):
        return jax.nn.gelu(gate_in, approximate=True) * up_in

    activ, glu_pull = jax.vjp(gated, gate_val, up_val)
    activ_low = activ.astype(jnp.bfloat16)
    down_val = jnp.dot(activ_low, w_down, preferred_element_type=jnp.float32)
    branch_two, post_pull = jax.vjp(rms_norm, down_val, g_post)
    block_output = (hidden + branch_two).astype(jnp.bfloat16)
    grad_output = cotangent.astype(jnp.float32)
    grad_down, grad_post = post_pull(grad_output)
    down_low = grad_down.astype(jnp.bfloat16)
    down_grad = jnp.dot(activ_low.T, down_low, preferred_element_type=jnp.float32)
    grad_act = jnp.dot(down_low, w_down.T, preferred_element_type=jnp.float32)
    grad_gate, grad_up = glu_pull(grad_act)
    gate_low = grad_gate.astype(jnp.bfloat16)
    up_low = grad_up.astype(jnp.bfloat16)
    gate_grad = jnp.dot(second_low.T, gate_low, preferred_element_type=jnp.float32)
    up_grad = jnp.dot(second_low.T, up_low, preferred_element_type=jnp.float32)
    grad_second = jnp.dot(gate_low, w_gate.T, preferred_element_type=jnp.float32) + jnp.dot(
        up_low, w_up.T, preferred_element_type=jnp.float32
    )
    grad_hidden_part, grad_pre = pre_pull(grad_second)
    grad_hidden = grad_output + grad_hidden_part
    grad_proj, grad_att_gain = att_pull(grad_hidden)
    proj_low = grad_proj.astype(jnp.bfloat16)
    out_grad = jnp.dot(att_low.T, proj_low, preferred_element_type=jnp.float32)
    grad_att = (
        jnp.dot(proj_low, w_out.T, preferred_element_type=jnp.float32)
        .astype(jnp.bfloat16)
        .reshape(tok_rows, H, HD)
    )
    grad_probs = jnp.einsum("thd,kd->htk", grad_att, values_low, preferred_element_type=jnp.float32)
    grad_scores = probs * (grad_probs - jnp.sum(grad_probs * probs, axis=-1, keepdims=True))
    scores_low = grad_scores.astype(jnp.bfloat16)
    grad_query = (
        jnp.einsum("htk,kd->thd", scores_low, keys_low, preferred_element_type=jnp.float32) * scale
    )
    grad_keys = (
        jnp.einsum("htk,thd->kd", scores_low, query_low, preferred_element_type=jnp.float32) * scale
    )
    grad_values = jnp.einsum("htk,thd->kd", probs_low, grad_att, preferred_element_type=jnp.float32)
    grad_kv = jnp.concatenate([grad_keys, grad_values], axis=1)
    own_grad = grad_kv[reach * tok_rows :]
    for distance in range(1, reach + 1):
        piece_grad = grad_kv[(reach - distance) * tok_rows : (reach - distance + 1) * tok_rows]
        own_grad = own_grad + from_behind(piece_grad.astype(jnp.bfloat16), "seq", -distance).astype(
            piece_grad.dtype
        )
    grad_k_raw, grad_k_gain = key_pull(own_grad[:, :HD])
    grad_q_raw, grad_q_gain = query_pull(grad_query)
    grad_mixed = jnp.concatenate(
        [grad_q_raw.reshape(tok_rows, H * HD), grad_k_raw, own_grad[:, HD:]], axis=1
    ).astype(jnp.bfloat16)
    qkv_grad = jnp.dot(normed_low.T, grad_mixed, preferred_element_type=jnp.float32)
    grad_normed = jnp.dot(grad_mixed, w_qkv.T, preferred_element_type=jnp.float32)
    grad_in_part, grad_in_gain = in_pull(grad_normed)
    input_grad = grad_hidden + grad_in_part
    gain_grad = jnp.concatenate(
        [grad_in_gain, grad_att_gain, grad_pre, grad_post, grad_q_gain, grad_k_gain]
    )
    masters = (qkv_weight, out_weight, gate_weight, up_weight, down_weight, gains)
    firsts = (qkv_first, out_first, gate_first, up_first, down_first, gain_first)
    seconds = (qkv_second, out_second, gate_second, up_second, down_second, gain_second)
    rates = (MATRIX_RATE, MATRIX_RATE, MATRIX_RATE, MATRIX_RATE, MATRIX_RATE, GAIN_RATE)
    decays = (MATRIX_DECAY, MATRIX_DECAY, MATRIX_DECAY, MATRIX_DECAY, MATRIX_DECAY, 0.0)
    fresh = []
    summed = reduce_gradients(qkv_grad, out_grad, gate_grad, up_grad, down_grad, gain_grad)
    for index in range(6):
        fresh.extend(
            adamw(
                masters[index],
                summed[index],
                firsts[index],
                seconds[index],
                rates[index],
                decays[index],
            )
        )
    return (block_output, input_grad) + tuple(fresh)


def solution(mesh):
    placed = (
        P(("wsh", "seq"), None),
        P(("wsh", "seq"), None),
        P(("wsh", "seq")),
        P(None, "wsh"),
        P("wsh", None),
        P(None, "wsh"),
        P(None, "wsh"),
        P("wsh", None),
        P("wsh"),
        P(None, "wsh"),
        P(None, "wsh"),
        P("wsh", None),
        P("wsh", None),
        P(None, "wsh"),
        P(None, "wsh"),
        P(None, "wsh"),
        P(None, "wsh"),
        P("wsh", None),
        P("wsh", None),
        P("wsh"),
        P("wsh"),
    )
    return jax.shard_map(
        on_device,
        mesh=mesh,
        in_specs=placed,
        out_specs=(
            P(("wsh", "seq"), None),
            P(("wsh", "seq"), None),
            P(None, "wsh"),
            P(None, "wsh"),
            P(None, "wsh"),
            P("wsh", None),
            P("wsh", None),
            P("wsh", None),
            P(None, "wsh"),
            P(None, "wsh"),
            P(None, "wsh"),
            P(None, "wsh"),
            P(None, "wsh"),
            P(None, "wsh"),
            P("wsh", None),
            P("wsh", None),
            P("wsh", None),
            P("wsh"),
            P("wsh"),
            P("wsh"),
        ),
        check_vma=False,
    )
```

```python
import types

import jax
import jax.numpy as jnp
import numpy as np
from jax import lax
from jax.experimental import pallas as pl
from jax.experimental.pallas import tpu as pltpu
from jax.sharding import PartitionSpec as P

D = 640
H = 4
HD = 256
WIN = 512
STEP = 10


EPS = 1e-06
ADAM_ONE = 0.9
ADAM_TWO = 0.999
ADAM_EPS = 1e-08
MATRIX_DECAY = 0.1
MATRIX_RATE = 0.05
GAIN_RATE = 0.8
ROPE_BASE = 10000.0


VMEM_BYTES = 64 * 2**20
BF, F32 = (jnp.bfloat16, jnp.float32)
MESH = pl.DeviceIdType.MESH
AXES = 4
QKV, OUT, GATE, UP, DOWN = range(5)
SHARD = ((640, 384), (256, 640), (640, 512), (640, 512), (512, 640))
GATHERED = (
    ((0, 128, "y"), (128, 256, "z")),
    ((0, 640, ""),),
    ((0, 512, "y"),),
    ((0, 512, "z"),),
    ((0, 384, "y"), (384, 256, "z")),
)
REDUCED = (
    ((0, 128, "y", "y"), (128, 128, "z", "z"), (256, 128, "y", "x")),
    ((0, 128, "y", "y"), (128, 256, "z", "z"), (384, 256, "y", "x")),
    ((0, 256, "y", "y"), (256, 128, "z", "z"), (384, 128, "z", "x")),
    ((0, 128, "y", "y"), (128, 256, "z", "z"), (384, 128, "y", "x")),
    ((0, 256, "y", "y"), (256, 128, "z", "z"), (384, 256, "z", "x")),
)
OTHER = {"y": "z", "z": "y"}
PEERS = (1, 2, 3)


class Net:
    def __init__(self, send_sems, recv_sems):
        token = lax.axis_index("seq")
        self.at = {"x": lax.axis_index("wsh"), "y": (token // 2) % 4, "z": token // 8, "c": token % 2}
        self.send_sems, self.recv_sems, self.count, self.started = (send_sems, recv_sems, 0, [])

    def peer(self, axis, by):
        size = 2 if axis == "c" else AXES
        return (self.at[axis] + by) % size

    def device(self, axis, by):
        if axis == "seq":
            return ((lax.axis_index("seq") + by) % 32, self.at["x"])
        at = dict(self.at)
        at[axis] = self.peer(axis, by)
        return ((at["z"] * 4 + at["y"]) * 2 + at["c"], at["x"])

    def greet(self):
        barrier = pltpu.get_barrier_semaphore()
        peers = [(axis, by) for axis in "xyz" for by in PEERS] + [("c", 1)]
        peers += [("seq", by) for by in (1, 2, -1, -2)]
        for axis, by in peers:
            pl.semaphore_signal(
                barrier, inc=1, device_id=self.device(axis, by), device_id_type=MESH
            )
        pl.semaphore_wait(barrier, len(peers))

    def batch(self, size):
        made = Batch(self, size, self.send_sems.at[self.count], self.recv_sems.at[self.count])
        self.count += 1
        self.started.append(made)
        return made

    def send(self, src, dst, axis, by):
        return self.batch(src).add(src, dst, axis, by)

    def drain(self):
        for made in self.started:
            pltpu.make_async_copy(made.size, made.size, made.send_sem).wait()
        self.started = []


class Batch:
    def __init__(self, net, size, send_sem, recv_sem):
        self.net, self.size, self.send_sem, self.recv_sem = (net, size, send_sem, recv_sem)

    def add(self, src, dst, axis, by):
        pltpu.make_async_remote_copy(
            src_ref=src,
            dst_ref=dst,
            send_sem=self.send_sem,
            recv_sem=self.recv_sem,
            device_id=self.net.device(axis, by),
            device_id_type=MESH,
        ).start()
        return self

    def arrived(self):
        pltpu.make_async_copy(self.size, self.size, self.recv_sem).wait()


class Gather:
    def __init__(self, net, weight, full):
        self.net, self.full, (self.rows, _), self.parts = (
            net,
            full,
            SHARD[weight],
            GATHERED[weight],
        )
        self.eighth, self.direct = (self.rows // 8, not self.parts[0][2])

    def block(self, x, part):
        first, width, axis = part
        at, count = (net_half(self.net, self.rows), self.rows // 2)
        if axis:
            at, count = (at + self.net.at[axis] * self.eighth, self.eighth)
        return self.full.at[x, pl.ds(pl.multiple_of(at, 16), count), pl.ds(first, width)]

    def start(self):
        each = self.rows // 2 if self.direct else self.eighth
        self.along_x = self.net.batch(self.full.at[0:3, pl.ds(0, each), :])
        for part in self.parts:
            mine = self.block(self.net.at["x"], part)
            for j in PEERS:
                self.along_x.add(mine, mine, "x", j)

    def spread(self):
        self.along_x.arrived()
        self.along_q = self.net.batch(self.full.at[0:3, pl.ds(0, 3 * self.eighth), :])
        for j in PEERS:
            for part in self.parts:
                got = self.block(self.net.peer("x", -j), part)
                for k in PEERS:
                    self.along_q.add(got, got, part[2], k)

    def share(self):
        (self.along_x if self.direct else self.along_q).arrived()
        half = self.rows // 2
        self.to_core = self.net.batch(self.full.at[0:3, pl.ds(0, half), :])
        for j in PEERS:
            got = self.full.at[self.net.peer("x", -j), pl.ds(net_half(self.net, self.rows), half), :]
            self.to_core.add(got, got, "c", 1)

    def finish(self):
        self.to_core.arrived()


def net_half(net, rows):
    return pl.multiple_of(net.at["c"] * (rows // 2), 16)


class Reduce:
    def __init__(self, net, weight, grad, core_got, got, total):
        self.net, self.grad, self.core_got, self.total = (net, grad, core_got, total)
        self.rows, self.columns = SHARD[weight]
        self.parts = [
            (pl.ds(first, width), axis, order, got[3 * k : 3 * k + 3])
            for k, (first, width, axis, order) in enumerate(REDUCED[weight])
        ]
        self.half, self.eighth = (self.rows // 2, self.rows // 8)
        self.half_start = net_half(net, self.rows)
        self.core, self.firsts = ([], None)

    def block(self, q):
        return pl.ds(pl.multiple_of(self.half_start + q * self.eighth, 16), self.eighth)

    def start(self, x):
        there = pl.multiple_of((1 - self.net.at["c"]) * self.half, 16)
        mine = self.grad.at[x, pl.ds(there, self.half), :]
        self.core.append(self.net.batch(mine).add(mine, self.core_got.at[x], "c", 1))

    def pair(self, x):
        self.core.pop(0).arrived()

        def add(block, carry):
            local = pl.ds(pl.multiple_of(block * self.eighth, 16), self.eighth)
            rows = self.block(block)
            both = self.grad[x, rows, :].astype(F32) + self.core_got[x, local, :].astype(F32)
            self.grad[x, rows, :] = both.astype(BF)
            return carry

        lax.fori_loop(0, 4, add, 0)
        if self.firsts is None:
            self.firsts = self.net.batch(self.grad.at[0:3, pl.ds(0, self.half), :])
        for columns, axis, order, got in self.parts:
            if order != "x":
                for j in PEERS:
                    src = self.grad.at[x, self.block(self.net.peer(axis, j)), columns]
                    self.firsts.add(src, got[0].at[j - 1, x], order, j)

    def along_x(self, j):
        for columns, axis, order, got in self.parts:
            if order == "x":
                rows = pl.ds(self.half_start, self.half)
                src = self.grad.at[self.net.peer("x", j), rows, columns]
                self.firsts.add(src, got[0].at[j - 1], order, j)

    def after_first(self):
        self.firsts.arrived()
        self.seconds = self.net.batch(self.grad.at[0, pl.ds(0, 3 * self.eighth), :])
        for columns, axis, order, got in self.parts:
            own = self.net.at[axis]

            def add(step, carry):
                if order == "x":
                    x, rows = (self.net.at["x"], self.block(step))
                    local = pl.ds(pl.multiple_of(step * self.eighth, 16), self.eighth)
                    pieces = [got[0][j, local, :] for j in range(3)]
                else:
                    x, rows = (step, self.block(own))
                    pieces = [got[0][j, step] for j in range(3)]
                total = self.grad[x, rows, columns].astype(F32)
                for piece in pieces:
                    total = total + piece.astype(F32)
                self.grad[x, rows, columns] = total.astype(BF)
                return carry

            lax.fori_loop(0, 4, add, 0)
            for j in PEERS:
                if order == "x":
                    x, q, along = (self.net.at["x"], self.net.peer(axis, j), axis)
                else:
                    x, q, along = (self.net.peer("x", j), own, "x")
                src = self.grad.at[x, self.block(q), columns]
                self.seconds.add(src, got[1].at[j - 1], along, j)

    def after_second(self):
        self.seconds.arrived()
        self.thirds = self.net.batch(self.grad.at[0, pl.ds(0, 3 * self.eighth), :])
        for columns, axis, order, got in self.parts:
            rows = self.block(self.net.at[axis])
            total = self.grad[self.net.at["x"], rows, columns].astype(F32)
            for j in range(3):
                total = total + got[1][j].astype(F32)
            mine = got[2].at[self.net.at[OTHER[axis]]]
            mine[...] = total.astype(BF)
            for j in PEERS:
                self.thirds.add(mine, mine, OTHER[axis], j)

    def after_third(self):
        self.thirds.arrived()
        self.fourths = self.net.batch(self.grad.at[0, pl.ds(0, 3 * self.eighth), :])
        for columns, axis, order, got in self.parts:
            total = got[2][0].astype(F32)
            for j in PEERS:
                total = total + got[2][j].astype(F32)
            mine = self.total.at[self.block(self.net.at[axis]), columns]
            mine[...] = total.astype(BF)
            for j in PEERS:
                self.fourths.add(mine, mine, axis, j)

    def share(self):
        self.fourths.arrived()
        mine = self.total.at[pl.ds(self.half_start, self.half), :]
        self.fifth = self.net.batch(mine).add(mine, mine, "c", 1)

    def finish(self):
        self.fifth.arrived()


class ReduceGains:
    def __init__(self, net, got):
        self.net, self.got = (net, got)

    def start(self, value):
        self.post(0, value)

    def post(self, stage, value):
        axis, peers = ("cxyz"[stage], PEERS if stage else (1,))
        mine = self.got.at[stage, self.net.at[axis]]
        mine[...] = value
        self.copies = self.net.batch(self.got.at[0, 0 : len(peers)])
        for j in peers:
            self.copies.add(mine, mine, axis, j)

    def step(self, stage):
        self.copies.arrived()
        total = self.got[stage, 0] + self.got[stage, 1]
        if stage:
            total = total + self.got[stage, 2] + self.got[stage, 3]
        if stage < 3:
            self.post(stage + 1, total)
        return total


def reduce_scratch():
    shapes = []
    for (rows, columns), parts in zip(SHARD, REDUCED):
        shapes.append((4, rows // 2, columns))
        for _, width, _, order in parts:
            shapes += [
                (3, rows // 2, width) if order == "x" else (3, 4, rows // 8, width),
                (3, rows // 8, width),
                (4, rows // 8, width),
            ]
    return [pltpu.VMEM(shape, BF) for shape in shapes]


TOK = 384
BEHIND = 512
KEYS = 640
G_IN, G_ATT, G_PRE, G_POST, G_Q, G_K = range(6)
NORM_ROWS = ((0, 5), (5, 5), (10, 5), (15, 5), (20, 2), (22, 2))

SCRATCH = (
    ("g_qkv", (4,) + SHARD[QKV], BF),
    ("x_ext", (BEHIND + TOK, D), BF),
    ("normed", (BEHIND + TOK, D), BF),
    ("cos", (BEHIND + TOK, 128), F32),
    ("sin", (BEHIND + TOK, 128), F32),
    ("mixed", (TOK, 1024), BF),
    ("k_raw", (BEHIND + TOK, HD), BF),
    ("q_rot", (3, 512, HD), BF),
    ("k_ext", (BEHIND + TOK, HD), BF),
    ("v_ext", (BEHIND + TOK, HD), BF),
    ("exps", (3, 512, KEYS), BF),
    ("scores", (512, KEYS), F32),
    ("bias", (128, KEYS), F32),
    ("inverse", (3, 512, 1), F32),
    ("att", (TOK, H * HD), BF),
    ("proj", (TOK, D), F32),
    ("hidden", (TOK, D), F32),
    ("wide", (TOK, D), F32),
    ("second", (TOK, D), BF),
    ("flip", (D, BEHIND + TOK), BF),
    ("activ", (TOK, 2048), BF),
    ("d_gate", (TOK, 2048), BF),
    ("d_up", (TOK, 2048), BF),
    ("low", (TOK, D), BF),
    ("cot", (TOK, D), BF),
    ("out_low", (TOK, D), BF),
    ("d_att", (3, 512, HD), BF),
    ("d_scores", (512, KEYS), BF),
    ("dkv", (BEHIND + TOK, 2 * HD), F32),
    ("d_kv", (BEHIND + TOK, 2 * HD), BF),
    ("halo_one", (TOK, 2 * HD), BF),
    ("halo_two", (128, 2 * HD), BF),
    ("d_mixed", (TOK, 1536), BF),
    ("gain_all", (4, 8, 128), F32),
    ("gain_grad", (4, 8, 128), F32),
    ("gain_got", (4, 4, 4, 8, 128), F32),
    ("ids", (8, 128), jnp.int32),
    ("ids_one", (8, 128), jnp.int32),
    ("ids_two", (8, 128), jnp.int32),
)
COPIES = 5 * 3 - 1 + 5 * 9 + 6 + 5
LOADS = 14


def nt(a, b):
    return lax.dot_general(a, b, (((1,), (1,)), ((), ())), preferred_element_type=F32)


def nn(a, b):
    return jnp.dot(a, b, preferred_element_type=F32)


def inverse_rms(value):
    return lax.rsqrt(jnp.mean(value * value, axis=-1, keepdims=True) + EPS)


def rms_back(value, gain, grad):
    scale = inverse_rms(value)
    unit = value * scale
    weighted = grad * gain
    back = scale * (weighted - unit * jnp.mean(weighted * unit, axis=-1, keepdims=True))
    return back, jnp.sum(grad * unit, axis=0, keepdims=True)


def turn(value, cosine, sine):
    first, last = (value[:, :128], value[:, 128:])
    return jnp.concatenate([first * cosine - last * sine, last * cosine + first * sine], axis=1)


def turn_back(grad, cosine, sine):
    first, last = (grad[:, :128], grad[:, 128:])
    return jnp.concatenate([first * cosine + last * sine, last * cosine - first * sine], axis=1)


def block_kernel(*refs):
    taken = iter(refs)
    r, take = (types.SimpleNamespace(), lambda count: [next(taken) for _ in range(count)])
    r.tokens, r.cotangent, r.segment, r.gains, r.freqs = take(5)
    r.masters = take(5)
    r.block_output, r.input_grad, r.s_gains = take(3)
    r.sums = take(5)
    w, r.totals, r.fulls = (take(5), take(5), take(5))
    for name, _, _ in SCRATCH:
        setattr(r, name, next(taken))
    pieces = [take(1 + 3 * len(parts)) for parts in REDUCED]
    send_sems, recv_sems, load_sems = take(3)
    net = Net(send_sems, recv_sems)
    own_x = net.at["x"]
    base = lax.axis_index("seq") * TOK
    loads = []

    def local(src, dst):
        copy = pltpu.make_async_copy(src, dst, load_sems.at[len(loads)])
        loads.append(copy)
        copy.start()
        return copy

    def chunks(count, body, carry=0):
        return lax.fori_loop(
            0, count, lambda i, kept: body(pl.ds(pl.multiple_of(i * 128, 128), 128), i, kept), carry
        )

    own_rows = pl.ds(BEHIND, TOK)
    fill = {QKV: local(r.masters[QKV], r.fulls[QKV])}
    fill_tokens = local(r.tokens, r.x_ext.at[own_rows])
    for name in (OUT, GATE, UP, DOWN):
        fill[name] = local(r.masters[name], r.fulls[name])
    fill_cot = local(r.cotangent, r.cot)
    r.gain_all[...] = jnp.zeros((4, 8, 128), F32)
    r.gain_grad[...] = jnp.zeros((4, 8, 128), F32)
    r.gain_all[own_x, 0:6] = r.gains[...].astype(BF).astype(F32)
    r.ids[...] = jnp.zeros((8, 128), jnp.int32)
    r.ids[0:3] = r.segment[...]
    net.greet()

    mine = r.gain_all.at[own_x]
    gain_copies = net.batch(r.gain_all.at[0:3])
    for j in PEERS:
        gain_copies.add(mine, mine, "x", j)
    parts = [Gather(net, name, w[name]) for name in range(5)]

    def launch(name):
        fill[name].wait()
        rows = SHARD[name][0] // 8

        def cast(step, carry):
            at = pl.ds(pl.multiple_of(step * rows, 16), rows)
            w[name][own_x, at, :] = r.fulls[name][at, :].astype(BF)
            return carry

        lax.fori_loop(0, 8, cast, 0)
        parts[name].start()

    def arrive(step, *which):
        for name in which:
            step(parts[name])

    launch(QKV)
    fill_tokens.wait()
    halo_copies = [
        net.send(r.x_ext.at[own_rows], r.x_ext.at[pl.ds(128, TOK)], "seq", 1),
        net.send(r.x_ext.at[pl.ds(BEHIND + 256, 128)], r.x_ext.at[pl.ds(0, 128)], "seq", 2),
        net.send(r.ids, r.ids_one, "seq", 1),
        net.send(r.ids, r.ids_two, "seq", 2),
    ]

    def angles(rows, i, kept):
        place = (base - BEHIND + i * 128 + lax.broadcasted_iota(jnp.int32, (128, 128), 0)).astype(F32)
        angle = place * r.freqs[...]
        r.cos[rows, :] = jnp.cos(angle)
        r.sin[rows, :] = jnp.sin(angle)
        return kept

    chunks(7, angles)
    launch(GATE)
    launch(UP)
    arrive(Gather.spread, QKV, GATE, UP)
    launch(DOWN)
    launch(OUT)
    gain_copies.arrived()
    gain = {}
    for name, (first, count) in enumerate(NORM_ROWS):
        rows = [(k // 6, k % 6) for k in range(first, first + count)]
        gain[name] = jnp.concatenate([r.gain_all[g, k : k + 1, :] for g, k in rows], axis=1)

    def put_gain(name, value):
        first, count = NORM_ROWS[name]
        for k in range(count):
            g, row = ((first + k) // 6, (first + k) % 6)
            r.gain_grad[g, row : row + 1, :] = value[:, 128 * k : 128 * (k + 1)]

    for copy in halo_copies:
        copy.arrived()

    def normalise(rows, i, kept):
        value = r.x_ext[rows, :].astype(F32)
        r.normed[rows, :] = (value * inverse_rms(value) * gain[G_IN]).astype(BF)
        return kept

    chunks(7, normalise)
    arrive(Gather.share, QKV)
    arrive(Gather.spread, DOWN)
    arrive(Gather.finish, QKV)

    normed_own = r.normed[own_rows, :]
    for x in range(4):
        width = 384 if x < 2 else (256 if x == 2 else 0)
        if width:
            r.mixed[:, x * 384 : x * 384 + width] = nn(
                normed_own, w[QKV][x, :, :width]
            ).astype(BF)
    normed_all = r.normed[...]
    r.dkv[:, 0:128] = nn(normed_all, w[QKV][2, :, 256:384])
    tail = nn(normed_all, w[QKV][3])
    r.dkv[:, 128:256] = tail[:, :128]
    r.v_ext[...] = tail[:, 128:].astype(BF)
    r.k_raw[...] = r.dkv[:, 0:256].astype(BF)

    def keys(rows, i, kept):
        value = r.dkv[rows, 0:256]
        value = value * inverse_rms(value) * gain[G_K]
        r.k_ext[rows, :] = turn(value, r.cos[rows, :], r.sin[rows, :]).astype(BF)
        return kept

    chunks(7, keys)

    def own_turn(i):
        at = pl.ds(pl.multiple_of(BEHIND + i * 128, 128), 128)
        return r.cos[at, :], r.sin[at, :]

    def queries(rows, i, kept):
        for h in range(H):
            value = r.mixed[rows, h * HD : (h + 1) * HD].astype(F32)
            value = value * inverse_rms(value) * gain[G_Q]
            r.q_rot[i, h * 128 : (h + 1) * 128, :] = (
                turn(value, *own_turn(i)) * HD**-0.5
            ).astype(BF)
        return kept

    chunks(3, queries)
    arrive(Gather.share, OUT)

    id_rows = [r.ids_two[2:3, :]] + [r.ids_one[k : k + 1, :] for k in range(3)]
    id_rows = [row.astype(F32) for row in id_rows + [r.ids[k : k + 1, :] for k in range(3)]]

    def attend(b):
        down_rows = lax.broadcasted_iota(jnp.int32, (128, 128), 0)
        across = lax.broadcasted_iota(jnp.int32, (128, 128), 1)
        own_id = jnp.broadcast_to(id_rows[4 + b], (128, 128)).T
        for j in range(5):
            allowed = jnp.broadcast_to(id_rows[b + j], (128, 128)) == own_id
            allowed = allowed & (base - BEHIND + (b + j) * 128 + across >= 0)
            if j == 0:
                allowed = allowed & (across > down_rows)
            if j == 4:
                allowed = allowed & (across <= down_rows)
            r.bias[:, j * 128 : (j + 1) * 128] = jnp.where(allowed, 0.0, -1e30)
        window = pl.ds(b * 128, KEYS)
        r.scores[...] = nt(r.q_rot[b], r.k_ext[window, :])
        for h in range(H):
            rows = pl.ds(h * 128, 128)
            weight = jnp.exp(r.scores[rows, :] + r.bias[...])
            r.inverse[b, rows, :] = 1.0 / jnp.sum(weight, axis=1, keepdims=True)
            r.exps[b, rows, :] = weight.astype(BF)
        mean = nn(r.exps[b], r.v_ext[window, :]) * r.inverse[b]
        for h in range(H):
            r.att[pl.ds(b * 128, 128), h * HD : (h + 1) * HD] = mean[
                h * 128 : (h + 1) * 128, :
            ].astype(BF)

    attend(0)
    attend(1)
    attend(2)
    arrive(Gather.share, GATE, UP)
    arrive(Gather.finish, OUT)
    r.proj[...] = nn(r.att[...], w[OUT][...].reshape(H * HD, D))

    def residual(rows, i, kept):
        value = r.proj[rows, :]
        hidden = r.x_ext[pl.ds(pl.multiple_of(BEHIND + i * 128, 128), 128), :].astype(F32)
        hidden = hidden + value * inverse_rms(value) * gain[G_ATT]
        r.hidden[rows, :] = hidden
        r.second[rows, :] = (hidden * inverse_rms(hidden) * gain[G_PRE]).astype(BF)
        return kept

    chunks(3, residual)

    def widen(step, kept):
        x, part = ((own_x + step // 2) % 4, step % 2)
        inner = pl.ds(pl.multiple_of(part * 256, 256), 256)
        columns = pl.ds(pl.multiple_of(x * 512 + part * 256, 256), 256)
        gate = nn(r.second[...], w[GATE][x, :, inner])
        up = nn(r.second[...], w[UP][x, :, inner])
        square = gate * gate
        bend = jnp.tanh(gate * (0.7978845608028654 + 0.7978845608028654 * 0.044715 * square))
        half = 0.5 + 0.5 * bend
        gelu = gate * half
        slope = half + (0.5 * gate) * (1.0 - bend * bend) * (
            0.7978845608028654 + 3.0 * 0.7978845608028654 * 0.044715 * square
        )
        r.activ[:, columns] = (gelu * up).astype(BF)
        r.d_gate[:, columns] = (slope * up).astype(BF)
        r.d_up[:, columns] = gelu.astype(BF)
        return kept

    lax.fori_loop(0, 2, widen, 0)
    arrive(Gather.finish, GATE, UP)
    arrive(Gather.share, DOWN)
    lax.fori_loop(2, 8, widen, 0)
    arrive(Gather.finish, DOWN)
    r.wide[...] = nn(r.activ[...], w[DOWN][...].reshape(2048, D))
    fill_cot.wait()

    def finish_forward(rows, i, kept):
        value = r.wide[rows, :]
        ended = r.hidden[rows, :] + value * inverse_rms(value) * gain[G_POST]
        r.out_low[rows, :] = ended.astype(BF)
        back, d_gain = rms_back(value, gain[G_POST], r.cot[rows, :].astype(F32))
        r.low[rows, :] = back.astype(BF)
        return kept + d_gain

    none = jnp.zeros((1, D), F32)
    put_gain(G_POST, chunks(3, finish_forward, none))
    store_out = local(r.out_low, r.block_output)
    net.drain()

    sums = [
        Reduce(net, k, r.g_qkv if k == QKV else w[k], pieces[k][0], pieces[k][1:], r.totals[k])
        for k in range(5)
    ]

    def reduce(step, *which):
        for name in which:
            step(sums[name])

    def paired(name, i):
        sums[name].pair((own_x + 1 + i) % 4)
        if i < 3:
            sums[name].along_x(i + 1)

    for i in range(4):
        x = (own_x + 1 + i) % 4
        columns = pl.ds(pl.multiple_of(x * 512, 512), 512)
        d_act = nt(r.low[...], w[DOWN][x])
        r.d_gate[:, columns] = (d_act * r.d_gate[:, columns].astype(F32)).astype(BF)
        r.d_up[:, columns] = (d_act * r.d_up[:, columns].astype(F32)).astype(BF)
        w[DOWN][x] = nn(r.activ[:, columns].T, r.low[...]).astype(BF)
        sums[DOWN].start(x)
        if i:
            paired(DOWN, i - 1)
    r.flip[:, 0:TOK] = r.second[...].T
    r.wide[...] = jnp.zeros((TOK, D), F32)
    for i in range(4):
        x = (own_x + 1 + i) % 4
        columns = pl.ds(pl.multiple_of(x * 512, 512), 512)
        d_gate, d_up = (r.d_gate[:, columns], r.d_up[:, columns])
        r.wide[...] += nt(d_gate, w[GATE][x]) + nt(d_up, w[UP][x])
        w[GATE][x] = nn(r.flip[:, 0:TOK], d_gate).astype(BF)
        sums[GATE].start(x)
        w[UP][x] = nn(r.flip[:, 0:TOK], d_up).astype(BF)
        sums[UP].start(x)
        if i:
            paired(GATE, i - 1)
            paired(UP, i - 1)
        else:
            paired(DOWN, 3)

    def to_hidden(rows, i, kept):
        d_pre, d_att = kept
        back, d_gain = rms_back(r.hidden[rows, :], gain[G_PRE], r.wide[rows, :])
        back = back + r.cot[rows, :].astype(F32)
        r.wide[rows, :] = back
        back, d_gain_att = rms_back(r.proj[rows, :], gain[G_ATT], back)
        r.low[rows, :] = back.astype(BF)
        return d_pre + d_gain, d_att + d_gain_att

    d_pre, d_att = chunks(3, to_hidden, (none, none))
    put_gain(G_PRE, d_pre)
    put_gain(G_ATT, d_att)
    paired(GATE, 3)
    paired(UP, 3)
    for i in range(4):
        h = (own_x + 1 + i) % 4
        columns = pl.ds(pl.multiple_of(h * HD, HD), HD)
        rows = pl.ds(pl.multiple_of(h * 128, 128), 128)
        d_head = nt(r.low[...], w[OUT][h])
        for b in range(3):
            r.d_att[b, rows, :] = (
                d_head[b * 128 : (b + 1) * 128, :] * r.inverse[b, rows, :]
            ).astype(BF)
        w[OUT][h] = nn(r.att[:, columns].T, r.low[...]).astype(BF)
        sums[OUT].start(h)
        if i:
            paired(OUT, i - 1)
    r.dkv[...] = jnp.zeros((BEHIND + TOK, 2 * HD), F32)

    def attend_back(b, d_q):
        window = pl.ds(b * 128, KEYS)
        at = pl.ds(b * 128, 128)
        r.scores[...] = nt(r.d_att[b], r.v_ext[window, :])
        for h in range(H):
            rows = pl.ds(h * 128, 128)
            both = r.d_att[b, rows, :].astype(F32) * r.att[at, h * HD : (h + 1) * HD].astype(F32)
            delta = jnp.sum(both, axis=1, keepdims=True)
            r.d_scores[rows, :] = (
                r.exps[b, rows, :].astype(F32) * (r.scores[rows, :] - delta)
            ).astype(BF)
        r.dkv[window, 0:HD] += nn(r.d_scores[...].T, r.q_rot[b])
        r.dkv[window, HD:] += nn(r.exps[b].T, r.d_att[b])
        d_query = nn(r.d_scores[...], r.k_ext[window, :]) * HD**-0.5
        for h in range(H):
            back = turn_back(d_query[h * 128 : (h + 1) * 128, :], *own_turn(b))
            value = r.mixed[at, h * HD : (h + 1) * HD].astype(F32)
            back, d_gain = rms_back(value, gain[G_Q], back)
            r.d_mixed[at, h * HD : (h + 1) * HD] = back.astype(BF)
            d_q = d_q + d_gain
        return d_q

    d_q = attend_back(0, jnp.zeros((1, HD), F32))
    paired(OUT, 3)
    reduce(Reduce.after_first, DOWN)
    d_q = attend_back(1, d_q)
    r.flip[...] = r.normed[...].T
    d_q = attend_back(2, d_q)
    put_gain(G_Q, d_q)

    def keys_back(rows, i, d_k):
        both = r.dkv[rows, :]
        back = turn_back(both[:, :HD], r.cos[rows, :], r.sin[rows, :])
        back, d_gain = rms_back(r.k_raw[rows, :].astype(F32), gain[G_K], back)
        r.d_kv[rows, 0:HD] = back.astype(BF)
        r.d_kv[rows, HD:] = both[:, HD:].astype(BF)
        return d_k + d_gain

    put_gain(G_K, chunks(7, keys_back, jnp.zeros((1, HD), F32)))
    back_two = net.send(r.d_kv.at[pl.ds(0, 128)], r.halo_two, "seq", -2)
    back_one = net.send(r.d_kv.at[pl.ds(128, TOK)], r.halo_one, "seq", -1)
    flip_own = r.flip[:, BEHIND:]
    for x in range(4):
        if x < 2:
            r.g_qkv[x] = nn(flip_own, r.d_mixed[:, x * 384 : (x + 1) * 384]).astype(BF)
        elif x == 2:
            r.g_qkv[x, :, 0:256] = nn(flip_own, r.d_mixed[:, 768:1024]).astype(BF)
            r.g_qkv[x, :, 256:384] = nn(r.flip[...], r.d_kv[:, 0:128]).astype(BF)
        else:
            r.g_qkv[x] = nn(r.flip[...], r.d_kv[:, 128:512]).astype(BF)
        sums[QKV].start(x)
        if x:
            sums[QKV].pair(x - 1)
    sums[QKV].pair(3)
    for j in PEERS:
        sums[QKV].along_x(j)
    reduce(Reduce.after_first, GATE, UP, OUT)
    reduce(Reduce.after_second, DOWN)
    back_two.arrived()
    back_one.arrived()
    r.d_mixed[:, 1024:1536] = r.d_kv[BEHIND:, :] + r.halo_one[...]
    last = pl.ds(256, 128)
    r.d_mixed[last, 1024:1536] = r.d_mixed[last, 1024:1536] + r.halo_two[...]
    r.proj[...] = (
        nt(r.d_mixed[:, 0:384], w[QKV][0])
        + nt(r.d_mixed[:, 384:768], w[QKV][1])
        + nt(r.d_mixed[:, 768:1152], w[QKV][2])
        + nt(r.d_mixed[:, 1152:1536], w[QKV][3])
    )

    def to_input(rows, i, kept):
        value = r.x_ext[pl.ds(pl.multiple_of(BEHIND + i * 128, 128), 128), :].astype(F32)
        back, d_gain = rms_back(value, gain[G_IN], r.proj[rows, :])
        r.wide[rows, :] += back
        return kept + d_gain

    put_gain(G_IN, chunks(3, to_input, none))
    store_grad = local(r.wide, r.input_grad)
    gains = ReduceGains(net, r.gain_got)
    gains.start(r.gain_grad[...])

    reduce(Reduce.after_first, QKV)
    reduce(Reduce.after_second, GATE, UP, OUT)
    reduce(Reduce.after_third, DOWN)
    gains.step(0)
    reduce(Reduce.after_second, QKV)
    reduce(Reduce.after_third, GATE, UP, OUT)
    reduce(Reduce.share, DOWN)
    gains.step(1)
    reduce(Reduce.after_third, QKV)
    reduce(Reduce.share, GATE, UP, OUT)
    gains.step(2)
    reduce(Reduce.share, QKV)
    r.s_gains[...] = gains.step(3)
    stores = []
    for name in (DOWN, GATE, UP, OUT, QKV):
        reduce(Reduce.finish, name)
        stores.append(local(r.totals[name], r.sums[name]))
    net.drain()
    for copy in stores + [store_out, store_grad]:
        copy.wait()


def run_block(tokens, cotangent, segment, masters, gains):
    vmem, anywhere = (pl.BlockSpec(memory_space=pltpu.VMEM), pl.BlockSpec(memory_space=pl.ANY))
    freqs = (ROPE_BASE ** (-np.arange(128) * 2.0 / HD)).astype(np.float32).reshape(1, 128)
    block_output, input_grad, gain_sums, *sums = pl.pallas_call(
        block_kernel,
        out_shape=[
            jax.ShapeDtypeStruct((TOK, D), BF),
            jax.ShapeDtypeStruct((TOK, D), F32),
            jax.ShapeDtypeStruct((4, 8, 128), F32),
        ]
        + [jax.ShapeDtypeStruct(shape, BF) for shape in SHARD],
        in_specs=[anywhere, anywhere, vmem, vmem, vmem] + [anywhere] * 5,
        out_specs=[anywhere, anywhere, vmem] + [anywhere] * 5,
        scratch_shapes=[pltpu.VMEM((4,) + shape, BF) for shape in SHARD]
        + [pltpu.VMEM(shape, BF) for shape in SHARD]
        + [pltpu.VMEM(shape, F32) for shape in SHARD]
        + [pltpu.VMEM(shape, kind) for _, shape, kind in SCRATCH]
        + reduce_scratch()
        + [
            pltpu.SemaphoreType.DMA((COPIES,)),
            pltpu.SemaphoreType.DMA((COPIES,)),
            pltpu.SemaphoreType.DMA((LOADS,)),
        ],
        compiler_params=pltpu.CompilerParams(
            collective_id=0, has_side_effects=True, vmem_limit_bytes=VMEM_BYTES
        ),
        name="block",
    )(
        tokens,
        cotangent,
        segment.reshape(3, 128),
        gains.reshape(6, 128),
        jnp.asarray(freqs),
        *masters,
    )
    return block_output, input_grad, sums, gain_sums


def adamw(weight, gradient, first, second, rate, decay):
    first_new = ADAM_ONE * first + (1.0 - ADAM_ONE) * gradient
    second_new = ADAM_TWO * second + (1.0 - ADAM_TWO) * gradient * gradient
    first_hat = first_new * (1.0 / (1.0 - ADAM_ONE**STEP))
    second_hat = second_new * (1.0 / (1.0 - ADAM_TWO**STEP))
    weight_new = weight - rate * (first_hat / (jnp.sqrt(second_hat) + ADAM_EPS) + decay * weight)
    return (weight_new, first_new, second_new)


CHUNKS = 4


def update_kernel(*refs):
    taken = iter(refs)
    take = lambda count: [next(taken) for _ in range(count)]
    states, gradients = ([take(3) for _ in SHARD], take(5))
    gain_states, gain_sums = (take(3), next(taken))
    fresh, gain_fresh = ([take(3) for _ in SHARD], take(3))
    held, low = (take(5), take(5))
    in_sems, low_sems, out_sems = take(3)

    def part(k, chunk):
        count = SHARD[k][0] // CHUNKS
        return pl.ds(chunk * count, count)

    for k in range(5):
        pltpu.make_async_copy(gradients[k], low[k], low_sems.at[k]).start()
        for chunk in range(CHUNKS):
            rows = part(k, chunk)
            for p in range(3):
                pltpu.make_async_copy(
                    states[k][p].at[rows], held[k].at[p, rows], in_sems.at[k, chunk]
                ).start()
    own = gain_sums[lax.axis_index("wsh"), 0:6]
    for ref, value in zip(
        gain_fresh, adamw(gain_states[0][...], own, gain_states[1][...], gain_states[2][...], GAIN_RATE, 0.0)
    ):
        ref[...] = value
    for k in range(5):
        pltpu.make_async_copy(low[k], low[k], low_sems.at[k]).wait()
        for chunk in range(CHUNKS):
            rows = part(k, chunk)
            whole = held[k].at[:, rows]
            pltpu.make_async_copy(whole, whole, in_sems.at[k, chunk]).wait()
            gradient = low[k][rows, :].astype(F32)
            state = [held[k][p, rows, :] for p in range(3)]
            values = adamw(state[0], gradient, state[1], state[2], MATRIX_RATE, MATRIX_DECAY)
            for p, value in enumerate(values):
                held[k][p, rows, :] = value
            for p in range(3):
                pltpu.make_async_copy(
                    held[k].at[p, rows], fresh[k][p].at[rows], out_sems.at[k]
                ).start()
    for k in range(5):
        pltpu.make_async_copy(held[k], held[k], out_sems.at[k]).wait()


def update(states, gradients, gain_states, gain_sums):
    vmem, anywhere = (pl.BlockSpec(memory_space=pltpu.VMEM), pl.BlockSpec(memory_space=pl.ANY))
    got = pl.pallas_call(
        update_kernel,
        out_shape=[jax.ShapeDtypeStruct(shape, F32) for shape in SHARD for _ in range(3)]
        + [jax.ShapeDtypeStruct((6, 128), F32)] * 3,
        in_specs=[anywhere] * 20 + [vmem] * 4,
        out_specs=[anywhere] * 15 + [vmem] * 3,
        scratch_shapes=[pltpu.VMEM((3,) + shape, F32) for shape in SHARD]
        + [pltpu.VMEM(shape, BF) for shape in SHARD]
        + [
            pltpu.SemaphoreType.DMA((5, CHUNKS)),
            pltpu.SemaphoreType.DMA((5,)),
            pltpu.SemaphoreType.DMA((5,)),
        ],
        compiler_params=pltpu.CompilerParams(vmem_limit_bytes=VMEM_BYTES),
        name="update",
    )(*[a for state in states for a in state], *gradients, *gain_states, gain_sums)
    return list(got[:15]) + [a.reshape(768) for a in got[15:]]


def on_device(
    tokens,
    cotangent,
    segment,
    qkv_weight,
    out_weight,
    gate_weight,
    up_weight,
    down_weight,
    gains,
    qkv_first,
    qkv_second,
    out_first,
    out_second,
    gate_first,
    gate_second,
    up_first,
    up_second,
    down_first,
    down_second,
    gain_first,
    gain_second,
):
    masters = (qkv_weight, out_weight, gate_weight, up_weight, down_weight)
    block_output, input_grad, sums, gain_sums = run_block(
        tokens, cotangent, segment, masters, gains
    )
    states = (
        (qkv_weight, qkv_first, qkv_second),
        (out_weight, out_first, out_second),
        (gate_weight, gate_first, gate_second),
        (up_weight, up_first, up_second),
        (down_weight, down_first, down_second),
    )
    gain_states = [a.reshape(6, 128) for a in (gains, gain_first, gain_second)]
    fresh = update(states, sums, gain_states, gain_sums)
    return (block_output, input_grad) + tuple(fresh)


def solution(mesh):
    placed = (
        P(("wsh", "seq"), None),
        P(("wsh", "seq"), None),
        P(("wsh", "seq")),
        P(None, "wsh"),
        P("wsh", None),
        P(None, "wsh"),
        P(None, "wsh"),
        P("wsh", None),
        P("wsh"),
        P(None, "wsh"),
        P(None, "wsh"),
        P("wsh", None),
        P("wsh", None),
        P(None, "wsh"),
        P(None, "wsh"),
        P(None, "wsh"),
        P(None, "wsh"),
        P("wsh", None),
        P("wsh", None),
        P("wsh"),
        P("wsh"),
    )
    return jax.shard_map(
        on_device,
        mesh=mesh,
        in_specs=placed,
        out_specs=(
            P(("wsh", "seq"), None),
            P(("wsh", "seq"), None),
            P(None, "wsh"),
            P(None, "wsh"),
            P(None, "wsh"),
            P("wsh", None),
            P("wsh", None),
            P("wsh", None),
            P(None, "wsh"),
            P(None, "wsh"),
            P(None, "wsh"),
            P(None, "wsh"),
            P(None, "wsh"),
            P(None, "wsh"),
            P("wsh", None),
            P("wsh", None),
            P("wsh", None),
            P("wsh"),
            P("wsh"),
            P("wsh"),
        ),
        check_vma=False,
    )
```

```python
import types

import jax
import jax.numpy as jnp
import numpy as np
from jax import lax
from jax.experimental import pallas as pl
from jax.experimental.pallas import tpu as pltpu
from jax.sharding import PartitionSpec as P

D = 640
H = 4
HD = 256
WIN = 512
STEP = 10


EPS = 1e-06
ADAM_ONE = 0.9
ADAM_TWO = 0.999
ADAM_EPS = 1e-08
MATRIX_DECAY = 0.1
MATRIX_RATE = 0.05
GAIN_RATE = 0.8
ROPE_BASE = 10000.0


BLOCK_BYTES, UPDATE_BYTES = (53 * 2**20, 24 * 2**20)
BF, F32 = (jnp.bfloat16, jnp.float32)
MESH = pl.DeviceIdType.MESH
AXES = 4
QKV, OUT, GATE, UP, DOWN = range(5)
SHARD = ((640, 384), (256, 640), (640, 512), (640, 512), (512, 640))
GATHERED = (
    ((0, 128, "y"), (128, 256, "z")),
    ((0, 640, ""),),
    ((0, 512, "y"),),
    ((0, 512, "z"),),
    ((0, 384, "y"), (384, 256, "z")),
)
REDUCED = (
    ((0, 128, "y", "y"), (128, 128, "z", "z"), (256, 128, "y", "x")),
    ((0, 128, "y", "y"), (128, 256, "z", "z"), (384, 256, "y", "x")),
    ((0, 256, "y", "y"), (256, 128, "z", "z"), (384, 128, "z", "x")),
    ((0, 128, "y", "y"), (128, 256, "z", "z"), (384, 128, "y", "x")),
    ((0, 256, "y", "y"), (256, 128, "z", "z"), (384, 256, "z", "x")),
)
OTHER = {"y": "z", "z": "y"}
PEERS = (1, 2, 3)


class Net:
    def __init__(self, send_sems, recv_sems):
        token = lax.axis_index("seq")
        self.at = {"x": lax.axis_index("wsh"), "y": (token // 2) % 4, "z": token // 8, "c": token % 2}
        self.send_sems, self.recv_sems, self.count, self.started = (send_sems, recv_sems, 0, [])

    def peer(self, axis, by):
        size = 2 if axis == "c" else AXES
        return (self.at[axis] + by) % size

    def device(self, axis, by):
        if axis == "seq":
            return ((lax.axis_index("seq") + by) % 32, self.at["x"])
        at = dict(self.at)
        at[axis] = self.peer(axis, by)
        return ((at["z"] * 4 + at["y"]) * 2 + at["c"], at["x"])

    def greet(self):
        barrier = pltpu.get_barrier_semaphore()
        peers = [(axis, by) for axis in "xyz" for by in PEERS] + [("c", 1)]
        peers += [("seq", by) for by in (1, 2, -1, -2)]
        for axis, by in peers:
            pl.semaphore_signal(
                barrier, inc=1, device_id=self.device(axis, by), device_id_type=MESH
            )
        pl.semaphore_wait(barrier, len(peers))

    def batch(self, size):
        made = Batch(self, size, self.send_sems.at[self.count], self.recv_sems.at[self.count])
        self.count += 1
        self.started.append(made)
        return made

    def send(self, src, dst, axis, by):
        return self.batch(src).add(src, dst, axis, by)

    def drain(self):
        for made in self.started:
            pltpu.make_async_copy(made.size, made.size, made.send_sem).wait()
        self.started = []


class Batch:
    def __init__(self, net, size, send_sem, recv_sem):
        self.net, self.size, self.send_sem, self.recv_sem = (net, size, send_sem, recv_sem)

    def add(self, src, dst, axis, by):
        pltpu.make_async_remote_copy(
            src_ref=src,
            dst_ref=dst,
            send_sem=self.send_sem,
            recv_sem=self.recv_sem,
            device_id=self.net.device(axis, by),
            device_id_type=MESH,
        ).start()
        return self

    def arrived(self):
        pltpu.make_async_copy(self.size, self.size, self.recv_sem).wait()


class Gather:
    def __init__(self, net, weight, full):
        self.net, self.full, (self.rows, _), self.parts = (
            net,
            full,
            SHARD[weight],
            GATHERED[weight],
        )
        self.eighth, self.direct = (self.rows // 8, not self.parts[0][2])

    def block(self, x, part):
        first, width, axis = part
        at, count = (net_half(self.net, self.rows), self.rows // 2)
        if axis:
            at, count = (at + self.net.at[axis] * self.eighth, self.eighth)
        return self.full.at[x, pl.ds(pl.multiple_of(at, 16), count), pl.ds(first, width)]

    def start(self):
        each = self.rows // 2 if self.direct else self.eighth
        self.along_x = self.net.batch(self.full.at[0:3, pl.ds(0, each), :])
        for part in self.parts:
            mine = self.block(self.net.at["x"], part)
            for j in PEERS:
                self.along_x.add(mine, mine, "x", j)

    def spread(self):
        self.along_x.arrived()
        self.along_q = self.net.batch(self.full.at[0:3, pl.ds(0, 3 * self.eighth), :])
        for j in PEERS:
            for part in self.parts:
                got = self.block(self.net.peer("x", -j), part)
                for k in PEERS:
                    self.along_q.add(got, got, part[2], k)

    def share(self):
        (self.along_x if self.direct else self.along_q).arrived()
        half = self.rows // 2
        self.to_core = self.net.batch(self.full.at[0:3, pl.ds(0, half), :])
        for j in PEERS:
            got = self.full.at[self.net.peer("x", -j), pl.ds(net_half(self.net, self.rows), half), :]
            self.to_core.add(got, got, "c", 1)

    def finish(self):
        self.to_core.arrived()


def net_half(net, rows):
    return pl.multiple_of(net.at["c"] * (rows // 2), 16)


class Reduce:
    def __init__(self, net, weight, grad, core_got, got, total):
        self.net, self.grad, self.core_got, self.total = (net, grad, core_got, total)
        self.rows, self.columns = SHARD[weight]
        self.parts = [
            (pl.ds(first, width), axis, order, got[3 * k : 3 * k + 3])
            for k, (first, width, axis, order) in enumerate(REDUCED[weight])
        ]
        self.half, self.eighth = (self.rows // 2, self.rows // 8)
        self.half_start = net_half(net, self.rows)
        self.core, self.firsts = ([], None)

    def block(self, q):
        return pl.ds(pl.multiple_of(self.half_start + q * self.eighth, 16), self.eighth)

    def start(self, x):
        there = pl.multiple_of((1 - self.net.at["c"]) * self.half, 16)
        mine = self.grad.at[x, pl.ds(there, self.half), :]
        self.core.append(self.net.batch(mine).add(mine, self.core_got.at[x], "c", 1))

    def pair(self, x):
        self.core.pop(0).arrived()

        def add(block, carry):
            local = pl.ds(pl.multiple_of(block * self.eighth, 16), self.eighth)
            rows = self.block(block)
            self.grad[x, rows, :] = self.grad[x, rows, :] + self.core_got[x, local, :]
            return carry

        lax.fori_loop(0, 4, add, 0)
        if self.firsts is None:
            self.firsts = self.net.batch(self.grad.at[0:3, pl.ds(0, self.half), :])
        for columns, axis, order, got in self.parts:
            if order != "x":
                for j in PEERS:
                    src = self.grad.at[x, self.block(self.net.peer(axis, j)), columns]
                    self.firsts.add(src, got[0].at[j - 1, x], order, j)

    def along_x(self, j):
        for columns, axis, order, got in self.parts:
            if order == "x":
                rows = pl.ds(self.half_start, self.half)
                src = self.grad.at[self.net.peer("x", j), rows, columns]
                self.firsts.add(src, got[0].at[j - 1], order, j)

    def after_first(self):
        self.firsts.arrived()
        self.seconds = self.net.batch(self.grad.at[0, pl.ds(0, 3 * self.eighth), :])
        for columns, axis, order, got in self.parts:
            own = self.net.at[axis]

            def add(step, carry):
                if order == "x":
                    x, rows = (self.net.at["x"], self.block(step))
                    local = pl.ds(pl.multiple_of(step * self.eighth, 16), self.eighth)
                    pieces = [got[0][j, local, :] for j in range(3)]
                else:
                    x, rows = (step, self.block(own))
                    pieces = [got[0][j, step] for j in range(3)]
                total = self.grad[x, rows, columns].astype(F32)
                for piece in pieces:
                    total = total + piece.astype(F32)
                self.grad[x, rows, columns] = total.astype(BF)
                return carry

            lax.fori_loop(0, 4, add, 0)
            for j in PEERS:
                if order == "x":
                    x, q, along = (self.net.at["x"], self.net.peer(axis, j), axis)
                else:
                    x, q, along = (self.net.peer("x", j), own, "x")
                src = self.grad.at[x, self.block(q), columns]
                self.seconds.add(src, got[1].at[j - 1], along, j)

    def after_second(self):
        self.seconds.arrived()
        self.thirds = self.net.batch(self.grad.at[0, pl.ds(0, 3 * self.eighth), :])
        for columns, axis, order, got in self.parts:
            rows = self.block(self.net.at[axis])
            total = self.grad[self.net.at["x"], rows, columns].astype(F32)
            for j in range(3):
                total = total + got[1][j].astype(F32)
            mine = got[2].at[self.net.at[OTHER[axis]]]
            mine[...] = total.astype(BF)
            for j in PEERS:
                self.thirds.add(mine, mine, OTHER[axis], j)

    def after_third(self):
        self.thirds.arrived()
        self.fourths = self.net.batch(self.grad.at[0, pl.ds(0, 3 * self.eighth), :])
        for columns, axis, order, got in self.parts:
            total = got[2][0].astype(F32)
            for j in PEERS:
                total = total + got[2][j].astype(F32)
            mine = self.total.at[self.block(self.net.at[axis]), columns]
            mine[...] = total.astype(BF)
            for j in PEERS:
                self.fourths.add(mine, mine, axis, j)

    def share(self):
        self.fourths.arrived()
        mine = self.total.at[pl.ds(self.half_start, self.half), :]
        self.fifth = self.net.batch(mine).add(mine, mine, "c", 1)

    def finish(self):
        self.fifth.arrived()


class ReduceGains:
    def __init__(self, net, got):
        self.net, self.got = (net, got)

    def start(self, value):
        self.post(0, value)

    def post(self, stage, value):
        axis, peers = ("cxyz"[stage], PEERS if stage else (1,))
        mine = self.got.at[stage, self.net.at[axis]]
        mine[...] = value
        self.copies = self.net.batch(self.got.at[0, 0 : len(peers)])
        for j in peers:
            self.copies.add(mine, mine, axis, j)

    def step(self, stage):
        self.copies.arrived()
        total = self.got[stage, 0] + self.got[stage, 1]
        if stage:
            total = total + self.got[stage, 2] + self.got[stage, 3]
        if stage < 3:
            self.post(stage + 1, total)
        return total


def reduce_scratch():
    shapes = []
    for (rows, columns), parts in zip(SHARD, REDUCED):
        shapes.append((4, rows // 2, columns))
        for _, width, _, order in parts:
            shapes += [
                (3, rows // 2, width) if order == "x" else (3, 4, rows // 8, width),
                (3, rows // 8, width),
                (4, rows // 8, width),
            ]
    return [pltpu.VMEM(shape, BF) for shape in shapes]


TOK = 384
BEHIND = 512
KEYS = 640
G_IN, G_ATT, G_PRE, G_POST, G_Q, G_K = range(6)
NORM_ROWS = ((0, 5), (5, 5), (10, 5), (15, 5), (20, 2), (22, 2))

SCRATCH = (
    ("g_qkv", (4,) + SHARD[QKV], BF),
    ("x_ext", (BEHIND + TOK, D), BF),
    ("normed", (BEHIND + TOK, D), BF),
    ("cos", (BEHIND + TOK, 128), F32),
    ("sin", (BEHIND + TOK, 128), F32),
    ("mixed", (TOK, 1024), BF),
    ("k_raw", (BEHIND + TOK, HD), BF),
    ("q_rot", (3, 512, HD), BF),
    ("k_ext", (BEHIND + TOK, HD), BF),
    ("v_ext", (BEHIND + TOK, HD), BF),
    ("exps", (3, 512, KEYS), BF),
    ("scores", (512, KEYS), F32),
    ("bias", (128, KEYS), F32),
    ("inverse", (3, 512, 1), F32),
    ("att", (TOK, H * HD), BF),
    ("proj", (TOK, D), F32),
    ("hidden", (TOK, D), F32),
    ("second", (TOK, D), BF),
    ("flip", (D, BEHIND + TOK), BF),
    ("activ", (TOK, 2048), BF),
    ("d_gate", (TOK, 2048), BF),
    ("d_up", (TOK, 2048), BF),
    ("low", (TOK, D), BF),
    ("cot", (TOK, D), BF),
    ("d_att", (3, 512, HD), BF),
    ("d_scores", (512, KEYS), BF),
    ("dkv", (BEHIND + TOK, 2 * HD), F32),
    ("d_kv", (BEHIND + TOK, 2 * HD), BF),
    ("halo_one", (TOK, 2 * HD), BF),
    ("halo_two", (128, 2 * HD), BF),
    ("d_mixed", (TOK, 1536), BF),
    ("gain_all", (4, 8, 128), F32),
    ("gain_grad", (4, 8, 128), F32),
    ("gain_got", (4, 4, 4, 8, 128), F32),
    ("ids", (8, 128), jnp.int32),
    ("ids_one", (8, 128), jnp.int32),
    ("ids_two", (8, 128), jnp.int32),
)
COPIES = 5 * 3 - 1 + 5 * 9 + 6 + 5
LOADS = 14


def nt(a, b):
    return lax.dot_general(a, b, (((1,), (1,)), ((), ())), preferred_element_type=F32)


def nn(a, b):
    return jnp.dot(a, b, preferred_element_type=F32)


def inverse_rms(value):
    return lax.rsqrt(jnp.mean(value * value, axis=-1, keepdims=True) + EPS)


def rms_back(value, gain, grad):
    scale = inverse_rms(value)
    unit = value * scale
    weighted = grad * gain
    back = scale * (weighted - unit * jnp.mean(weighted * unit, axis=-1, keepdims=True))
    return back, jnp.sum(grad * unit, axis=0, keepdims=True)


def turn(value, cosine, sine):
    first, last = (value[:, :128], value[:, 128:])
    return jnp.concatenate([first * cosine - last * sine, last * cosine + first * sine], axis=1)


def turn_back(grad, cosine, sine):
    first, last = (grad[:, :128], grad[:, 128:])
    return jnp.concatenate([first * cosine + last * sine, last * cosine - first * sine], axis=1)


def block_kernel(*refs):
    taken = iter(refs)
    r, take = (types.SimpleNamespace(), lambda count: [next(taken) for _ in range(count)])
    r.tokens, r.cotangent, r.segment, r.gains, r.freqs = take(5)
    r.masters = take(5)
    r.out_low, r.wide, r.s_gains = take(3)
    r.totals, r.fulls, w = (take(5), take(5), take(5))
    for name, _, _ in SCRATCH:
        setattr(r, name, next(taken))
    pieces = [take(1 + 3 * len(parts)) for parts in REDUCED]
    send_sems, recv_sems, load_sems = take(3)
    net = Net(send_sems, recv_sems)
    own_x = net.at["x"]
    base = lax.axis_index("seq") * TOK
    loads = []

    def local(src, dst):
        copy = pltpu.make_async_copy(src, dst, load_sems.at[len(loads)])
        loads.append(copy)
        copy.start()
        return copy

    def chunks(count, body, carry=0):
        return lax.fori_loop(
            0, count, lambda i, kept: body(pl.ds(pl.multiple_of(i * 128, 128), 128), i, kept), carry
        )

    own_rows = pl.ds(BEHIND, TOK)
    fill = {QKV: local(r.masters[QKV], r.fulls[QKV])}
    fill_tokens = local(r.tokens, r.x_ext.at[own_rows])
    for name in (OUT, GATE, UP, DOWN):
        fill[name] = local(r.masters[name], r.fulls[name])
    fill_cot = local(r.cotangent, r.cot)
    r.gain_all[...] = jnp.zeros((4, 8, 128), F32)
    r.gain_grad[...] = jnp.zeros((4, 8, 128), F32)
    r.gain_all[own_x, 0:6] = r.gains[...].astype(BF).astype(F32)
    r.ids[...] = jnp.zeros((8, 128), jnp.int32)
    r.ids[0:3] = r.segment[...]
    net.greet()

    mine = r.gain_all.at[own_x]
    gain_copies = net.batch(r.gain_all.at[0:3])
    for j in PEERS:
        gain_copies.add(mine, mine, "x", j)
    parts = [Gather(net, name, w[name]) for name in range(5)]

    def launch(name):
        fill[name].wait()
        rows = SHARD[name][0] // 8

        def cast(step, carry):
            at = pl.ds(pl.multiple_of(step * rows, 16), rows)
            w[name][own_x, at, :] = r.fulls[name][at, :].astype(BF)
            return carry

        lax.fori_loop(0, 8, cast, 0)
        parts[name].start()

    def arrive(step, *which):
        for name in which:
            step(parts[name])

    launch(QKV)
    fill_tokens.wait()
    halo_copies = [
        net.send(r.x_ext.at[own_rows], r.x_ext.at[pl.ds(128, TOK)], "seq", 1),
        net.send(r.x_ext.at[pl.ds(BEHIND + 256, 128)], r.x_ext.at[pl.ds(0, 128)], "seq", 2),
        net.send(r.ids, r.ids_one, "seq", 1),
        net.send(r.ids, r.ids_two, "seq", 2),
    ]

    def angles(rows, i, kept):
        place = (base - BEHIND + i * 128 + lax.broadcasted_iota(jnp.int32, (128, 128), 0)).astype(F32)
        angle = place * r.freqs[...]
        r.cos[rows, :] = jnp.cos(angle)
        r.sin[rows, :] = jnp.sin(angle)
        return kept

    chunks(7, angles)
    launch(GATE)
    launch(UP)
    arrive(Gather.spread, QKV, GATE, UP)
    launch(DOWN)
    launch(OUT)
    gain_copies.arrived()
    gain = {}
    for name, (first, count) in enumerate(NORM_ROWS):
        rows = [(k // 6, k % 6) for k in range(first, first + count)]
        gain[name] = jnp.concatenate([r.gain_all[g, k : k + 1, :] for g, k in rows], axis=1)

    def put_gain(name, value):
        first, count = NORM_ROWS[name]
        for k in range(count):
            g, row = ((first + k) // 6, (first + k) % 6)
            r.gain_grad[g, row : row + 1, :] = value[:, 128 * k : 128 * (k + 1)]

    for copy in halo_copies:
        copy.arrived()

    def normalise(rows, i, kept):
        value = r.x_ext[rows, :].astype(F32)
        r.normed[rows, :] = (value * inverse_rms(value) * gain[G_IN]).astype(BF)
        return kept

    chunks(7, normalise)
    arrive(Gather.share, QKV)
    arrive(Gather.finish, QKV)

    normed_own = r.normed[own_rows, :]
    for x in range(4):
        width = 384 if x < 2 else (256 if x == 2 else 0)
        if width:
            r.mixed[:, x * 384 : x * 384 + width] = nn(
                normed_own, w[QKV][x, :, :width]
            ).astype(BF)
    normed_all = r.normed[...]
    r.dkv[:, 0:128] = nn(normed_all, w[QKV][2, :, 256:384])
    tail = nn(normed_all, w[QKV][3])
    r.dkv[:, 128:256] = tail[:, :128]
    r.v_ext[...] = tail[:, 128:].astype(BF)
    r.k_raw[...] = r.dkv[:, 0:256].astype(BF)
    arrive(Gather.spread, DOWN)

    def keys(rows, i, kept):
        value = r.dkv[rows, 0:256]
        value = value * inverse_rms(value) * gain[G_K]
        r.k_ext[rows, :] = turn(value, r.cos[rows, :], r.sin[rows, :]).astype(BF)
        return kept

    chunks(7, keys)

    def own_turn(i):
        at = pl.ds(pl.multiple_of(BEHIND + i * 128, 128), 128)
        return r.cos[at, :], r.sin[at, :]

    def queries(rows, i, kept):
        for h in range(H):
            value = r.mixed[rows, h * HD : (h + 1) * HD].astype(F32)
            value = value * inverse_rms(value) * gain[G_Q]
            r.q_rot[i, h * 128 : (h + 1) * 128, :] = (
                turn(value, *own_turn(i)) * HD**-0.5
            ).astype(BF)
        return kept

    chunks(3, queries)
    arrive(Gather.share, OUT)

    id_rows = [r.ids_two[2:3, :]] + [r.ids_one[k : k + 1, :] for k in range(3)]
    id_rows = [row.astype(F32) for row in id_rows + [r.ids[k : k + 1, :] for k in range(3)]]

    def attend(b):
        down_rows = lax.broadcasted_iota(jnp.int32, (128, 128), 0)
        across = lax.broadcasted_iota(jnp.int32, (128, 128), 1)
        own_id = jnp.broadcast_to(id_rows[4 + b], (128, 128)).T
        for j in range(5):
            allowed = jnp.broadcast_to(id_rows[b + j], (128, 128)) == own_id
            allowed = allowed & (base - BEHIND + (b + j) * 128 + across >= 0)
            if j == 0:
                allowed = allowed & (across > down_rows)
            if j == 4:
                allowed = allowed & (across <= down_rows)
            r.bias[:, j * 128 : (j + 1) * 128] = jnp.where(allowed, 0.0, -1e30)
        window = pl.ds(b * 128, KEYS)
        r.scores[...] = nt(r.q_rot[b], r.k_ext[window, :])
        for h in range(H):
            rows = pl.ds(h * 128, 128)
            weight = jnp.exp(r.scores[rows, :] + r.bias[...])
            r.inverse[b, rows, :] = 1.0 / jnp.sum(weight, axis=1, keepdims=True)
            r.exps[b, rows, :] = weight.astype(BF)
        mean = nn(r.exps[b], r.v_ext[window, :]) * r.inverse[b]
        for h in range(H):
            r.att[pl.ds(b * 128, 128), h * HD : (h + 1) * HD] = mean[
                h * 128 : (h + 1) * 128, :
            ].astype(BF)

    attend(0)
    attend(1)
    attend(2)
    arrive(Gather.share, GATE, UP)
    arrive(Gather.finish, OUT)
    r.proj[...] = nn(r.att[...], w[OUT][...].reshape(H * HD, D))

    def residual(rows, i, kept):
        value = r.proj[rows, :]
        hidden = r.x_ext[pl.ds(pl.multiple_of(BEHIND + i * 128, 128), 128), :].astype(F32)
        hidden = hidden + value * inverse_rms(value) * gain[G_ATT]
        r.hidden[rows, :] = hidden
        r.second[rows, :] = (hidden * inverse_rms(hidden) * gain[G_PRE]).astype(BF)
        return kept

    chunks(3, residual)

    def widen(step, kept):
        x, part = ((own_x + step // 2) % 4, step % 2)
        inner = pl.ds(pl.multiple_of(part * 256, 256), 256)
        columns = pl.ds(pl.multiple_of(x * 512 + part * 256, 256), 256)
        gate = nn(r.second[...], w[GATE][x, :, inner])
        up = nn(r.second[...], w[UP][x, :, inner])
        square = gate * gate
        bend = jnp.tanh(gate * (0.7978845608028654 + 0.7978845608028654 * 0.044715 * square))
        half = 0.5 + 0.5 * bend
        gelu = gate * half
        slope = half + (0.5 * gate) * (1.0 - bend * bend) * (
            0.7978845608028654 + 3.0 * 0.7978845608028654 * 0.044715 * square
        )
        r.activ[:, columns] = (gelu * up).astype(BF)
        r.d_gate[:, columns] = (slope * up).astype(BF)
        r.d_up[:, columns] = gelu.astype(BF)
        return kept

    lax.fori_loop(0, 2, widen, 0)
    arrive(Gather.finish, GATE, UP)
    arrive(Gather.share, DOWN)
    lax.fori_loop(2, 8, widen, 0)
    arrive(Gather.finish, DOWN)
    r.wide[...] = nn(r.activ[...], w[DOWN][...].reshape(2048, D))
    fill_cot.wait()

    def finish_forward(rows, i, kept):
        value = r.wide[rows, :]
        ended = r.hidden[rows, :] + value * inverse_rms(value) * gain[G_POST]
        r.out_low[rows, :] = ended.astype(BF)
        back, d_gain = rms_back(value, gain[G_POST], r.cot[rows, :].astype(F32))
        r.low[rows, :] = back.astype(BF)
        return kept + d_gain

    none = jnp.zeros((1, D), F32)
    put_gain(G_POST, chunks(3, finish_forward, none))
    net.drain()

    sums = [
        Reduce(net, k, r.g_qkv if k == QKV else w[k], pieces[k][0], pieces[k][1:], r.totals[k])
        for k in range(5)
    ]

    def reduce(step, *which):
        for name in which:
            step(sums[name])

    def paired(name, i):
        sums[name].pair((own_x + 1 + i) % 4)
        if i < 3:
            sums[name].along_x(i + 1)

    for i in range(4):
        x = (own_x + 1 + i) % 4
        columns = pl.ds(pl.multiple_of(x * 512, 512), 512)
        d_act = nt(r.low[...], w[DOWN][x])
        r.d_gate[:, columns] = (d_act * r.d_gate[:, columns].astype(F32)).astype(BF)
        r.d_up[:, columns] = (d_act * r.d_up[:, columns].astype(F32)).astype(BF)
        w[DOWN][x] = nn(r.activ[:, columns].T, r.low[...]).astype(BF)
        sums[DOWN].start(x)
        if i:
            paired(DOWN, i - 1)
    r.flip[:, 0:TOK] = r.second[...].T
    r.wide[...] = jnp.zeros((TOK, D), F32)
    for i in range(4):
        x = (own_x + 1 + i) % 4
        columns = pl.ds(pl.multiple_of(x * 512, 512), 512)
        d_gate, d_up = (r.d_gate[:, columns], r.d_up[:, columns])
        r.wide[...] += nt(d_gate, w[GATE][x]) + nt(d_up, w[UP][x])
        w[GATE][x] = nn(r.flip[:, 0:TOK], d_gate).astype(BF)
        sums[GATE].start(x)
        w[UP][x] = nn(r.flip[:, 0:TOK], d_up).astype(BF)
        sums[UP].start(x)
        if i:
            paired(GATE, i - 1)
            paired(UP, i - 1)
        else:
            paired(DOWN, 3)

    def to_hidden(rows, i, kept):
        d_pre, d_att = kept
        back, d_gain = rms_back(r.hidden[rows, :], gain[G_PRE], r.wide[rows, :])
        back = back + r.cot[rows, :].astype(F32)
        r.wide[rows, :] = back
        back, d_gain_att = rms_back(r.proj[rows, :], gain[G_ATT], back)
        r.low[rows, :] = back.astype(BF)
        return d_pre + d_gain, d_att + d_gain_att

    d_pre, d_att = chunks(3, to_hidden, (none, none))
    put_gain(G_PRE, d_pre)
    put_gain(G_ATT, d_att)
    paired(GATE, 3)
    paired(UP, 3)
    for i in range(4):
        h = (own_x + 1 + i) % 4
        columns = pl.ds(pl.multiple_of(h * HD, HD), HD)
        rows = pl.ds(pl.multiple_of(h * 128, 128), 128)
        d_head = nt(r.low[...], w[OUT][h])
        for b in range(3):
            r.d_att[b, rows, :] = (
                d_head[b * 128 : (b + 1) * 128, :] * r.inverse[b, rows, :]
            ).astype(BF)
        w[OUT][h] = nn(r.att[:, columns].T, r.low[...]).astype(BF)
        sums[OUT].start(h)
        if i:
            paired(OUT, i - 1)
    r.dkv[...] = jnp.zeros((BEHIND + TOK, 2 * HD), F32)

    def attend_back(b, d_q):
        window = pl.ds(b * 128, KEYS)
        at = pl.ds(b * 128, 128)
        r.scores[...] = nt(r.d_att[b], r.v_ext[window, :])
        for h in range(H):
            rows = pl.ds(h * 128, 128)
            both = r.d_att[b, rows, :].astype(F32) * r.att[at, h * HD : (h + 1) * HD].astype(F32)
            delta = jnp.sum(both, axis=1, keepdims=True)
            r.d_scores[rows, :] = (
                r.exps[b, rows, :].astype(F32) * (r.scores[rows, :] - delta)
            ).astype(BF)
        r.dkv[window, 0:HD] += nn(r.d_scores[...].T, r.q_rot[b])
        r.dkv[window, HD:] += nn(r.exps[b].T, r.d_att[b])
        d_query = nn(r.d_scores[...], r.k_ext[window, :]) * HD**-0.5
        for h in range(H):
            back = turn_back(d_query[h * 128 : (h + 1) * 128, :], *own_turn(b))
            value = r.mixed[at, h * HD : (h + 1) * HD].astype(F32)
            back, d_gain = rms_back(value, gain[G_Q], back)
            r.d_mixed[at, h * HD : (h + 1) * HD] = back.astype(BF)
            d_q = d_q + d_gain
        return d_q

    d_q = attend_back(0, jnp.zeros((1, HD), F32))
    paired(OUT, 3)
    reduce(Reduce.after_first, DOWN)
    d_q = attend_back(1, d_q)
    r.flip[...] = r.normed[...].T
    d_q = attend_back(2, d_q)
    put_gain(G_Q, d_q)
    reduce(Reduce.after_first, GATE, UP)

    def keys_back(rows, i, d_k):
        both = r.dkv[rows, :]
        back = turn_back(both[:, :HD], r.cos[rows, :], r.sin[rows, :])
        back, d_gain = rms_back(r.k_raw[rows, :].astype(F32), gain[G_K], back)
        r.d_kv[rows, 0:HD] = back.astype(BF)
        r.d_kv[rows, HD:] = both[:, HD:].astype(BF)
        return d_k + d_gain

    put_gain(G_K, chunks(7, keys_back, jnp.zeros((1, HD), F32)))
    back_two = net.send(r.d_kv.at[pl.ds(0, 128)], r.halo_two, "seq", -2)
    back_one = net.send(r.d_kv.at[pl.ds(128, TOK)], r.halo_one, "seq", -1)
    flip_own = r.flip[:, BEHIND:]
    for x in range(4):
        if x < 2:
            r.g_qkv[x] = nn(flip_own, r.d_mixed[:, x * 384 : (x + 1) * 384]).astype(BF)
        elif x == 2:
            r.g_qkv[x, :, 0:256] = nn(flip_own, r.d_mixed[:, 768:1024]).astype(BF)
            r.g_qkv[x, :, 256:384] = nn(r.flip[...], r.d_kv[:, 0:128]).astype(BF)
        else:
            r.g_qkv[x] = nn(r.flip[...], r.d_kv[:, 128:512]).astype(BF)
        sums[QKV].start(x)
        if x:
            sums[QKV].pair(x - 1)
    sums[QKV].pair(3)
    for j in PEERS:
        sums[QKV].along_x(j)
    reduce(Reduce.after_first, OUT)
    reduce(Reduce.after_second, DOWN)
    back_two.arrived()
    back_one.arrived()
    r.d_mixed[:, 1024:1536] = r.d_kv[BEHIND:, :] + r.halo_one[...]
    last = pl.ds(256, 128)
    r.d_mixed[last, 1024:1536] = r.d_mixed[last, 1024:1536] + r.halo_two[...]
    r.proj[...] = (
        nt(r.d_mixed[:, 0:384], w[QKV][0])
        + nt(r.d_mixed[:, 384:768], w[QKV][1])
        + nt(r.d_mixed[:, 768:1152], w[QKV][2])
        + nt(r.d_mixed[:, 1152:1536], w[QKV][3])
    )

    def to_input(rows, i, kept):
        value = r.x_ext[pl.ds(pl.multiple_of(BEHIND + i * 128, 128), 128), :].astype(F32)
        back, d_gain = rms_back(value, gain[G_IN], r.proj[rows, :])
        r.wide[rows, :] += back
        return kept + d_gain

    put_gain(G_IN, chunks(3, to_input, none))
    gains = ReduceGains(net, r.gain_got)
    gains.start(r.gain_grad[...])

    reduce(Reduce.after_first, QKV)
    reduce(Reduce.after_second, GATE, UP, OUT)
    reduce(Reduce.after_third, DOWN)
    gains.step(0)
    reduce(Reduce.after_second, QKV)
    reduce(Reduce.after_third, GATE, UP, OUT)
    reduce(Reduce.share, DOWN)
    gains.step(1)
    reduce(Reduce.after_third, QKV)
    reduce(Reduce.share, GATE, UP, OUT)
    gains.step(2)
    reduce(Reduce.share, QKV)
    r.s_gains[...] = gains.step(3)
    reduce(Reduce.finish, DOWN, GATE, UP, OUT, QKV)
    net.drain()


def run_block(tokens, cotangent, segment, masters, gains):
    vmem, anywhere = (pl.BlockSpec(memory_space=pltpu.VMEM), pl.BlockSpec(memory_space=pl.ANY))
    freqs = (ROPE_BASE ** (-np.arange(128) * 2.0 / HD)).astype(np.float32).reshape(1, 128)
    block_output, input_grad, gain_sums, *rest = pl.pallas_call(
        block_kernel,
        out_shape=[pltpu.VMEM((TOK, D), BF), pltpu.VMEM((TOK, D), F32), pltpu.VMEM((4, 8, 128), F32)]
        + [pltpu.VMEM(shape, BF) for shape in SHARD]
        + [pltpu.VMEM(shape, F32) for shape in SHARD],
        in_specs=[anywhere, anywhere, vmem, vmem, vmem] + [anywhere] * 5,
        out_specs=[vmem] * 13,
        scratch_shapes=[pltpu.VMEM((4,) + shape, BF) for shape in SHARD]
        + [pltpu.VMEM(shape, kind) for _, shape, kind in SCRATCH]
        + reduce_scratch()
        + [
            pltpu.SemaphoreType.DMA((COPIES,)),
            pltpu.SemaphoreType.DMA((COPIES,)),
            pltpu.SemaphoreType.DMA((LOADS,)),
        ],
        compiler_params=pltpu.CompilerParams(
            collective_id=0, has_side_effects=True, vmem_limit_bytes=BLOCK_BYTES
        ),
        name="block",
    )(
        tokens,
        cotangent,
        segment.reshape(3, 128),
        gains.reshape(6, 128),
        jnp.asarray(freqs),
        *masters,
    )
    return block_output, input_grad, rest[:5], rest[5:], gain_sums


def reciprocal(value):
    guess = pl.reciprocal(value, approx=True)
    return guess * (2.0 - value * guess)


def adamw(weight, gradient, first, second, rate, decay):
    first_new = ADAM_ONE * first + (1.0 - ADAM_ONE) * gradient
    second_new = ADAM_TWO * second + (1.0 - ADAM_TWO) * (gradient * gradient)
    second_hat = second_new * (1.0 / (1.0 - ADAM_TWO**STEP))
    root = second_hat * lax.rsqrt(second_hat)
    step = (first_new * (rate / (1.0 - ADAM_ONE**STEP))) * reciprocal(root + ADAM_EPS)
    weight_new = weight * (1.0 - rate * decay) - step
    return (weight_new, first_new, second_new)


CHUNKS = 4


def update_kernel(*refs):
    taken = iter(refs)
    take = lambda count: [next(taken) for _ in range(count)]
    states, weights, gradients = ([take(2) for _ in SHARD], take(5), take(5))
    gain_states, gain_sums, done = (take(3), next(taken), take(2))
    results, fresh, gain_fresh = (take(2), [take(3) for _ in SHARD], take(3))
    held, weight_new = (take(5), take(5))
    in_sems, out_sems, done_sems = take(3)

    def part(k, chunk):
        count = SHARD[k][0] // CHUNKS
        return pl.ds(chunk * count, count)

    for k in range(5):
        for chunk in range(CHUNKS):
            rows = part(k, chunk)
            for p in range(2):
                pltpu.make_async_copy(
                    states[k][p].at[rows], held[k].at[p, rows], in_sems.at[k, chunk]
                ).start()
    passed = [pltpu.make_async_copy(done[p], results[p], done_sems.at[p]) for p in range(2)]
    for copy in passed:
        copy.start()
    own = gain_sums[lax.axis_index("wsh"), 0:6]
    for ref, value in zip(
        gain_fresh, adamw(gain_states[0][...], own, gain_states[1][...], gain_states[2][...], GAIN_RATE, 0.0)
    ):
        ref[...] = value
    for k in range(5):
        for chunk in range(CHUNKS):
            rows = part(k, chunk)
            whole = held[k].at[:, rows]
            pltpu.make_async_copy(whole, whole, in_sems.at[k, chunk]).wait()
            gradient = gradients[k][rows, :].astype(F32)
            values = adamw(
                weights[k][rows, :],
                gradient,
                held[k][0, rows, :],
                held[k][1, rows, :],
                MATRIX_RATE,
                MATRIX_DECAY,
            )
            weight_new[k][rows, :] = values[0]
            held[k][0, rows, :] = values[1]
            held[k][1, rows, :] = values[2]
            for p, source in enumerate((weight_new[k].at[rows], held[k].at[0, rows], held[k].at[1, rows])):
                pltpu.make_async_copy(source, fresh[k][p].at[rows], out_sems.at[k, p]).start()
    for k in range(5):
        for p in range(3):
            whole = weight_new[k]
            pltpu.make_async_copy(whole, whole, out_sems.at[k, p]).wait()
    for copy in passed:
        copy.wait()


def update(states, weights, gradients, gain_states, gain_sums, done):
    vmem, hbm = (pl.BlockSpec(memory_space=pltpu.VMEM), pl.BlockSpec(memory_space=pltpu.HBM))
    here = [
        pltpu.with_memory_space_constraint(a, pltpu.VMEM)
        for a in (*weights, *gradients, gain_sums, *done)
    ]
    there = [pltpu.with_memory_space_constraint(a, pltpu.HBM) for state in states for a in state]
    got = pl.pallas_call(
        update_kernel,
        out_shape=[jax.ShapeDtypeStruct(a.shape, a.dtype) for a in done]
        + [jax.ShapeDtypeStruct(shape, F32) for shape in SHARD for _ in range(3)]
        + [jax.ShapeDtypeStruct((6, 128), F32)] * 3,
        in_specs=[hbm] * 10 + [vmem] * 16,
        out_specs=[hbm] * 17 + [vmem] * 3,
        scratch_shapes=[pltpu.VMEM((2,) + shape, F32) for shape in SHARD]
        + [pltpu.VMEM(shape, F32) for shape in SHARD]
        + [
            pltpu.SemaphoreType.DMA((5, CHUNKS)),
            pltpu.SemaphoreType.DMA((5, 3)),
            pltpu.SemaphoreType.DMA((2,)),
        ],
        compiler_params=pltpu.CompilerParams(vmem_limit_bytes=UPDATE_BYTES),
        name="update",
    )(*there, *here[:10], *gain_states, *here[10:])
    return tuple(got[:17]) + tuple(a.reshape(768) for a in got[17:])


def on_device(
    tokens,
    cotangent,
    segment,
    qkv_weight,
    out_weight,
    gate_weight,
    up_weight,
    down_weight,
    gains,
    qkv_first,
    qkv_second,
    out_first,
    out_second,
    gate_first,
    gate_second,
    up_first,
    up_second,
    down_first,
    down_second,
    gain_first,
    gain_second,
):
    masters = (qkv_weight, out_weight, gate_weight, up_weight, down_weight)
    block_output, input_grad, sums, fulls, gain_sums = run_block(
        tokens, cotangent, segment, masters, gains
    )
    states = (
        (qkv_first, qkv_second),
        (out_first, out_second),
        (gate_first, gate_second),
        (up_first, up_second),
        (down_first, down_second),
    )
    gain_states = [a.reshape(6, 128) for a in (gains, gain_first, gain_second)]
    return update(states, fulls, sums, gain_states, gain_sums, (block_output, input_grad))


def solution(mesh):
    placed = (
        P(("wsh", "seq"), None),
        P(("wsh", "seq"), None),
        P(("wsh", "seq")),
        P(None, "wsh"),
        P("wsh", None),
        P(None, "wsh"),
        P(None, "wsh"),
        P("wsh", None),
        P("wsh"),
        P(None, "wsh"),
        P(None, "wsh"),
        P("wsh", None),
        P("wsh", None),
        P(None, "wsh"),
        P(None, "wsh"),
        P(None, "wsh"),
        P(None, "wsh"),
        P("wsh", None),
        P("wsh", None),
        P("wsh"),
        P("wsh"),
    )
    return jax.shard_map(
        on_device,
        mesh=mesh,
        in_specs=placed,
        out_specs=(
            P(("wsh", "seq"), None),
            P(("wsh", "seq"), None),
            P(None, "wsh"),
            P(None, "wsh"),
            P(None, "wsh"),
            P("wsh", None),
            P("wsh", None),
            P("wsh", None),
            P(None, "wsh"),
            P(None, "wsh"),
            P(None, "wsh"),
            P(None, "wsh"),
            P(None, "wsh"),
            P(None, "wsh"),
            P("wsh", None),
            P("wsh", None),
            P("wsh", None),
            P("wsh"),
            P("wsh"),
            P("wsh"),
        ),
        check_vma=False,
    )
```

```python
import types

import jax
import jax.numpy as jnp
import numpy as np
from jax import lax
from jax.experimental import pallas as pl
from jax.experimental.pallas import tpu as pltpu
from jax.sharding import PartitionSpec as P

D = 640
H = 4
HD = 256
WIN = 512
STEP = 10


EPS = 1e-06
ADAM_ONE = 0.9
ADAM_TWO = 0.999
ADAM_EPS = 1e-08
MATRIX_DECAY = 0.1
MATRIX_RATE = 0.05
GAIN_RATE = 0.8
ROPE_BASE = 10000.0


BLOCK_BYTES, UPDATE_BYTES = (49 * 2**20, 24 * 2**20)
BF, F32 = (jnp.bfloat16, jnp.float32)
MESH = pl.DeviceIdType.MESH
AXES = 4
QKV, OUT, GATE, UP, DOWN = range(5)
SHARD = ((640, 384), (256, 640), (640, 512), (640, 512), (512, 640))
GATHERED = (
    ((0, 128, "y"), (128, 256, "z")),
    ((0, 640, ""),),
    ((0, 256, "y"), (256, 256, "z")),
    ((0, 256, "y"), (256, 256, "z")),
    ((0, 384, "y"), (384, 256, "z")),
)
REDUCED = (
    ((0, 128, "y", "y"), (128, 128, "z", "z"), (256, 128, "y", "x")),
    ((0, 128, "y", "y"), (128, 256, "z", "z"), (384, 256, "y", "x")),
    ((0, 256, "y", "y"), (256, 128, "z", "z"), (384, 128, "z", "x")),
    ((0, 128, "y", "y"), (128, 256, "z", "z"), (384, 128, "y", "x")),
    ((0, 256, "y", "y"), (256, 128, "z", "z"), (384, 256, "z", "x")),
)
OTHER = {"y": "z", "z": "y"}
PEERS = (1, 2, 3)


class Net:
    def __init__(self, send_sems, recv_sems):
        token = lax.axis_index("seq")
        self.at = {"x": lax.axis_index("wsh"), "y": (token // 2) % 4, "z": token // 8, "c": token % 2}
        self.send_sems, self.recv_sems, self.count, self.started = (send_sems, recv_sems, 0, [])

    def peer(self, axis, by):
        size = 2 if axis == "c" else AXES
        return (self.at[axis] + by) % size

    def device(self, axis, by):
        if axis == "seq":
            return ((lax.axis_index("seq") + by) % 32, self.at["x"])
        at = dict(self.at)
        if isinstance(by, tuple):
            by, at["c"] = (by[0], 1 - at["c"])
        at[axis] = self.peer(axis, by)
        return ((at["z"] * 4 + at["y"]) * 2 + at["c"], at["x"])

    def greet(self):
        barrier = pltpu.get_barrier_semaphore()
        peers = [(axis, by) for axis in "xyz" for by in PEERS] + [("c", 1)]
        peers += [(axis, (by, 1)) for axis in "yz" for by in PEERS]
        peers += [("seq", by) for by in (1, 2, -1, -2)]
        for axis, by in peers:
            pl.semaphore_signal(
                barrier, inc=1, device_id=self.device(axis, by), device_id_type=MESH
            )
        pl.semaphore_wait(barrier, len(peers))

    def batch(self, size):
        made = Batch(self, size, self.send_sems.at[self.count], self.recv_sems.at[self.count])
        self.count += 1
        self.started.append(made)
        return made

    def send(self, src, dst, axis, by):
        return self.batch(src).add(src, dst, axis, by)

    def drain(self):
        for made in self.started:
            pltpu.make_async_copy(made.size, made.size, made.send_sem).wait()
        self.started = []


class Batch:
    def __init__(self, net, size, send_sem, recv_sem):
        self.net, self.size, self.send_sem, self.recv_sem = (net, size, send_sem, recv_sem)

    def add(self, src, dst, axis, by):
        pltpu.make_async_remote_copy(
            src_ref=src,
            dst_ref=dst,
            send_sem=self.send_sem,
            recv_sem=self.recv_sem,
            device_id=self.net.device(axis, by),
            device_id_type=MESH,
        ).start()
        return self

    def arrived(self):
        pltpu.make_async_copy(self.size, self.size, self.recv_sem).wait()


class Gather:
    def __init__(self, net, weight, full):
        self.net, self.full, (self.rows, _), self.parts = (
            net,
            full,
            SHARD[weight],
            GATHERED[weight],
        )
        self.eighth, self.direct = (self.rows // 8, not self.parts[0][2])

    def block(self, x, part):
        first, width, axis = part
        at, count = (net_half(self.net, self.rows), self.rows // 2)
        if axis:
            at, count = (at + self.net.at[axis] * self.eighth, self.eighth)
        return self.full.at[x, pl.ds(pl.multiple_of(at, 16), count), pl.ds(first, width)]

    def start(self):
        each = self.rows // 2 if self.direct else self.eighth
        self.along_x = self.net.batch(self.full.at[0:3, pl.ds(0, each), :])
        for part in self.parts:
            mine = self.block(self.net.at["x"], part)
            for j in PEERS:
                self.along_x.add(mine, mine, "x", j)

    def spread(self):
        self.along_x.arrived()
        self.along_q = self.net.batch(self.full.at[0:3, pl.ds(0, 3 * self.eighth), :])
        for j in PEERS:
            for part in self.parts:
                got = self.block(self.net.peer("x", -j), part)
                for k in PEERS:
                    self.along_q.add(got, got, part[2], k)

    def share(self):
        (self.along_x if self.direct else self.along_q).arrived()
        half = self.rows // 2
        self.to_core = self.net.batch(self.full.at[0:3, pl.ds(0, half), :])
        for j in PEERS:
            got = self.full.at[self.net.peer("x", -j), pl.ds(net_half(self.net, self.rows), half), :]
            self.to_core.add(got, got, "c", 1)

    def finish(self):
        self.to_core.arrived()


def net_half(net, rows):
    return pl.multiple_of(net.at["c"] * (rows // 2), 16)


class Reduce:
    def __init__(self, net, weight, grad, core_got, got, total):
        self.net, self.grad, self.core_got, self.total = (net, grad, core_got, total)
        self.rows, self.columns = SHARD[weight]
        self.parts = [
            (pl.ds(first, width), axis, order, got[3 * k : 3 * k + 3])
            for k, (first, width, axis, order) in enumerate(REDUCED[weight])
        ]
        self.half, self.eighth = (self.rows // 2, self.rows // 8)
        self.half_start = net_half(net, self.rows)
        self.core, self.firsts = ([], None)
        self.merged = weight == QKV

    def block(self, q):
        return pl.ds(pl.multiple_of(self.half_start + q * self.eighth, 16), self.eighth)

    def start(self, x):
        there = pl.multiple_of((1 - self.net.at["c"]) * self.half, 16)
        mine = self.grad.at[x, pl.ds(there, self.half), :]
        self.core.append(self.net.batch(mine).add(mine, self.core_got.at[x], "c", 1))

    def pair(self, x):
        self.core.pop(0).arrived()

        def add(block, carry):
            local = pl.ds(pl.multiple_of(block * self.eighth, 16), self.eighth)
            rows = self.block(block)
            self.grad[x, rows, :] = self.grad[x, rows, :] + self.core_got[x, local, :]
            return carry

        lax.fori_loop(0, 4, add, 0)
        if self.firsts is None:
            self.firsts = self.net.batch(self.grad.at[0:3, pl.ds(0, self.half), :])
        for columns, axis, order, got in self.parts:
            if order != "x":
                for j in PEERS:
                    src = self.grad.at[x, self.block(self.net.peer(axis, j)), columns]
                    self.firsts.add(src, got[0].at[j - 1, x], order, j)

    def along_x(self, j):
        for columns, axis, order, got in self.parts:
            if order == "x":
                rows = pl.ds(self.half_start, self.half)
                src = self.grad.at[self.net.peer("x", j), rows, columns]
                self.firsts.add(src, got[0].at[j - 1], order, j)

    def after_first(self):
        self.firsts.arrived()
        self.seconds = self.net.batch(self.grad.at[0, pl.ds(0, 3 * self.eighth), :])
        for columns, axis, order, got in self.parts:
            own = self.net.at[axis]

            def add(step, carry):
                if order == "x":
                    x, rows = (self.net.at["x"], self.block(step))
                    local = pl.ds(pl.multiple_of(step * self.eighth, 16), self.eighth)
                    pieces = [got[0][j, local, :] for j in range(3)]
                else:
                    x, rows = (step, self.block(own))
                    pieces = [got[0][j, step] for j in range(3)]
                total = self.grad[x, rows, columns].astype(F32)
                for piece in pieces:
                    total = total + piece.astype(F32)
                self.grad[x, rows, columns] = total.astype(BF)
                return carry

            lax.fori_loop(0, 4, add, 0)
            for j in PEERS:
                if order == "x":
                    x, q, along = (self.net.at["x"], self.net.peer(axis, j), axis)
                else:
                    x, q, along = (self.net.peer("x", j), own, "x")
                src = self.grad.at[x, self.block(q), columns]
                self.seconds.add(src, got[1].at[j - 1], along, j)

    def after_second(self):
        self.seconds.arrived()
        self.thirds = self.net.batch(self.grad.at[0, pl.ds(0, 3 * self.eighth), :])
        for columns, axis, order, got in self.parts:
            rows = self.block(self.net.at[axis])
            total = self.grad[self.net.at["x"], rows, columns].astype(F32)
            for j in range(3):
                total = total + got[1][j].astype(F32)
            mine = got[2].at[self.net.at[OTHER[axis]]]
            mine[...] = total.astype(BF)
            for j in PEERS:
                self.thirds.add(mine, mine, OTHER[axis], j)

    def after_third(self):
        self.thirds.arrived()
        count = 7 if self.merged else 3
        self.fourths = self.net.batch(self.grad.at[0, pl.ds(0, count * self.eighth), :])
        for columns, axis, order, got in self.parts:
            total = got[2][0].astype(F32)
            for j in PEERS:
                total = total + got[2][j].astype(F32)
            mine = self.total.at[self.block(self.net.at[axis]), columns]
            mine[...] = total.astype(BF)
            for j in PEERS:
                self.fourths.add(mine, mine, axis, j)
                if self.merged:
                    self.fourths.add(mine, mine, axis, (j, 1))
            if self.merged:
                self.fourths.add(mine, mine, "c", 1)

    def share(self):
        self.fourths.arrived()
        if self.merged:
            return
        mine = self.total.at[pl.ds(self.half_start, self.half), :]
        self.fifth = self.net.batch(mine).add(mine, mine, "c", 1)

    def finish(self):
        if not self.merged:
            self.fifth.arrived()


class ReduceGains:
    def __init__(self, net, got):
        self.net, self.got = (net, got)

    def start(self, value):
        self.post(0, value)

    def post(self, stage, value):
        axis, peers = ("cxyz"[stage], PEERS if stage else (1,))
        mine = self.got.at[stage, self.net.at[axis]]
        mine[...] = value
        self.copies = self.net.batch(self.got.at[0, 0 : len(peers)])
        for j in peers:
            self.copies.add(mine, mine, axis, j)

    def step(self, stage):
        self.copies.arrived()
        total = self.got[stage, 0] + self.got[stage, 1]
        if stage:
            total = total + self.got[stage, 2] + self.got[stage, 3]
        if stage < 3:
            self.post(stage + 1, total)
        return total


def reduce_scratch():
    shapes = []
    for (rows, columns), parts in zip(SHARD, REDUCED):
        shapes.append((4, rows // 2, columns))
        for _, width, _, order in parts:
            shapes += [
                (3, rows // 2, width) if order == "x" else (3, 4, rows // 8, width),
                (3, rows // 8, width),
                (4, rows // 8, width),
            ]
    return [pltpu.VMEM(shape, BF) for shape in shapes]


TOK = 384
BEHIND = 512
KEYS = 640
G_IN, G_ATT, G_PRE, G_POST, G_Q, G_K = range(6)
NORM_ROWS = ((0, 5), (5, 5), (10, 5), (15, 5), (20, 2), (22, 2))

SCRATCH = (
    ("g_qkv", (4,) + SHARD[QKV], BF),
    ("x_ext", (BEHIND + TOK, D), BF),
    ("normed", (BEHIND + TOK, D), BF),
    ("cos", (BEHIND + TOK, 128), F32),
    ("sin", (BEHIND + TOK, 128), F32),
    ("mixed", (TOK, 1024), BF),
    ("k_raw", (BEHIND + TOK, HD), BF),
    ("q_rot", (3, 512, HD), BF),
    ("k_ext", (BEHIND + TOK, HD), BF),
    ("v_ext", (BEHIND + TOK, HD), BF),
    ("exps", (3, 512, KEYS), BF),
    ("scores", (512, KEYS), F32),
    ("inverse", (3, 512, 1), F32),
    ("att", (TOK, H * HD), BF),
    ("proj", (TOK, D), F32),
    ("hidden", (TOK, D), F32),
    ("second", (TOK, D), BF),
    ("flip", (D, BEHIND + TOK), BF),
    ("activ", (TOK, 2048), BF),
    ("d_gate", (TOK, 2048), BF),
    ("d_up", (TOK, 2048), BF),
    ("low", (TOK, D), BF),
    ("cot", (TOK, D), BF),
    ("d_att", (3, 512, HD), BF),
    ("d_scores", (512, KEYS), BF),
    ("halo_one", (TOK, 2 * HD), BF),
    ("halo_two", (128, 2 * HD), BF),
    ("gain_all", (4, 8, 128), F32),
    ("gain_grad", (4, 8, 128), F32),
    ("gain_got", (4, 4, 4, 8, 128), F32),
    ("ids", (8, 128), jnp.int32),
    ("ids_one", (8, 128), jnp.int32),
    ("ids_two", (8, 128), jnp.int32),
)
COPIES = 5 * 3 - 1 + 5 * 9 + 6 + 5
LOADS = 12


def nt(a, b):
    return lax.dot_general(a, b, (((1,), (1,)), ((), ())), preferred_element_type=F32)


def nn(a, b):
    return jnp.dot(a, b, preferred_element_type=F32)


def inverse_rms(value):
    return lax.rsqrt(jnp.mean(value * value, axis=-1, keepdims=True) + EPS)


def rms_back(value, gain, grad):
    scale = inverse_rms(value)
    unit = value * scale
    weighted = grad * gain
    back = scale * (weighted - unit * jnp.mean(weighted * unit, axis=-1, keepdims=True))
    return back, jnp.sum(grad * unit, axis=0, keepdims=True)


def turn(value, cosine, sine):
    first, last = (value[:, :128], value[:, 128:])
    return jnp.concatenate([first * cosine - last * sine, last * cosine + first * sine], axis=1)


def turn_back(grad, cosine, sine):
    first, last = (grad[:, :128], grad[:, 128:])
    return jnp.concatenate([first * cosine + last * sine, last * cosine - first * sine], axis=1)


def block_kernel(*refs):
    taken = iter(refs)
    r, take = (types.SimpleNamespace(), lambda count: [next(taken) for _ in range(count)])
    r.tokens, r.cotangent, r.segment, r.gains, r.freqs = take(5)
    r.masters, r.states = (take(5), take(4))
    r.out_low, r.wide, r.s_gains, r.moments = take(4)
    r.totals, r.fulls, w = (take(5), take(5), take(5))
    for name, _, _ in SCRATCH:
        setattr(r, name, next(taken))
    pieces = [take(1 + 3 * len(parts)) for parts in REDUCED]
    send_sems, recv_sems, load_sems = take(3)
    net = Net(send_sems, recv_sems)
    own_x = net.at["x"]
    base = lax.axis_index("seq") * TOK
    loads = []

    def local(src, dst):
        copy = pltpu.make_async_copy(src, dst, load_sems.at[len(loads)])
        loads.append(copy)
        copy.start()
        return copy

    def chunks(count, body, carry=0):
        return lax.fori_loop(
            0, count, lambda i, kept: body(pl.ds(pl.multiple_of(i * 128, 128), 128), i, kept), carry
        )

    own_rows = pl.ds(BEHIND, TOK)
    fill = {QKV: local(r.masters[QKV], r.fulls[QKV])}
    fill_tokens = local(r.tokens, r.x_ext.at[own_rows])
    for name in (OUT, GATE, UP, DOWN):
        fill[name] = local(r.masters[name], r.fulls[name])
    fill_cot = local(r.cotangent, r.cot)
    r.gain_all[...] = jnp.zeros((4, 8, 128), F32)
    r.gain_grad[...] = jnp.zeros((4, 8, 128), F32)
    r.gain_all[own_x, 0:6] = r.gains[...].astype(BF).astype(F32)
    r.ids[...] = jnp.zeros((8, 128), jnp.int32)
    r.ids[0:3] = r.segment[...]
    net.greet()

    mine = r.gain_all.at[own_x]
    gain_copies = net.batch(r.gain_all.at[0:3])
    for j in PEERS:
        gain_copies.add(mine, mine, "x", j)
    parts = [Gather(net, name, w[name]) for name in range(5)]

    def launch(name):
        fill[name].wait()
        rows = SHARD[name][0] // 8

        def cast(step, carry):
            at = pl.ds(pl.multiple_of(step * rows, 16), rows)
            w[name][own_x, at, :] = r.fulls[name][at, :].astype(BF)
            return carry

        lax.fori_loop(0, 8, cast, 0)
        parts[name].start()

    def arrive(step, *which):
        for name in which:
            step(parts[name])

    launch(QKV)
    fill_tokens.wait()
    halo_copies = [
        net.send(r.x_ext.at[own_rows], r.x_ext.at[pl.ds(128, TOK)], "seq", 1),
        net.send(r.x_ext.at[pl.ds(BEHIND + 256, 128)], r.x_ext.at[pl.ds(0, 128)], "seq", 2),
        net.send(r.ids, r.ids_one, "seq", 1),
        net.send(r.ids, r.ids_two, "seq", 2),
    ]

    def angles(rows, i, kept):
        place = (base - BEHIND + i * 128 + lax.broadcasted_iota(jnp.int32, (128, 128), 0)).astype(F32)
        angle = place * r.freqs[...]
        r.cos[rows, :] = jnp.cos(angle)
        r.sin[rows, :] = jnp.sin(angle)
        return kept

    chunks(7, angles)
    launch(GATE)
    launch(UP)
    arrive(Gather.spread, QKV, GATE, UP)
    launch(DOWN)
    launch(OUT)
    gain_copies.arrived()
    gain = {}
    for name, (first, count) in enumerate(NORM_ROWS):
        rows = [(k // 6, k % 6) for k in range(first, first + count)]
        gain[name] = jnp.concatenate([r.gain_all[g, k : k + 1, :] for g, k in rows], axis=1)

    def put_gain(name, value):
        first, count = NORM_ROWS[name]
        for k in range(count):
            g, row = ((first + k) // 6, (first + k) % 6)
            r.gain_grad[g, row : row + 1, :] = value[:, 128 * k : 128 * (k + 1)]

    for copy in halo_copies:
        copy.arrived()

    def normalise(rows, i, kept):
        value = r.x_ext[rows, :].astype(F32)
        r.normed[rows, :] = (value * inverse_rms(value) * gain[G_IN]).astype(BF)
        return kept

    chunks(7, normalise)
    arrive(Gather.share, QKV)
    arrive(Gather.finish, QKV)

    normed_own = r.normed[own_rows, :]
    for x in range(4):
        width = 384 if x < 2 else (256 if x == 2 else 0)
        if width:
            r.mixed[:, x * 384 : x * 384 + width] = nn(
                normed_own, w[QKV][x, :, :width]
            ).astype(BF)
    normed_all = r.normed[...]
    head = nn(normed_all, w[QKV][2, :, 256:384])
    tail = nn(normed_all, w[QKV][3])
    for at, rows in ((0, slice(0, 640)), (1, slice(640, 896))):
        count = rows.stop - rows.start
        r.moments[at, 0:count, 0:128] = head[rows]
        r.moments[at, 0:count, 128:256] = tail[rows, :128]
    r.k_raw[:, 0:128] = head.astype(BF)
    r.k_raw[:, 128:256] = tail[:, :128].astype(BF)
    r.v_ext[...] = tail[:, 128:].astype(BF)
    arrive(Gather.spread, DOWN)

    def held(i):
        return i // 5, pl.ds(pl.multiple_of(i % 5 * 128, 128), 128)

    def keys(rows, i, kept):
        value = r.moments[(*held(i), slice(0, 256))]
        value = value * inverse_rms(value) * gain[G_K]
        r.k_ext[rows, :] = turn(value, r.cos[rows, :], r.sin[rows, :]).astype(BF)
        return kept

    chunks(7, keys)

    def own_turn(i):
        at = pl.ds(pl.multiple_of(BEHIND + i * 128, 128), 128)
        return r.cos[at, :], r.sin[at, :]

    def queries(rows, i, kept):
        for h in range(H):
            value = r.mixed[rows, h * HD : (h + 1) * HD].astype(F32)
            value = value * inverse_rms(value) * gain[G_Q]
            r.q_rot[i, h * 128 : (h + 1) * 128, :] = (
                turn(value, *own_turn(i)) * HD**-0.5
            ).astype(BF)
        return kept

    chunks(3, queries)
    arrive(Gather.share, OUT)

    id_rows = [r.ids_two[2:3, :]] + [r.ids_one[k : k + 1, :] for k in range(3)]
    id_rows = [row.astype(F32) for row in id_rows + [r.ids[k : k + 1, :] for k in range(3)]]

    def attend(b):
        down_rows = lax.broadcasted_iota(jnp.int32, (128, 128), 0)
        across = lax.broadcasted_iota(jnp.int32, (128, 128), 1)
        own_id = jnp.broadcast_to(id_rows[4 + b], (128, 128)).T
        for j in range(5):
            allowed = jnp.broadcast_to(id_rows[b + j], (128, 128)) == own_id
            allowed = allowed & (base - BEHIND + (b + j) * 128 + across >= 0)
            if j == 0:
                allowed = allowed & (across > down_rows)
            if j == 4:
                allowed = allowed & (across <= down_rows)
            r.wide[0:128, j * 128 : (j + 1) * 128] = jnp.where(allowed, 0.0, -1e30)
        window = pl.ds(b * 128, KEYS)
        r.scores[...] = nt(r.q_rot[b], r.k_ext[window, :])
        for h in range(H):
            rows = pl.ds(h * 128, 128)
            weight = jnp.exp(r.scores[rows, :] + r.wide[0:128, :])
            r.inverse[b, rows, :] = 1.0 / jnp.sum(weight, axis=1, keepdims=True)
            r.exps[b, rows, :] = weight.astype(BF)
        mean = nn(r.exps[b], r.v_ext[window, :]) * r.inverse[b]
        for h in range(H):
            r.att[pl.ds(b * 128, 128), h * HD : (h + 1) * HD] = mean[
                h * 128 : (h + 1) * 128, :
            ].astype(BF)

    attend(0)
    attend(1)
    attend(2)
    arrive(Gather.share, GATE, UP)
    arrive(Gather.finish, OUT)
    r.proj[...] = nn(r.att[...], w[OUT][...].reshape(H * HD, D))

    def residual(rows, i, kept):
        value = r.proj[rows, :]
        hidden = r.x_ext[pl.ds(pl.multiple_of(BEHIND + i * 128, 128), 128), :].astype(F32)
        hidden = hidden + value * inverse_rms(value) * gain[G_ATT]
        r.hidden[rows, :] = hidden
        r.second[rows, :] = (hidden * inverse_rms(hidden) * gain[G_PRE]).astype(BF)
        return kept

    chunks(3, residual)

    def widen(step, kept):
        x, part = ((own_x + step // 2) % 4, step % 2)
        inner = pl.ds(pl.multiple_of(part * 256, 256), 256)
        columns = pl.ds(pl.multiple_of(x * 512 + part * 256, 256), 256)
        gate = nn(r.second[...], w[GATE][x, :, inner])
        up = nn(r.second[...], w[UP][x, :, inner])
        square = gate * gate
        bend = jnp.tanh(gate * (0.7978845608028654 + 0.7978845608028654 * 0.044715 * square))
        half = 0.5 + 0.5 * bend
        gelu = gate * half
        slope = half + (0.5 * gate) * (1.0 - bend * bend) * (
            0.7978845608028654 + 3.0 * 0.7978845608028654 * 0.044715 * square
        )
        r.activ[:, columns] = (gelu * up).astype(BF)
        r.d_gate[:, columns] = (slope * up).astype(BF)
        r.d_up[:, columns] = gelu.astype(BF)
        return kept

    lax.fori_loop(0, 2, widen, 0)
    arrive(Gather.finish, GATE, UP)
    arrive(Gather.share, DOWN)
    lax.fori_loop(2, 8, widen, 0)
    arrive(Gather.finish, DOWN)
    r.wide[...] = nn(r.activ[...], w[DOWN][...].reshape(2048, D))
    fill_cot.wait()

    def finish_forward(rows, i, kept):
        value = r.wide[rows, :]
        ended = r.hidden[rows, :] + value * inverse_rms(value) * gain[G_POST]
        r.out_low[rows, :] = ended.astype(BF)
        back, d_gain = rms_back(value, gain[G_POST], r.cot[rows, :].astype(F32))
        r.low[rows, :] = back.astype(BF)
        return kept + d_gain

    none = jnp.zeros((1, D), F32)
    put_gain(G_POST, chunks(3, finish_forward, none))
    net.drain()

    sums = [
        Reduce(net, k, r.g_qkv if k == QKV else w[k], pieces[k][0], pieces[k][1:], r.totals[k])
        for k in range(5)
    ]

    def reduce(step, *which):
        for name in which:
            step(sums[name])

    def paired(name, i):
        sums[name].pair((own_x + 1 + i) % 4)
        if i < 3:
            sums[name].along_x(i + 1)

    for i in range(4):
        x = (own_x + 1 + i) % 4
        columns = pl.ds(pl.multiple_of(x * 512, 512), 512)
        d_act = nt(r.low[...], w[DOWN][x]).astype(BF)
        r.d_gate[:, columns] = d_act * r.d_gate[:, columns]
        r.d_up[:, columns] = d_act * r.d_up[:, columns]
        w[DOWN][x] = nn(r.activ[:, columns].T, r.low[...]).astype(BF)
        sums[DOWN].start(x)
        if i:
            paired(DOWN, i - 1)
    r.flip[:, 0:TOK] = r.second[...].T
    for i in range(4):
        x = (own_x + 1 + i) % 4
        columns = pl.ds(pl.multiple_of(x * 512, 512), 512)
        d_gate, d_up = (r.d_gate[:, columns], r.d_up[:, columns])
        both = nt(d_gate, w[GATE][x]) + nt(d_up, w[UP][x])
        r.wide[...] = both + r.wide[...] if i else both
        w[GATE][x] = nn(r.flip[:, 0:TOK], d_gate).astype(BF)
        sums[GATE].start(x)
        w[UP][x] = nn(r.flip[:, 0:TOK], d_up).astype(BF)
        sums[UP].start(x)
        if i:
            paired(GATE, i - 1)
            paired(UP, i - 1)
        else:
            paired(DOWN, 3)

    def to_hidden(rows, i, kept):
        d_pre, d_att = kept
        back, d_gain = rms_back(r.hidden[rows, :], gain[G_PRE], r.wide[rows, :])
        back = back + r.cot[rows, :].astype(F32)
        r.wide[rows, :] = back
        back, d_gain_att = rms_back(r.proj[rows, :], gain[G_ATT], back)
        r.low[rows, :] = back.astype(BF)
        return d_pre + d_gain, d_att + d_gain_att

    d_pre, d_att = chunks(3, to_hidden, (none, none))
    put_gain(G_PRE, d_pre)
    put_gain(G_ATT, d_att)
    paired(GATE, 3)
    paired(UP, 3)
    for i in range(4):
        h = (own_x + 1 + i) % 4
        columns = pl.ds(pl.multiple_of(h * HD, HD), HD)
        rows = pl.ds(pl.multiple_of(h * 128, 128), 128)
        d_head = nt(r.low[...], w[OUT][h])
        for b in range(3):
            r.d_att[b, rows, :] = (
                d_head[b * 128 : (b + 1) * 128, :] * r.inverse[b, rows, :]
            ).astype(BF)
        w[OUT][h] = nn(r.att[:, columns].T, r.low[...]).astype(BF)
        sums[OUT].start(h)
        if i:
            paired(OUT, i - 1)
    r.moments[0] = jnp.zeros((640, 2 * HD), F32)
    r.moments[1, 0:256, :] = jnp.zeros((256, 2 * HD), F32)

    def attend_back(b, d_q):
        window = pl.ds(b * 128, KEYS)
        at = pl.ds(b * 128, 128)
        r.scores[...] = nt(r.d_att[b], r.v_ext[window, :])
        for h in range(H):
            rows = pl.ds(h * 128, 128)
            both = r.d_att[b, rows, :].astype(F32) * r.att[at, h * HD : (h + 1) * HD].astype(F32)
            delta = jnp.sum(both, axis=1, keepdims=True)
            r.d_scores[rows, :] = r.exps[b, rows, :] * (r.scores[rows, :] - delta).astype(BF)
        d_keys = nn(r.d_scores[...].T, r.q_rot[b])
        d_values = nn(r.exps[b].T, r.d_att[b])
        here = KEYS - b * 128
        r.moments[0, b * 128 :, 0:HD] += d_keys[0:here]
        r.moments[0, b * 128 :, HD:] += d_values[0:here]
        if b:
            r.moments[1, 0 : b * 128, 0:HD] += d_keys[here:]
            r.moments[1, 0 : b * 128, HD:] += d_values[here:]
        d_query = nn(r.d_scores[...], r.k_ext[window, :]) * HD**-0.5
        for h in range(H):
            back = turn_back(d_query[h * 128 : (h + 1) * 128, :], *own_turn(b))
            value = r.mixed[at, h * HD : (h + 1) * HD].astype(F32)
            back, d_gain = rms_back(value, gain[G_Q], back)
            r.activ[at, h * HD : (h + 1) * HD] = back.astype(BF)
            d_q = d_q + d_gain
        return d_q

    d_q = attend_back(0, jnp.zeros((1, HD), F32))
    paired(OUT, 3)
    reduce(Reduce.after_first, DOWN)
    d_q = attend_back(1, d_q)
    r.flip[...] = r.normed[...].T
    d_q = attend_back(2, d_q)
    put_gain(G_Q, d_q)
    reduce(Reduce.after_first, GATE, UP)

    def keys_back(rows, i, d_k):
        both = r.moments[held(i)]
        back = turn_back(both[:, :HD], r.cos[rows, :], r.sin[rows, :])
        back, d_gain = rms_back(r.k_raw[rows, :].astype(F32), gain[G_K], back)
        r.normed[rows, 0:HD] = back.astype(BF)
        r.normed[rows, HD : 2 * HD] = both[:, HD:].astype(BF)
        return d_k + d_gain

    put_gain(G_K, chunks(7, keys_back, jnp.zeros((1, HD), F32)))
    fetched = [local(state, r.moments.at[k]) for k, state in enumerate(r.states)]
    back_two = net.send(r.normed.at[pl.ds(0, 128), pl.ds(0, 2 * HD)], r.halo_two, "seq", -2)
    back_one = net.send(r.normed.at[pl.ds(128, TOK), pl.ds(0, 2 * HD)], r.halo_one, "seq", -1)
    flip_own = r.flip[:, BEHIND:]
    for x in range(4):
        if x < 2:
            r.g_qkv[x] = nn(flip_own, r.activ[:, x * 384 : (x + 1) * 384]).astype(BF)
        elif x == 2:
            r.g_qkv[x, :, 0:256] = nn(flip_own, r.activ[:, 768:1024]).astype(BF)
            r.g_qkv[x, :, 256:384] = nn(r.flip[...], r.normed[:, 0:128]).astype(BF)
        else:
            r.g_qkv[x] = nn(r.flip[...], r.normed[:, 128:512]).astype(BF)
        sums[QKV].start(x)
        if x:
            sums[QKV].pair(x - 1)
    sums[QKV].pair(3)
    for j in PEERS:
        sums[QKV].along_x(j)
    reduce(Reduce.after_first, OUT)
    reduce(Reduce.after_second, DOWN)
    back_two.arrived()
    back_one.arrived()
    r.activ[:, 1024:1536] = r.normed[BEHIND:, 0 : 2 * HD] + r.halo_one[...]
    last = pl.ds(256, 128)
    r.activ[last, 1024:1536] = r.activ[last, 1024:1536] + r.halo_two[...]
    r.proj[...] = (
        nt(r.activ[:, 0:384], w[QKV][0])
        + nt(r.activ[:, 384:768], w[QKV][1])
        + nt(r.activ[:, 768:1152], w[QKV][2])
        + nt(r.activ[:, 1152:1536], w[QKV][3])
    )

    def to_input(rows, i, kept):
        value = r.x_ext[pl.ds(pl.multiple_of(BEHIND + i * 128, 128), 128), :].astype(F32)
        back, d_gain = rms_back(value, gain[G_IN], r.proj[rows, :])
        r.wide[rows, :] += back
        return kept + d_gain

    put_gain(G_IN, chunks(3, to_input, none))
    gains = ReduceGains(net, r.gain_got)
    gains.start(r.gain_grad[...])

    reduce(Reduce.after_first, QKV)
    reduce(Reduce.after_second, GATE, UP, OUT)
    reduce(Reduce.after_third, DOWN)
    gains.step(0)
    reduce(Reduce.after_second, QKV)
    reduce(Reduce.after_third, GATE, UP, OUT)
    reduce(Reduce.share, DOWN)
    gains.step(1)
    reduce(Reduce.after_third, QKV)
    reduce(Reduce.share, GATE, UP, OUT)
    gains.step(2)
    reduce(Reduce.share, QKV)
    r.s_gains[...] = gains.step(3)
    reduce(Reduce.finish, DOWN, GATE, UP, OUT, QKV)
    net.drain()
    for copy in fetched:
        copy.wait()


def run_block(tokens, cotangent, segment, masters, gains, moments):
    vmem, anywhere = (pl.BlockSpec(memory_space=pltpu.VMEM), pl.BlockSpec(memory_space=pl.ANY))
    freqs = (ROPE_BASE ** (-np.arange(128) * 2.0 / HD)).astype(np.float32).reshape(1, 128)
    block_output, input_grad, gain_sums, moments, *rest = pl.pallas_call(
        block_kernel,
        out_shape=[pltpu.VMEM((TOK, D), BF), pltpu.VMEM((TOK, D), F32), pltpu.VMEM((4, 8, 128), F32)]
        + [pltpu.VMEM((4, 640, 512), F32)]
        + [pltpu.VMEM(shape, BF) for shape in SHARD]
        + [pltpu.VMEM(shape, F32) for shape in SHARD],
        in_specs=[anywhere, anywhere, vmem, vmem, vmem] + [anywhere] * 9,
        out_specs=[vmem] * 14,
        scratch_shapes=[pltpu.VMEM((4,) + shape, BF) for shape in SHARD]
        + [pltpu.VMEM(shape, kind) for _, shape, kind in SCRATCH]
        + reduce_scratch()
        + [
            pltpu.SemaphoreType.DMA((COPIES,)),
            pltpu.SemaphoreType.DMA((COPIES,)),
            pltpu.SemaphoreType.DMA((LOADS,)),
        ],
        compiler_params=pltpu.CompilerParams(
            collective_id=0, has_side_effects=True, vmem_limit_bytes=BLOCK_BYTES
        ),
        name="block",
    )(
        tokens,
        cotangent,
        segment.reshape(3, 128),
        gains.reshape(6, 128),
        jnp.asarray(freqs),
        *masters,
        *moments,
    )
    return block_output, input_grad, rest[:5], rest[5:], gain_sums, moments


def reciprocal(value):
    guess = pl.reciprocal(value, approx=True)
    return guess * (2.0 - value * guess)


def adamw(weight, gradient, first, second, rate, decay):
    first_new = ADAM_ONE * first + (1.0 - ADAM_ONE) * gradient
    second_new = ADAM_TWO * second + (1.0 - ADAM_TWO) * (gradient * gradient)
    second_hat = second_new * (1.0 / (1.0 - ADAM_TWO**STEP))
    root = second_hat * lax.rsqrt(second_hat)
    step = (first_new * (rate / (1.0 - ADAM_ONE**STEP))) * reciprocal(root + ADAM_EPS)
    weight_new = weight * (1.0 - rate * decay) - step
    return (weight_new, first_new, second_new)


CHUNKS = 4
FETCHED = (QKV, OUT, DOWN)


def update_kernel(*refs):
    taken = iter(refs)
    take = lambda count: [next(taken) for _ in range(count)]
    states, weights, gradients = ({k: take(2) for k in FETCHED}, take(5), take(5))
    gain_states, gain_sums, done, moments = (take(3), next(taken), take(2), next(taken))
    results, fresh, gain_fresh = (take(2), [take(3) for _ in SHARD], take(3))
    held, weight_new = (take(5), take(5))
    in_sems, out_sems, done_sems = take(3)

    def part(k, chunk):
        count = SHARD[k][0] // CHUNKS
        return pl.ds(chunk * count, count)

    for k in FETCHED:
        for chunk in range(CHUNKS):
            rows = part(k, chunk)
            for p in range(2):
                pltpu.make_async_copy(
                    states[k][p].at[rows], held[k].at[p, rows], in_sems.at[k, chunk]
                ).start()
    passed = [pltpu.make_async_copy(done[p], results[p], done_sems.at[p]) for p in range(2)]
    for copy in passed:
        copy.start()
    own = gain_sums[lax.axis_index("wsh"), 0:6]
    for ref, value in zip(
        gain_fresh, adamw(gain_states[0][...], own, gain_states[1][...], gain_states[2][...], GAIN_RATE, 0.0)
    ):
        ref[...] = value
    for k in (GATE, UP) + FETCHED:
        for chunk in range(CHUNKS):
            rows = part(k, chunk)
            if k in FETCHED:
                whole = held[k].at[:, rows]
                pltpu.make_async_copy(whole, whole, in_sems.at[k, chunk]).wait()
                state = [held[k][p, rows, :] for p in range(2)]
            else:
                state = [moments[2 * (k - GATE) + p, rows, :] for p in range(2)]
            gradient = gradients[k][rows, :].astype(F32)
            values = adamw(
                weights[k][rows, :], gradient, state[0], state[1], MATRIX_RATE, MATRIX_DECAY
            )
            weight_new[k][rows, :] = values[0]
            held[k][0, rows, :] = values[1]
            held[k][1, rows, :] = values[2]
            for p, source in enumerate((weight_new[k].at[rows], held[k].at[0, rows], held[k].at[1, rows])):
                pltpu.make_async_copy(source, fresh[k][p].at[rows], out_sems.at[k, p]).start()
    for k in range(5):
        for p in range(3):
            whole = weight_new[k]
            pltpu.make_async_copy(whole, whole, out_sems.at[k, p]).wait()
    for copy in passed:
        copy.wait()


def update(states, weights, gradients, gain_states, gain_sums, done, moments):
    vmem, hbm = (pl.BlockSpec(memory_space=pltpu.VMEM), pl.BlockSpec(memory_space=pltpu.HBM))
    here = [
        pltpu.with_memory_space_constraint(a, pltpu.VMEM)
        for a in (*weights, *gradients, gain_sums, *done, moments)
    ]
    there = [pltpu.with_memory_space_constraint(a, pltpu.HBM) for state in states for a in state]
    got = pl.pallas_call(
        update_kernel,
        out_shape=[jax.ShapeDtypeStruct(a.shape, a.dtype) for a in done]
        + [jax.ShapeDtypeStruct(shape, F32) for shape in SHARD for _ in range(3)]
        + [jax.ShapeDtypeStruct((6, 128), F32)] * 3,
        in_specs=[hbm] * 6 + [vmem] * 17,
        out_specs=[hbm] * 17 + [vmem] * 3,
        scratch_shapes=[pltpu.VMEM((2,) + shape, F32) for shape in SHARD]
        + [pltpu.VMEM(shape, F32) for shape in SHARD]
        + [
            pltpu.SemaphoreType.DMA((5, CHUNKS)),
            pltpu.SemaphoreType.DMA((5, 3)),
            pltpu.SemaphoreType.DMA((2,)),
        ],
        compiler_params=pltpu.CompilerParams(vmem_limit_bytes=UPDATE_BYTES),
        name="update",
    )(*there, *here[:10], *gain_states, *here[10:])
    return tuple(got[:17]) + tuple(a.reshape(768) for a in got[17:])


def on_device(
    tokens,
    cotangent,
    segment,
    qkv_weight,
    out_weight,
    gate_weight,
    up_weight,
    down_weight,
    gains,
    qkv_first,
    qkv_second,
    out_first,
    out_second,
    gate_first,
    gate_second,
    up_first,
    up_second,
    down_first,
    down_second,
    gain_first,
    gain_second,
):
    masters = (qkv_weight, out_weight, gate_weight, up_weight, down_weight)
    block_output, input_grad, sums, fulls, gain_sums, moments = run_block(
        tokens, cotangent, segment, masters, gains, (gate_first, gate_second, up_first, up_second)
    )
    states = (
        (qkv_first, qkv_second),
        (out_first, out_second),
        (down_first, down_second),
    )
    gain_states = [a.reshape(6, 128) for a in (gains, gain_first, gain_second)]
    return update(states, fulls, sums, gain_states, gain_sums, (block_output, input_grad), moments)


def solution(mesh):
    placed = (
        P(("wsh", "seq"), None),
        P(("wsh", "seq"), None),
        P(("wsh", "seq")),
        P(None, "wsh"),
        P("wsh", None),
        P(None, "wsh"),
        P(None, "wsh"),
        P("wsh", None),
        P("wsh"),
        P(None, "wsh"),
        P(None, "wsh"),
        P("wsh", None),
        P("wsh", None),
        P(None, "wsh"),
        P(None, "wsh"),
        P(None, "wsh"),
        P(None, "wsh"),
        P("wsh", None),
        P("wsh", None),
        P("wsh"),
        P("wsh"),
    )
    return jax.shard_map(
        on_device,
        mesh=mesh,
        in_specs=placed,
        out_specs=(
            P(("wsh", "seq"), None),
            P(("wsh", "seq"), None),
            P(None, "wsh"),
            P(None, "wsh"),
            P(None, "wsh"),
            P("wsh", None),
            P("wsh", None),
            P("wsh", None),
            P(None, "wsh"),
            P(None, "wsh"),
            P(None, "wsh"),
            P(None, "wsh"),
            P(None, "wsh"),
            P(None, "wsh"),
            P("wsh", None),
            P("wsh", None),
            P("wsh", None),
            P("wsh"),
            P("wsh"),
            P("wsh"),
        ),
        check_vma=False,
    )
```

```python
import types

import jax
import jax.numpy as jnp
import numpy as np
from jax import lax
from jax.experimental import pallas as pl
from jax.experimental.pallas import tpu as pltpu
from jax.sharding import PartitionSpec as P

D = 640
H = 4
HD = 256
WIN = 512
STEP = 10


EPS = 1e-06
ADAM_ONE = 0.9
ADAM_TWO = 0.999
ADAM_EPS = 1e-08
MATRIX_DECAY = 0.1
MATRIX_RATE = 0.05
GAIN_RATE = 0.8
ROPE_BASE = 10000.0


BLOCK_BYTES, UPDATE_BYTES = (47 * 2**20, 24 * 2**20)
BF, F32 = (jnp.bfloat16, jnp.float32)
MESH = pl.DeviceIdType.MESH
AXES = 4
QKV, OUT, GATE, UP, DOWN = range(5)
SHARD = ((640, 384), (256, 640), (640, 512), (640, 512), (512, 640))
GATHERED = (
    ((0, 128, "y"), (128, 256, "z")),
    ((0, 640, ""),),
    ((0, 256, "y"), (256, 256, "z")),
    ((0, 256, "y"), (256, 256, "z")),
    ((0, 384, "y"), (384, 256, "z")),
)
REDUCED = (
    ((0, 128, "y", "y"), (128, 128, "z", "z"), (256, 128, "y", "x")),
    ((0, 128, "y", "y"), (128, 256, "z", "z"), (384, 256, "y", "x")),
    ((0, 256, "y", "y"), (256, 128, "z", "z"), (384, 128, "z", "x")),
    ((0, 128, "y", "y"), (128, 256, "z", "z"), (384, 128, "y", "x")),
    ((0, 256, "y", "y"), (256, 128, "z", "z"), (384, 256, "z", "x")),
)
OTHER = {"y": "z", "z": "y"}
PEERS = (1, 2, 3)


class Net:
    def __init__(self, send_sems, recv_sems):
        token = lax.axis_index("seq")
        self.at = {"x": lax.axis_index("wsh"), "y": (token // 2) % 4, "z": token // 8, "c": token % 2}
        self.send_sems, self.recv_sems, self.count, self.started = (send_sems, recv_sems, 0, [])

    def peer(self, axis, by):
        size = 2 if axis == "c" else AXES
        return (self.at[axis] + by) % size

    def device(self, axis, by):
        if axis == "seq":
            return ((lax.axis_index("seq") + by) % 32, self.at["x"])
        at = dict(self.at)
        if isinstance(by, tuple):
            by, at["c"] = (by[0], 1 - at["c"])
        at[axis] = self.peer(axis, by)
        return ((at["z"] * 4 + at["y"]) * 2 + at["c"], at["x"])

    def greet(self):
        barrier = pltpu.get_barrier_semaphore()
        peers = [(axis, by) for axis in "xyz" for by in PEERS] + [("c", 1)]
        peers += [(axis, (by, 1)) for axis in "yz" for by in PEERS]
        peers += [("seq", by) for by in (1, 2, -1, -2)]
        for axis, by in peers:
            pl.semaphore_signal(
                barrier, inc=1, device_id=self.device(axis, by), device_id_type=MESH
            )
        pl.semaphore_wait(barrier, len(peers))

    def batch(self, size):
        made = Batch(self, size, self.send_sems.at[self.count], self.recv_sems.at[self.count])
        self.count += 1
        self.started.append(made)
        return made

    def send(self, src, dst, axis, by):
        return self.batch(src).add(src, dst, axis, by)

    def drain(self):
        for made in self.started:
            pltpu.make_async_copy(made.size, made.size, made.send_sem).wait()
        self.started = []


class Batch:
    def __init__(self, net, size, send_sem, recv_sem):
        self.net, self.size, self.send_sem, self.recv_sem = (net, size, send_sem, recv_sem)

    def add(self, src, dst, axis, by):
        pltpu.make_async_remote_copy(
            src_ref=src,
            dst_ref=dst,
            send_sem=self.send_sem,
            recv_sem=self.recv_sem,
            device_id=self.net.device(axis, by),
            device_id_type=MESH,
        ).start()
        return self

    def arrived(self):
        pltpu.make_async_copy(self.size, self.size, self.recv_sem).wait()


class Gather:
    def __init__(self, net, weight, full):
        self.net, self.full, (self.rows, _), self.parts = (
            net,
            full,
            SHARD[weight],
            GATHERED[weight],
        )
        self.eighth, self.direct = (self.rows // 8, not self.parts[0][2])

    def block(self, x, part):
        first, width, axis = part
        at, count = (net_half(self.net, self.rows), self.rows // 2)
        if axis:
            at, count = (at + self.net.at[axis] * self.eighth, self.eighth)
        return self.full.at[x, pl.ds(pl.multiple_of(at, 16), count), pl.ds(first, width)]

    def start(self):
        each = self.rows // 2 if self.direct else self.eighth
        self.along_x = self.net.batch(self.full.at[0:3, pl.ds(0, each), :])
        for part in self.parts:
            mine = self.block(self.net.at["x"], part)
            for j in PEERS:
                self.along_x.add(mine, mine, "x", j)

    def spread(self):
        self.along_x.arrived()
        self.along_q = self.net.batch(self.full.at[0:3, pl.ds(0, 3 * self.eighth), :])
        for j in PEERS:
            for part in self.parts:
                got = self.block(self.net.peer("x", -j), part)
                for k in PEERS:
                    self.along_q.add(got, got, part[2], k)

    def share(self):
        (self.along_x if self.direct else self.along_q).arrived()
        half = self.rows // 2
        self.to_core = self.net.batch(self.full.at[0:3, pl.ds(0, half), :])
        for j in PEERS:
            got = self.full.at[self.net.peer("x", -j), pl.ds(net_half(self.net, self.rows), half), :]
            self.to_core.add(got, got, "c", 1)

    def finish(self):
        self.to_core.arrived()


def net_half(net, rows):
    return pl.multiple_of(net.at["c"] * (rows // 2), 16)


class Reduce:
    def __init__(self, net, weight, grad, core_got, got, total):
        self.net, self.grad, self.core_got, self.total = (net, grad, core_got, total)
        self.rows, self.columns = SHARD[weight]
        self.parts = [
            (pl.ds(first, width), axis, order, got[3 * k : 3 * k + 3])
            for k, (first, width, axis, order) in enumerate(REDUCED[weight])
        ]
        self.half, self.eighth = (self.rows // 2, self.rows // 8)
        self.half_start = net_half(net, self.rows)
        self.core, self.firsts = ([], None)
        self.merged = weight == QKV

    def block(self, q):
        return pl.ds(pl.multiple_of(self.half_start + q * self.eighth, 16), self.eighth)

    def start(self, x):
        there = pl.multiple_of((1 - self.net.at["c"]) * self.half, 16)
        mine = self.grad.at[x, pl.ds(there, self.half), :]
        self.core.append(self.net.batch(mine).add(mine, self.core_got.at[x], "c", 1))

    def pair(self, x):
        self.core.pop(0).arrived()

        def add(block, carry):
            local = pl.ds(pl.multiple_of(block * self.eighth, 16), self.eighth)
            rows = self.block(block)
            self.grad[x, rows, :] = self.grad[x, rows, :] + self.core_got[x, local, :]
            return carry

        lax.fori_loop(0, 4, add, 0)
        if self.firsts is None:
            self.firsts = self.net.batch(self.grad.at[0:3, pl.ds(0, self.half), :])
        for columns, axis, order, got in self.parts:
            if order != "x":
                for j in PEERS:
                    src = self.grad.at[x, self.block(self.net.peer(axis, j)), columns]
                    self.firsts.add(src, got[0].at[j - 1, x], order, j)

    def along_x(self, j):
        for columns, axis, order, got in self.parts:
            if order == "x":
                rows = pl.ds(self.half_start, self.half)
                src = self.grad.at[self.net.peer("x", j), rows, columns]
                self.firsts.add(src, got[0].at[j - 1], order, j)

    def after_first(self):
        self.firsts.arrived()
        self.seconds = self.net.batch(self.grad.at[0, pl.ds(0, 3 * self.eighth), :])
        for columns, axis, order, got in self.parts:
            own = self.net.at[axis]

            def add(step, carry):
                if order == "x":
                    x, rows = (self.net.at["x"], self.block(step))
                    local = pl.ds(pl.multiple_of(step * self.eighth, 16), self.eighth)
                    pieces = [got[0][j, local, :] for j in range(3)]
                else:
                    x, rows = (step, self.block(own))
                    pieces = [got[0][j, step] for j in range(3)]
                total = self.grad[x, rows, columns].astype(F32)
                for piece in pieces:
                    total = total + piece.astype(F32)
                self.grad[x, rows, columns] = total.astype(BF)
                return carry

            lax.fori_loop(0, 4, add, 0)
            for j in PEERS:
                if order == "x":
                    x, q, along = (self.net.at["x"], self.net.peer(axis, j), axis)
                else:
                    x, q, along = (self.net.peer("x", j), own, "x")
                src = self.grad.at[x, self.block(q), columns]
                self.seconds.add(src, got[1].at[j - 1], along, j)

    def after_second(self):
        self.seconds.arrived()
        self.thirds = self.net.batch(self.grad.at[0, pl.ds(0, 3 * self.eighth), :])
        for columns, axis, order, got in self.parts:
            rows = self.block(self.net.at[axis])
            total = self.grad[self.net.at["x"], rows, columns].astype(F32)
            for j in range(3):
                total = total + got[1][j].astype(F32)
            mine = got[2].at[self.net.at[OTHER[axis]]]
            mine[...] = total.astype(BF)
            for j in PEERS:
                self.thirds.add(mine, mine, OTHER[axis], j)

    def after_third(self):
        self.thirds.arrived()
        count = 7 if self.merged else 3
        self.fourths = self.net.batch(self.grad.at[0, pl.ds(0, count * self.eighth), :])
        for columns, axis, order, got in self.parts:
            total = got[2][0].astype(F32)
            for j in PEERS:
                total = total + got[2][j].astype(F32)
            mine = self.total.at[self.block(self.net.at[axis]), columns]
            mine[...] = total.astype(BF)
            for j in PEERS:
                self.fourths.add(mine, mine, axis, j)
                if self.merged:
                    self.fourths.add(mine, mine, axis, (j, 1))
            if self.merged:
                self.fourths.add(mine, mine, "c", 1)

    def share(self):
        self.fourths.arrived()
        if self.merged:
            return
        mine = self.total.at[pl.ds(self.half_start, self.half), :]
        self.fifth = self.net.batch(mine).add(mine, mine, "c", 1)

    def finish(self):
        if not self.merged:
            self.fifth.arrived()


class ReduceGains:
    def __init__(self, net, got):
        self.net, self.got = (net, got)

    def start(self, value):
        self.post(0, value)

    def post(self, stage, value):
        axis, peers = ("cxyz"[stage], PEERS if stage else (1,))
        mine = self.got.at[stage, self.net.at[axis]]
        mine[...] = value
        self.copies = self.net.batch(self.got.at[0, 0 : len(peers)])
        for j in peers:
            self.copies.add(mine, mine, axis, j)

    def step(self, stage):
        self.copies.arrived()
        total = self.got[stage, 0] + self.got[stage, 1]
        if stage:
            total = total + self.got[stage, 2] + self.got[stage, 3]
        if stage < 3:
            self.post(stage + 1, total)
        return total


def reduce_scratch():
    shapes = []
    for (rows, columns), parts in zip(SHARD, REDUCED):
        shapes.append((4, rows // 2, columns))
        for _, width, _, order in parts:
            shapes += [
                (3, rows // 2, width) if order == "x" else (3, 4, rows // 8, width),
                (3, rows // 8, width),
                (4, rows // 8, width),
            ]
    return [pltpu.VMEM(shape, BF) for shape in shapes]


TOK = 384
BEHIND = 512
KEYS = 640
G_IN, G_ATT, G_PRE, G_POST, G_Q, G_K = range(6)
NORM_ROWS = ((0, 5), (5, 5), (10, 5), (15, 5), (20, 2), (22, 2))

SCRATCH = (
    ("g_qkv", (4,) + SHARD[QKV], BF),
    ("x_ext", (BEHIND + TOK, D), BF),
    ("normed", (BEHIND + TOK, D), BF),
    ("cos", (BEHIND + TOK, 128), F32),
    ("sin", (BEHIND + TOK, 128), F32),
    ("mixed", (TOK, 1024), BF),
    ("k_raw", (BEHIND + TOK, HD), BF),
    ("q_rot", (3, 512, HD), BF),
    ("k_ext", (BEHIND + TOK, HD), BF),
    ("v_ext", (BEHIND + TOK, HD), BF),
    ("exps", (3, 512, KEYS), BF),
    ("inverse", (3, 512, 1), F32),
    ("att", (TOK, H * HD), BF),
    ("hidden", (TOK, D), F32),
    ("second", (TOK, D), BF),
    ("flip", (D, BEHIND + TOK), BF),
    ("activ", (TOK, 2048), BF),
    ("d_gate", (TOK, 2048), BF),
    ("d_up", (TOK, 2048), BF),
    ("low", (TOK, D), BF),
    ("cot", (TOK, D), BF),
    ("d_att", (3, 512, HD), BF),
    ("d_scores", (512, KEYS), BF),
    ("halo_one", (TOK, 2 * HD), BF),
    ("halo_two", (128, 2 * HD), BF),
    ("gain_all", (4, 8, 128), F32),
    ("gain_grad", (4, 8, 128), F32),
    ("gain_got", (4, 4, 4, 8, 128), F32),
    ("ids", (8, 128), jnp.int32),
    ("ids_one", (8, 128), jnp.int32),
    ("ids_two", (8, 128), jnp.int32),
)
COPIES = 5 * 3 - 1 + 5 * 9 + 6 + 5
LOADS = 14


def nt(a, b):
    return lax.dot_general(a, b, (((1,), (1,)), ((), ())), preferred_element_type=F32)


def nn(a, b):
    return jnp.dot(a, b, preferred_element_type=F32)


def inverse_rms(value):
    return lax.rsqrt(jnp.mean(value * value, axis=-1, keepdims=True) + EPS)


def rms_back(value, gain, grad):
    scale = inverse_rms(value)
    unit = value * scale
    weighted = grad * gain
    back = scale * (weighted - unit * jnp.mean(weighted * unit, axis=-1, keepdims=True))
    return back, jnp.sum(grad * unit, axis=0, keepdims=True)


def turn(value, cosine, sine):
    first, last = (value[:, :128], value[:, 128:])
    return jnp.concatenate([first * cosine - last * sine, last * cosine + first * sine], axis=1)


def turn_back(grad, cosine, sine):
    first, last = (grad[:, :128], grad[:, 128:])
    return jnp.concatenate([first * cosine + last * sine, last * cosine - first * sine], axis=1)


def block_kernel(*refs):
    taken = iter(refs)
    r, take = (types.SimpleNamespace(), lambda count: [next(taken) for _ in range(count)])
    r.tokens, r.cotangent, r.segment, r.gains, r.freqs = take(5)
    r.masters, r.states = (take(5), take(6))
    r.out_low, r.wide, r.s_gains, r.moments, r.tall = take(5)
    r.totals, r.fulls, w = (take(5), take(5), take(5))
    for name, _, _ in SCRATCH:
        setattr(r, name, next(taken))
    pieces = [take(1 + 3 * len(parts)) for parts in REDUCED]
    send_sems, recv_sems, load_sems = take(3)
    net = Net(send_sems, recv_sems)
    own_x = net.at["x"]
    base = lax.axis_index("seq") * TOK
    loads = []

    def local(src, dst):
        copy = pltpu.make_async_copy(src, dst, load_sems.at[len(loads)])
        loads.append(copy)
        copy.start()
        return copy

    def chunks(count, body, carry=0):
        return lax.fori_loop(
            0, count, lambda i, kept: body(pl.ds(pl.multiple_of(i * 128, 128), 128), i, kept), carry
        )

    own_rows = pl.ds(BEHIND, TOK)
    fill = {QKV: local(r.masters[QKV], r.fulls[QKV])}
    fill_tokens = local(r.tokens, r.x_ext.at[own_rows])
    for name in (OUT, GATE, UP, DOWN):
        fill[name] = local(r.masters[name], r.fulls[name])
    fill_cot = local(r.cotangent, r.cot)
    r.gain_all[...] = jnp.zeros((4, 8, 128), F32)
    r.gain_grad[...] = jnp.zeros((4, 8, 128), F32)
    r.gain_all[own_x, 0:6] = r.gains[...].astype(BF).astype(F32)
    r.ids[...] = jnp.zeros((8, 128), jnp.int32)
    r.ids[0:3] = r.segment[...]
    net.greet()

    mine = r.gain_all.at[own_x]
    gain_copies = net.batch(r.gain_all.at[0:3])
    for j in PEERS:
        gain_copies.add(mine, mine, "x", j)
    parts = [Gather(net, name, w[name]) for name in range(5)]

    def launch(name):
        fill[name].wait()
        rows = SHARD[name][0] // 8

        def cast(step, carry):
            at = pl.ds(pl.multiple_of(step * rows, 16), rows)
            w[name][own_x, at, :] = r.fulls[name][at, :].astype(BF)
            return carry

        lax.fori_loop(0, 8, cast, 0)
        parts[name].start()

    def arrive(step, *which):
        for name in which:
            step(parts[name])

    launch(QKV)
    fill_tokens.wait()
    halo_copies = [
        net.send(r.x_ext.at[own_rows], r.x_ext.at[pl.ds(128, TOK)], "seq", 1),
        net.send(r.x_ext.at[pl.ds(BEHIND + 256, 128)], r.x_ext.at[pl.ds(0, 128)], "seq", 2),
        net.send(r.ids, r.ids_one, "seq", 1),
        net.send(r.ids, r.ids_two, "seq", 2),
    ]

    def angles(rows, i, kept):
        place = (base - BEHIND + i * 128 + lax.broadcasted_iota(jnp.int32, (128, 128), 0)).astype(F32)
        angle = place * r.freqs[...]
        r.cos[rows, :] = jnp.cos(angle)
        r.sin[rows, :] = jnp.sin(angle)
        return kept

    chunks(7, angles)
    launch(GATE)
    launch(UP)
    arrive(Gather.spread, QKV, GATE, UP)
    launch(DOWN)
    launch(OUT)
    gain_copies.arrived()
    gain = {}
    for name, (first, count) in enumerate(NORM_ROWS):
        rows = [(k // 6, k % 6) for k in range(first, first + count)]
        gain[name] = jnp.concatenate([r.gain_all[g, k : k + 1, :] for g, k in rows], axis=1)

    def put_gain(name, value):
        first, count = NORM_ROWS[name]
        for k in range(count):
            g, row = ((first + k) // 6, (first + k) % 6)
            r.gain_grad[g, row : row + 1, :] = value[:, 128 * k : 128 * (k + 1)]

    for copy in halo_copies:
        copy.arrived()

    def normalise(rows, i, kept):
        value = r.x_ext[rows, :].astype(F32)
        r.normed[rows, :] = (value * inverse_rms(value) * gain[G_IN]).astype(BF)
        return kept

    chunks(7, normalise)
    arrive(Gather.share, QKV)
    arrive(Gather.finish, QKV)

    normed_own = r.normed[own_rows, :]
    for x in range(4):
        width = 384 if x < 2 else (256 if x == 2 else 0)
        if width:
            r.mixed[:, x * 384 : x * 384 + width] = nn(
                normed_own, w[QKV][x, :, :width]
            ).astype(BF)
    normed_all = r.normed[...]
    head = nn(normed_all, w[QKV][2, :, 256:384])
    tail = nn(normed_all, w[QKV][3])
    for at, rows in ((0, slice(0, 640)), (1, slice(640, 896))):
        count = rows.stop - rows.start
        r.moments[at, 0:count, 0:128] = head[rows]
        r.moments[at, 0:count, 128:256] = tail[rows, :128]
    r.k_raw[:, 0:128] = head.astype(BF)
    r.k_raw[:, 128:256] = tail[:, :128].astype(BF)
    r.v_ext[...] = tail[:, 128:].astype(BF)
    arrive(Gather.spread, DOWN)

    def held(i):
        return i // 5, pl.ds(pl.multiple_of(i % 5 * 128, 128), 128)

    def keys(rows, i, kept):
        value = r.moments[(*held(i), slice(0, 256))]
        value = value * inverse_rms(value) * gain[G_K]
        r.k_ext[rows, :] = turn(value, r.cos[rows, :], r.sin[rows, :]).astype(BF)
        return kept

    chunks(7, keys)

    def own_turn(i):
        at = pl.ds(pl.multiple_of(BEHIND + i * 128, 128), 128)
        return r.cos[at, :], r.sin[at, :]

    def queries(rows, i, kept):
        for h in range(H):
            value = r.mixed[rows, h * HD : (h + 1) * HD].astype(F32)
            value = value * inverse_rms(value) * gain[G_Q]
            r.q_rot[i, h * 128 : (h + 1) * 128, :] = (
                turn(value, *own_turn(i)) * HD**-0.5
            ).astype(BF)
        return kept

    chunks(3, queries)
    arrive(Gather.share, OUT)

    id_rows = [r.ids_two[2:3, :]] + [r.ids_one[k : k + 1, :] for k in range(3)]
    id_rows = [row.astype(F32) for row in id_rows + [r.ids[k : k + 1, :] for k in range(3)]]

    def attend(b):
        down_rows = lax.broadcasted_iota(jnp.int32, (128, 128), 0)
        across = lax.broadcasted_iota(jnp.int32, (128, 128), 1)
        own_id = jnp.broadcast_to(id_rows[4 + b], (128, 128)).T
        for j in range(5):
            allowed = jnp.broadcast_to(id_rows[b + j], (128, 128)) == own_id
            allowed = allowed & (base - BEHIND + (b + j) * 128 + across >= 0)
            if j == 0:
                allowed = allowed & (across > down_rows)
            if j == 4:
                allowed = allowed & (across <= down_rows)
            r.wide[0:128, j * 128 : (j + 1) * 128] = jnp.where(allowed, 0.0, -1e30)
        window = pl.ds(b * 128, KEYS)
        r.tall[0] = nt(r.q_rot[b], r.k_ext[window, :])
        for h in range(H):
            rows = pl.ds(h * 128, 128)
            weight = jnp.exp(r.tall[0, rows, :] + r.wide[0:128, :])
            r.inverse[b, rows, :] = 1.0 / jnp.sum(weight, axis=1, keepdims=True)
            r.exps[b, rows, :] = weight.astype(BF)
        mean = nn(r.exps[b], r.v_ext[window, :]) * r.inverse[b]
        for h in range(H):
            r.att[pl.ds(b * 128, 128), h * HD : (h + 1) * HD] = mean[
                h * 128 : (h + 1) * 128, :
            ].astype(BF)

    attend(0)
    attend(1)
    attend(2)
    arrive(Gather.share, GATE, UP)
    arrive(Gather.finish, OUT)
    r.tall[1, 0:TOK, :] = nn(r.att[...], w[OUT][...].reshape(H * HD, D))

    def residual(rows, i, kept):
        value = r.tall[1, rows, :]
        hidden = r.x_ext[pl.ds(pl.multiple_of(BEHIND + i * 128, 128), 128), :].astype(F32)
        hidden = hidden + value * inverse_rms(value) * gain[G_ATT]
        r.hidden[rows, :] = hidden
        r.second[rows, :] = (hidden * inverse_rms(hidden) * gain[G_PRE]).astype(BF)
        return kept

    chunks(3, residual)

    def widen(step, kept):
        x, part = ((own_x + step // 2) % 4, step % 2)
        inner = pl.ds(pl.multiple_of(part * 256, 256), 256)
        columns = pl.ds(pl.multiple_of(x * 512 + part * 256, 256), 256)
        gate = nn(r.second[...], w[GATE][x, :, inner])
        up = nn(r.second[...], w[UP][x, :, inner])
        square = gate * gate
        bend = jnp.tanh(gate * (0.7978845608028654 + 0.7978845608028654 * 0.044715 * square))
        half = 0.5 + 0.5 * bend
        gelu = gate * half
        slope = half + (0.5 * gate) * (1.0 - bend * bend) * (
            0.7978845608028654 + 3.0 * 0.7978845608028654 * 0.044715 * square
        )
        r.activ[:, columns] = (gelu * up).astype(BF)
        r.d_gate[:, columns] = (slope * up).astype(BF)
        r.d_up[:, columns] = gelu.astype(BF)
        return kept

    lax.fori_loop(0, 2, widen, 0)
    arrive(Gather.finish, GATE, UP)
    arrive(Gather.share, DOWN)
    lax.fori_loop(2, 8, widen, 0)
    arrive(Gather.finish, DOWN)
    r.wide[...] = nn(r.activ[...], w[DOWN][...].reshape(2048, D))
    fill_cot.wait()

    def finish_forward(rows, i, kept):
        value = r.wide[rows, :]
        ended = r.hidden[rows, :] + value * inverse_rms(value) * gain[G_POST]
        r.out_low[rows, :] = ended.astype(BF)
        back, d_gain = rms_back(value, gain[G_POST], r.cot[rows, :].astype(F32))
        r.low[rows, :] = back.astype(BF)
        return kept + d_gain

    none = jnp.zeros((1, D), F32)
    put_gain(G_POST, chunks(3, finish_forward, none))
    net.drain()

    sums = [
        Reduce(net, k, r.g_qkv if k == QKV else w[k], pieces[k][0], pieces[k][1:], r.totals[k])
        for k in range(5)
    ]

    def reduce(step, *which):
        for name in which:
            step(sums[name])

    def paired(name, i):
        sums[name].pair((own_x + 1 + i) % 4)
        if i < 3:
            sums[name].along_x(i + 1)

    for i in range(4):
        x = (own_x + 1 + i) % 4
        columns = pl.ds(pl.multiple_of(x * 512, 512), 512)
        d_act = nt(r.low[...], w[DOWN][x]).astype(BF)
        r.d_gate[:, columns] = d_act * r.d_gate[:, columns]
        r.d_up[:, columns] = d_act * r.d_up[:, columns]
        w[DOWN][x] = nn(r.activ[:, columns].T, r.low[...]).astype(BF)
        sums[DOWN].start(x)
        if i:
            paired(DOWN, i - 1)
    r.flip[:, 0:TOK] = r.second[...].T
    for i in range(4):
        x = (own_x + 1 + i) % 4
        columns = pl.ds(pl.multiple_of(x * 512, 512), 512)
        d_gate, d_up = (r.d_gate[:, columns], r.d_up[:, columns])
        both = nt(d_gate, w[GATE][x]) + nt(d_up, w[UP][x])
        r.wide[...] = both + r.wide[...] if i else both
        w[GATE][x] = nn(r.flip[:, 0:TOK], d_gate).astype(BF)
        sums[GATE].start(x)
        w[UP][x] = nn(r.flip[:, 0:TOK], d_up).astype(BF)
        sums[UP].start(x)
        if i:
            paired(GATE, i - 1)
            paired(UP, i - 1)
        else:
            paired(DOWN, 3)

    def to_hidden(rows, i, kept):
        d_pre, d_att = kept
        back, d_gain = rms_back(r.hidden[rows, :], gain[G_PRE], r.wide[rows, :])
        back = back + r.cot[rows, :].astype(F32)
        r.wide[rows, :] = back
        back, d_gain_att = rms_back(r.tall[1, rows, :], gain[G_ATT], back)
        r.low[rows, :] = back.astype(BF)
        return d_pre + d_gain, d_att + d_gain_att

    d_pre, d_att = chunks(3, to_hidden, (none, none))
    put_gain(G_PRE, d_pre)
    put_gain(G_ATT, d_att)
    paired(GATE, 3)
    paired(UP, 3)
    for i in range(4):
        h = (own_x + 1 + i) % 4
        columns = pl.ds(pl.multiple_of(h * HD, HD), HD)
        rows = pl.ds(pl.multiple_of(h * 128, 128), 128)
        d_head = nt(r.low[...], w[OUT][h])
        for b in range(3):
            r.d_att[b, rows, :] = (
                d_head[b * 128 : (b + 1) * 128, :] * r.inverse[b, rows, :]
            ).astype(BF)
        w[OUT][h] = nn(r.att[:, columns].T, r.low[...]).astype(BF)
        sums[OUT].start(h)
        if i:
            paired(OUT, i - 1)
    r.moments[0] = jnp.zeros((640, 2 * HD), F32)
    r.moments[1, 0:256, :] = jnp.zeros((256, 2 * HD), F32)

    def attend_back(b, d_q):
        window = pl.ds(b * 128, KEYS)
        at = pl.ds(b * 128, 128)
        r.tall[0] = nt(r.d_att[b], r.v_ext[window, :])
        for h in range(H):
            rows = pl.ds(h * 128, 128)
            both = r.d_att[b, rows, :].astype(F32) * r.att[at, h * HD : (h + 1) * HD].astype(F32)
            delta = jnp.sum(both, axis=1, keepdims=True)
            r.d_scores[rows, :] = r.exps[b, rows, :] * (r.tall[0, rows, :] - delta).astype(BF)
        d_keys = nn(r.d_scores[...].T, r.q_rot[b])
        d_values = nn(r.exps[b].T, r.d_att[b])
        here = KEYS - b * 128
        r.moments[0, b * 128 :, 0:HD] += d_keys[0:here]
        r.moments[0, b * 128 :, HD:] += d_values[0:here]
        if b:
            r.moments[1, 0 : b * 128, 0:HD] += d_keys[here:]
            r.moments[1, 0 : b * 128, HD:] += d_values[here:]
        d_query = nn(r.d_scores[...], r.k_ext[window, :]) * HD**-0.5
        for h in range(H):
            back = turn_back(d_query[h * 128 : (h + 1) * 128, :], *own_turn(b))
            value = r.mixed[at, h * HD : (h + 1) * HD].astype(F32)
            back, d_gain = rms_back(value, gain[G_Q], back)
            r.activ[at, h * HD : (h + 1) * HD] = back.astype(BF)
            d_q = d_q + d_gain
        return d_q

    d_q = attend_back(0, jnp.zeros((1, HD), F32))
    paired(OUT, 3)
    reduce(Reduce.after_first, DOWN)
    d_q = attend_back(1, d_q)
    r.flip[...] = r.normed[...].T
    d_q = attend_back(2, d_q)
    put_gain(G_Q, d_q)
    reduce(Reduce.after_first, GATE, UP)

    def keys_back(rows, i, d_k):
        both = r.moments[held(i)]
        back = turn_back(both[:, :HD], r.cos[rows, :], r.sin[rows, :])
        back, d_gain = rms_back(r.k_raw[rows, :].astype(F32), gain[G_K], back)
        r.normed[rows, 0:HD] = back.astype(BF)
        r.normed[rows, HD : 2 * HD] = both[:, HD:].astype(BF)
        return d_k + d_gain

    put_gain(G_K, chunks(7, keys_back, jnp.zeros((1, HD), F32)))
    fetched = [local(state, r.moments.at[k]) for k, state in enumerate(r.states[:4])]
    fetched.append(local(r.states[4], r.tall.at[0]))
    back_two = net.send(r.normed.at[pl.ds(0, 128), pl.ds(0, 2 * HD)], r.halo_two, "seq", -2)
    back_one = net.send(r.normed.at[pl.ds(128, TOK), pl.ds(0, 2 * HD)], r.halo_one, "seq", -1)
    flip_own = r.flip[:, BEHIND:]
    for x in range(4):
        if x < 2:
            r.g_qkv[x] = nn(flip_own, r.activ[:, x * 384 : (x + 1) * 384]).astype(BF)
        elif x == 2:
            r.g_qkv[x, :, 0:256] = nn(flip_own, r.activ[:, 768:1024]).astype(BF)
            r.g_qkv[x, :, 256:384] = nn(r.flip[...], r.normed[:, 0:128]).astype(BF)
        else:
            r.g_qkv[x] = nn(r.flip[...], r.normed[:, 128:512]).astype(BF)
        sums[QKV].start(x)
        if x:
            sums[QKV].pair(x - 1)
    sums[QKV].pair(3)
    for j in PEERS:
        sums[QKV].along_x(j)
    reduce(Reduce.after_first, OUT)
    reduce(Reduce.after_second, DOWN)
    back_two.arrived()
    back_one.arrived()
    r.activ[:, 1024:1536] = r.normed[BEHIND:, 0 : 2 * HD] + r.halo_one[...]
    last = pl.ds(256, 128)
    r.activ[last, 1024:1536] = r.activ[last, 1024:1536] + r.halo_two[...]
    r.tall[1, 0:TOK, :] = (
        nt(r.activ[:, 0:384], w[QKV][0])
        + nt(r.activ[:, 384:768], w[QKV][1])
        + nt(r.activ[:, 768:1152], w[QKV][2])
        + nt(r.activ[:, 1152:1536], w[QKV][3])
    )

    def to_input(rows, i, kept):
        value = r.x_ext[pl.ds(pl.multiple_of(BEHIND + i * 128, 128), 128), :].astype(F32)
        back, d_gain = rms_back(value, gain[G_IN], r.tall[1, rows, :])
        r.wide[rows, :] += back
        return kept + d_gain

    put_gain(G_IN, chunks(3, to_input, none))
    fetched.append(local(r.states[5], r.tall.at[1]))
    gains = ReduceGains(net, r.gain_got)
    gains.start(r.gain_grad[...])

    reduce(Reduce.after_first, QKV)
    reduce(Reduce.after_second, GATE, UP, OUT)
    reduce(Reduce.after_third, DOWN)
    gains.step(0)
    reduce(Reduce.after_second, QKV)
    reduce(Reduce.after_third, GATE, UP, OUT)
    reduce(Reduce.share, DOWN)
    gains.step(1)
    reduce(Reduce.after_third, QKV)
    reduce(Reduce.share, GATE, UP, OUT)
    gains.step(2)
    reduce(Reduce.share, QKV)
    r.s_gains[...] = gains.step(3)
    reduce(Reduce.finish, DOWN, GATE, UP, OUT, QKV)
    net.drain()
    for copy in fetched:
        copy.wait()


def run_block(tokens, cotangent, segment, masters, gains, moments):
    vmem, anywhere = (pl.BlockSpec(memory_space=pltpu.VMEM), pl.BlockSpec(memory_space=pl.ANY))
    freqs = (ROPE_BASE ** (-np.arange(128) * 2.0 / HD)).astype(np.float32).reshape(1, 128)
    block_output, input_grad, gain_sums, moments, tall, *rest = pl.pallas_call(
        block_kernel,
        out_shape=[pltpu.VMEM((TOK, D), BF), pltpu.VMEM((TOK, D), F32), pltpu.VMEM((4, 8, 128), F32)]
        + [pltpu.VMEM((4, 640, 512), F32), pltpu.VMEM((2, 512, KEYS), F32)]
        + [pltpu.VMEM(shape, BF) for shape in SHARD]
        + [pltpu.VMEM(shape, F32) for shape in SHARD],
        in_specs=[anywhere, anywhere, vmem, vmem, vmem] + [anywhere] * 11,
        out_specs=[vmem] * 15,
        scratch_shapes=[pltpu.VMEM((4,) + shape, BF) for shape in SHARD]
        + [pltpu.VMEM(shape, kind) for _, shape, kind in SCRATCH]
        + reduce_scratch()
        + [
            pltpu.SemaphoreType.DMA((COPIES,)),
            pltpu.SemaphoreType.DMA((COPIES,)),
            pltpu.SemaphoreType.DMA((LOADS,)),
        ],
        compiler_params=pltpu.CompilerParams(
            collective_id=0, has_side_effects=True, vmem_limit_bytes=BLOCK_BYTES
        ),
        name="block",
    )(
        tokens,
        cotangent,
        segment.reshape(3, 128),
        gains.reshape(6, 128),
        jnp.asarray(freqs),
        *masters,
        *moments,
    )
    return block_output, input_grad, rest[:5], rest[5:], gain_sums, moments, tall


def reciprocal(value):
    guess = pl.reciprocal(value, approx=True)
    return guess * (2.0 - value * guess)


def adamw(weight, gradient, first, second, rate, decay):
    first_new = ADAM_ONE * first + (1.0 - ADAM_ONE) * gradient
    second_new = ADAM_TWO * second + (1.0 - ADAM_TWO) * (gradient * gradient)
    second_hat = second_new * (1.0 / (1.0 - ADAM_TWO**STEP))
    root = second_hat * lax.rsqrt(second_hat)
    step = (first_new * (rate / (1.0 - ADAM_ONE**STEP))) * reciprocal(root + ADAM_EPS)
    weight_new = weight * (1.0 - rate * decay) - step
    return (weight_new, first_new, second_new)


CHUNKS = 4
FETCHED = (QKV, OUT)


def update_kernel(*refs):
    taken = iter(refs)
    take = lambda count: [next(taken) for _ in range(count)]
    states, weights, gradients = ({k: take(2) for k in FETCHED}, take(5), take(5))
    gain_states, gain_sums, done, (moments, tall) = (take(3), next(taken), take(2), take(2))
    results, fresh, gain_fresh = (take(2), [take(3) for _ in SHARD], take(3))
    held, weight_new = (take(5), take(5))
    in_sems, out_sems, done_sems = take(3)

    def part(k, chunk):
        count = SHARD[k][0] // CHUNKS
        return pl.ds(chunk * count, count)

    for k in FETCHED:
        for chunk in range(CHUNKS):
            rows = part(k, chunk)
            for p in range(2):
                pltpu.make_async_copy(
                    states[k][p].at[rows], held[k].at[p, rows], in_sems.at[k, chunk]
                ).start()
    passed = [pltpu.make_async_copy(done[p], results[p], done_sems.at[p]) for p in range(2)]
    for copy in passed:
        copy.start()
    own = gain_sums[lax.axis_index("wsh"), 0:6]
    for ref, value in zip(
        gain_fresh, adamw(gain_states[0][...], own, gain_states[1][...], gain_states[2][...], GAIN_RATE, 0.0)
    ):
        ref[...] = value
    for k in (GATE, UP, DOWN) + FETCHED:
        for chunk in range(CHUNKS):
            rows = part(k, chunk)
            if k in FETCHED:
                whole = held[k].at[:, rows]
                pltpu.make_async_copy(whole, whole, in_sems.at[k, chunk]).wait()
                state = [held[k][p, rows, :] for p in range(2)]
            else:
                place, at = (tall, 0) if k == DOWN else (moments, 2 * (k - GATE))
                state = [place[at + p, rows, :] for p in range(2)]
            gradient = gradients[k][rows, :].astype(F32)
            values = adamw(
                weights[k][rows, :], gradient, state[0], state[1], MATRIX_RATE, MATRIX_DECAY
            )
            weight_new[k][rows, :] = values[0]
            held[k][0, rows, :] = values[1]
            held[k][1, rows, :] = values[2]
            for p, source in enumerate((weight_new[k].at[rows], held[k].at[0, rows], held[k].at[1, rows])):
                pltpu.make_async_copy(source, fresh[k][p].at[rows], out_sems.at[k, p]).start()
    for k in range(5):
        for p in range(3):
            whole = weight_new[k]
            pltpu.make_async_copy(whole, whole, out_sems.at[k, p]).wait()
    for copy in passed:
        copy.wait()


def update(states, weights, gradients, gain_states, gain_sums, done, moments, tall):
    vmem, hbm = (pl.BlockSpec(memory_space=pltpu.VMEM), pl.BlockSpec(memory_space=pltpu.HBM))
    here = [
        pltpu.with_memory_space_constraint(a, pltpu.VMEM)
        for a in (*weights, *gradients, gain_sums, *done, moments, tall)
    ]
    there = [pltpu.with_memory_space_constraint(a, pltpu.HBM) for state in states for a in state]
    got = pl.pallas_call(
        update_kernel,
        out_shape=[jax.ShapeDtypeStruct(a.shape, a.dtype) for a in done]
        + [jax.ShapeDtypeStruct(shape, F32) for shape in SHARD for _ in range(3)]
        + [jax.ShapeDtypeStruct((6, 128), F32)] * 3,
        in_specs=[hbm] * 4 + [vmem] * 18,
        out_specs=[hbm] * 17 + [vmem] * 3,
        scratch_shapes=[pltpu.VMEM((2,) + shape, F32) for shape in SHARD]
        + [pltpu.VMEM(shape, F32) for shape in SHARD]
        + [
            pltpu.SemaphoreType.DMA((5, CHUNKS)),
            pltpu.SemaphoreType.DMA((5, 3)),
            pltpu.SemaphoreType.DMA((2,)),
        ],
        compiler_params=pltpu.CompilerParams(vmem_limit_bytes=UPDATE_BYTES),
        name="update",
    )(*there, *here[:10], *gain_states, *here[10:])
    return tuple(got[:17]) + tuple(a.reshape(768) for a in got[17:])


def on_device(
    tokens,
    cotangent,
    segment,
    qkv_weight,
    out_weight,
    gate_weight,
    up_weight,
    down_weight,
    gains,
    qkv_first,
    qkv_second,
    out_first,
    out_second,
    gate_first,
    gate_second,
    up_first,
    up_second,
    down_first,
    down_second,
    gain_first,
    gain_second,
):
    masters = (qkv_weight, out_weight, gate_weight, up_weight, down_weight)
    block_output, input_grad, sums, fulls, gain_sums, moments, tall = run_block(
        tokens,
        cotangent,
        segment,
        masters,
        gains,
        (gate_first, gate_second, up_first, up_second, down_first, down_second),
    )
    states = (
        (qkv_first, qkv_second),
        (out_first, out_second),
    )
    gain_states = [a.reshape(6, 128) for a in (gains, gain_first, gain_second)]
    return update(states, fulls, sums, gain_states, gain_sums, (block_output, input_grad), moments, tall)


def solution(mesh):
    placed = (
        P(("wsh", "seq"), None),
        P(("wsh", "seq"), None),
        P(("wsh", "seq")),
        P(None, "wsh"),
        P("wsh", None),
        P(None, "wsh"),
        P(None, "wsh"),
        P("wsh", None),
        P("wsh"),
        P(None, "wsh"),
        P(None, "wsh"),
        P("wsh", None),
        P("wsh", None),
        P(None, "wsh"),
        P(None, "wsh"),
        P(None, "wsh"),
        P(None, "wsh"),
        P("wsh", None),
        P("wsh", None),
        P("wsh"),
        P("wsh"),
    )
    return jax.shard_map(
        on_device,
        mesh=mesh,
        in_specs=placed,
        out_specs=(
            P(("wsh", "seq"), None),
            P(("wsh", "seq"), None),
            P(None, "wsh"),
            P(None, "wsh"),
            P(None, "wsh"),
            P("wsh", None),
            P("wsh", None),
            P("wsh", None),
            P(None, "wsh"),
            P(None, "wsh"),
            P(None, "wsh"),
            P(None, "wsh"),
            P(None, "wsh"),
            P(None, "wsh"),
            P("wsh", None),
            P("wsh", None),
            P("wsh", None),
            P("wsh"),
            P("wsh"),
            P("wsh"),
        ),
        check_vma=False,
    )
```
